32 devices in a mesh: seg: 8 (over z, x), rep: 4 (over y, core).
Axes of the slice: x: 2, y: 2, z: 4, core: 2. Of those that a mesh axis runs over, the one named last changes fastest.
Arguments:
- tokens: bfloat16 [2, 4, 64, 128, 768], P(None, 'rep', 'seg'), may hold values from -6 to 6
- cotangent: bfloat16 [2, 4, 64, 128, 768], P(None, 'rep', 'seg'), may hold values from -6 to 6
- doc_counts: int32 [2, 4, 3], P(None, 'rep'), may hold values from 1 to 57, 64 in all within a row
- w_qkv: bfloat16 [768, 2304], P('seg'), may hold values from -0.21875 to 0.21875
- w_out: bfloat16 [768, 768], P('seg'), may hold values from -0.625 to 0.625
- w_up: bfloat16 [768, 3072], P('seg'), may hold values from -0.21875 to 0.21875
- w_down: bfloat16 [3072, 768], P('seg'), may hold values from -0.109375 to 0.109375
- c_qkv: bfloat16 [768, 2304], P('seg'), may hold values from -0.21875 to 0.21875
- c_out: bfloat16 [768, 768], P('seg'), may hold values from -0.625 to 0.625
- pos_table: bfloat16 [64, 768], P('seg'), may hold values from -6 to 6
- norm_gains: bfloat16 [3, 768], P(None, 'seg'), may hold values from 0.5 to 1.5
- norm_shifts: bfloat16 [3, 768], P(None, 'seg'), may hold values from -1.5 to 1.5
Outputs:
- layer_out: bfloat16 [2, 4, 64, 128, 768], P(None, 'rep', 'seg')
- input_grad: float32 [2, 4, 64, 128, 768], P(None, 'rep', 'seg')
- grad_w_qkv: float32 [768, 2304], P('seg')
- grad_w_out: float32 [768, 768], P('seg')
- grad_w_up: float32 [768, 3072], P('seg')
- grad_w_down: float32 [3072, 768], P('seg')
- grad_c_qkv: float32 [768, 2304], P('seg')
- grad_c_out: float32 [768, 768], P('seg')
- grad_pos_table: float32 [64, 768], P('seg')
- grad_norm_gains: float32 [3, 768], P(None, 'seg')
- grad_norm_shifts: float32 [3, 768], P(None, 'seg')
The draws below stay inside these ranges and needn't reach their ends.
Inputs may be any that keep to these rules, and one draw needn't show every extreme that they name: `doc_counts`: for each micro-batch and group the 3 counts sum to 64, and one of them is exactly 57.
All inputs are finite; a program needn't handle non-finite values.
Results may differ from the reference program's by a relative error of at most 0.03.
Values may be sent and summed in bfloat16 or wider, within the bound.
No kernel may reach another device: no remote copies, remote signals or barrier semaphores. Data moves between devices by JAX's collectives and lax.ppermute only.
A program may use at most 320 MiB of HBM per device.

```python
import math
import jax
import jax.numpy as jnp
import numpy as np
from jax import lax

D = 768
FF = 3072
HEAD_DIM = 64
SEGLEN = 128
SEG_DEV = 8
MB = 2
DOCS = 3
SEGS = 64
N_REP = 4


def shard_levels(key, shape, cuts, least, largest):
    def one(axis_at, parts):
        draws = jax.random.uniform(jax.random.fold_in(jax.random.fold_in(key, 6), axis_at), (parts,), jnp.float32, least / len(cuts), largest / len(cuts))
        return jnp.repeat(jnp.exp(draws), shape[axis_at] // parts).reshape((-1,) + (1,) * (len(shape) - axis_at - 1))

    factor_of = one(*cuts[0])
    for cut in cuts[1:]:
        factor_of = factor_of * one(*cut)
    return factor_of


def split_up(number_of, total, limit, lean):
    weights = [(1 << 20) // math.isqrt(standing ** lean) + 1 for standing in range(2, number_of + 1)]
    rest, given = total - limit - (number_of - 1), [1] * (number_of - 1)
    while rest > 0:
        movable = [i for i in range(number_of - 1) if given[i] < limit]
        whole, remaining = sum([weights[i] for i in movable]), rest
        for i in movable:
            more = min(limit - given[i], max(1, remaining * weights[i] // whole), rest)
            given[i] = given[i] + more
            rest = rest - more
    return np.array([limit] + given)


def uneven_parts(stream_key, number_of, total, reach, lean):
    if number_of == 2:
        one = jax.random.randint(stream_key, (), max(1, total - reach), min(reach, total - 1) + 1)
        return jnp.stack([one, total - one])
    tallies = jnp.asarray(split_up(number_of, total, reach, lean), jnp.int32)
    twos = (number_of - 1) // 2
    donor, taker = tallies[1:1 + 2 * twos:2], tallies[2:2 + 2 * twos:2]
    slack = jnp.minimum(donor - 1, reach - taker)
    shifted = jax.random.randint(jax.random.fold_in(stream_key, 1), (twos,), 0, 1 << 20) % (slack + 1)
    tallies = tallies.at[1:1 + 2 * twos:2].set(donor - shifted).at[2:2 + 2 * twos:2].set(taker + shifted)
    return tallies[jax.random.permutation(jax.random.fold_in(stream_key, 2), number_of)]


def gaussian(key, extent, deviation, reach, shards=(), kind=jnp.bfloat16):
    values = deviation * jax.random.normal(key, extent, jnp.float32)
    if shards:
        values = values * shard_levels(key, extent, shards, -0.22, 0.18)
    return jnp.clip(values, -reach, reach).astype(kind)


def setup_inputs(seed: int = 0) -> dict:
    key_of = jax.random.split(jax.random.key(seed), 13)
    return {
        "tokens": gaussian(key_of[0], (MB, N_REP, SEGS, SEGLEN, D), 1.0, 6.0, ((1, 4), (2, 8))),
        "cotangent": gaussian(key_of[1], (MB, N_REP, SEGS, SEGLEN, D), 1.0, 6.0, ((1, 4), (2, 8))),
        "doc_counts": jax.vmap(lambda own: uneven_parts(own, DOCS, SEGS, SEGS - SEG_DEV + 1, 1))(jax.random.split(key_of[2], MB * N_REP)).reshape((MB, N_REP, DOCS)).astype(jnp.int32),
        "w_qkv": gaussian(key_of[3], (D, 3 * D), D ** -0.5, 0.21875, ((0, 8),)),
        "w_out": gaussian(key_of[4], (D, D), (D // 8) ** -0.5, 0.625, ((0, 8),)),
        "w_up": gaussian(key_of[5], (D, FF), D ** -0.5, 0.21875, ((0, 8),)),
        "w_down": gaussian(key_of[6], (FF, D), FF ** -0.5, 0.109375, ((0, 8),)),
        "c_qkv": gaussian(key_of[7], (D, 3 * D), D ** -0.5, 0.21875, ((0, 8),)),
        "c_out": gaussian(key_of[8], (D, D), (D // 8) ** -0.5, 0.625, ((0, 8),)),
        "pos_table": gaussian(key_of[9], (SEGS, D), 1.0, 6.0, ((0, 8),)),
        "norm_gains": jnp.clip(1.0 + 0.1 * jax.random.normal(key_of[10], (3, D), jnp.float32), 0.5, 1.5).astype(jnp.bfloat16),
        "norm_shifts": gaussian(key_of[11], (3, D), 0.3, 1.5, ((1, 8),)),
    }


@jax.custom_vjp
def low(v):
    return lax.optimization_barrier(v.astype(jnp.bfloat16)).astype(jnp.float32)

@jax.custom_vjp
def low_back(v):
    return v

def low_keep(v):
    return (low(v), None)

def low_pass(kept, grad):
    return (grad,)

def back_keep(v):
    return (v, None)

def back_low(kept, grad):
    return (low(grad),)
low.defvjp(low_keep, low_pass)
low_back.defvjp(back_keep, back_low)
EPSILON = 1e-05
NEGATIVE = -1e+30
HIGHEST = lax.Precision.HIGHEST

def matmul_high(left, right):
    return jnp.dot(left, right, precision=HIGHEST)

def layer_norm(values, gain, shift):
    center = values - lax.optimization_barrier(jnp.mean(values, axis=-1, keepdims=True))
    spread = lax.optimization_barrier(jnp.mean(center * center, axis=-1, keepdims=True))
    return center * lax.rsqrt(spread + EPSILON) * gain + shift

def doc_layout(counts):
    counts = counts.astype(jnp.int32)
    doc_ends = jnp.cumsum(counts).astype(jnp.int32)
    doc_starts = doc_ends - counts
    seg_index = jnp.arange(SEGS, dtype=jnp.int32)
    doc_ids = lax.optimization_barrier(jnp.sum((seg_index[:, None] >= doc_ends[None, :]).astype(jnp.int32), axis=1)).astype(jnp.int32)
    owned = doc_ids[:, None] == jnp.arange(DOCS, dtype=jnp.int32)[None, :]
    positions = seg_index - lax.optimization_barrier(jnp.sum(jnp.where(owned, doc_starts[None, :], 0), axis=1)).astype(jnp.int32)
    return (doc_ids, positions.astype(jnp.int32))

def segment_block(blocks, params):
    w_qkv, w_out, w_up, w_down, gains, shifts = params
    seg_count, seg_length, model_width = blocks.shape
    head_count = model_width // HEAD_DIM
    score_scale = HEAD_DIM ** (-0.5)
    flat_rows = blocks.reshape(seg_count * seg_length, model_width)
    projected = low_back(low(matmul_high(flat_rows, w_qkv)))
    projected = projected.reshape(seg_count, seg_length, 3, head_count, HEAD_DIM)
    queries = projected[:, :, 0]
    keys_all = projected[:, :, 1]
    values_all = projected[:, :, 2]
    scores = jnp.einsum('bqhd,bkhd->bhqk', queries, keys_all, precision=HIGHEST) * score_scale
    scores = low_back(scores)
    soft_probs = low(jax.nn.softmax(scores, axis=-1))
    mixed_rows = jnp.einsum('bhqk,bkhd->bqhd', soft_probs, values_all, precision=HIGHEST)
    mixed_rows = low_back(low(mixed_rows.reshape(seg_count * seg_length, model_width)))
    attended = low_back(matmul_high(mixed_rows, w_out))
    first_norm = layer_norm(flat_rows + attended, gains[0], shifts[0])
    hidden_pre = low_back(matmul_high(low(first_norm), w_up))
    activated = low(jax.nn.gelu(hidden_pre, approximate=False))
    branch_out = low_back(matmul_high(activated, w_down))
    second_norm = layer_norm(first_norm + branch_out, gains[1], shifts[1])
    return second_norm.reshape(seg_count, seg_length, model_width)

def cross_block(cls_rows, doc_ids, positions, params):
    c_qkv, c_out, pos_table, gains, shifts = params
    seg_total, model_width = cls_rows.shape
    head_count = model_width // HEAD_DIM
    score_scale = HEAD_DIM ** (-0.5)
    embedded = cls_rows + pos_table[positions]
    projected = low_back(low(matmul_high(low(embedded), c_qkv)))
    projected = projected.reshape(seg_total, 3, head_count, HEAD_DIM)
    scores = jnp.einsum('qhd,khd->hqk', projected[:, 0], projected[:, 1], precision=HIGHEST) * score_scale
    same_doc = doc_ids[:, None] == doc_ids[None, :]
    scores = low_back(jnp.where(same_doc[None], scores, NEGATIVE))
    soft_probs = low(jax.nn.softmax(scores, axis=-1))
    mixed_rows = jnp.einsum('hqk,khd->qhd', soft_probs, projected[:, 2], precision=HIGHEST)
    mixed_rows = low_back(low(mixed_rows.reshape(seg_total, model_width)))
    attended = low_back(matmul_high(mixed_rows, c_out))
    return layer_norm(embedded + attended, gains[2], shifts[2])

def group_forward(token_group, doc_ids, positions, params):
    w_qkv, w_out, w_up, w_down, c_qkv, c_out, pos_table, gains, shifts = params
    block_segs = math.gcd(SEGS, max(1, 4096 // SEGLEN))
    blocks = token_group.reshape(SEGS // block_segs, block_segs, SEGLEN, D)
    seg_params = (w_qkv, w_out, w_up, w_down, gains, shifts)

    def run_block(block_rows):
        return segment_block(block_rows, seg_params)
    seg_out = lax.map(jax.checkpoint(run_block), blocks).reshape(SEGS, SEGLEN, D)
    cls_new = cross_block(seg_out[:, 0, :], doc_ids, positions, (c_qkv, c_out, pos_table, gains, shifts))
    return seg_out.at[:, 0, :].set(cls_new)

def reference(tokens, cotangent, doc_counts, w_qkv, w_out, w_up, w_down, c_qkv, c_out, pos_table, norm_gains, norm_shifts):
    params = tuple((weight.astype(jnp.float32) for weight in (w_qkv, w_out, w_up, w_down, c_qkv, c_out, pos_table, norm_gains, norm_shifts)))
    group_total = MB * N_REP
    token_rows = tokens.reshape(group_total, SEGS, SEGLEN, D)
    cot_rows = cotangent.reshape(group_total, SEGS, SEGLEN, D)
    count_rows = doc_counts.reshape(group_total, DOCS)

    def step(totals, inputs):
        token_group, cot_group, count_group = inputs
        doc_ids, positions = doc_layout(count_group)

        def forward_fn(values, *weights):
            return group_forward(values, doc_ids, positions, weights)
        result, pull = jax.vjp(forward_fn, token_group.astype(jnp.float32), *params)
        grads = pull(cot_group.astype(jnp.float32))
        totals = tuple((left + right for left, right in zip(totals, grads[1:])))
        return (totals, (result.astype(jnp.bfloat16), grads[0]))
    zeros = tuple((jnp.zeros_like(weight) for weight in params))
    totals, (outputs, input_grads) = lax.scan(step, zeros, (token_rows, cot_rows, count_rows))
    return (outputs.reshape(tokens.shape), input_grads.reshape(tokens.shape), totals[0], totals[1], totals[2], totals[3], totals[4], totals[5], totals[6], totals[7], totals[8])
```

```python
from functools import partial
import jax
import jax.numpy as jnp
from jax import lax
from jax.experimental import pallas as pl
from jax.experimental.pallas import tpu as pltpu
from jax.sharding import PartitionSpec as P

HEAD_DIM = 64
PAIR = 2 * HEAD_DIM
EPSILON = 1e-05
NEGATIVE = -1e30
F32 = jnp.float32
BF16 = jnp.bfloat16
MIB = 1 << 20


def dot_nn(left, right):
    return lax.dot_general(left, right, (((1,), (0,)), ((), ())), preferred_element_type=F32)


def dot_nt(left, right):
    return lax.dot_general(left, right, (((1,), (1,)), ((), ())), preferred_element_type=F32)


def dot_tn(left, right):
    return lax.dot_general(left, right, (((0,), (0,)), ((), ())), preferred_element_type=F32)


def norm_parts(values):
    center = values - jnp.mean(values, axis=-1, keepdims=True)
    spread = jnp.mean(center * center, axis=-1, keepdims=True)
    inverse = lax.rsqrt(spread + EPSILON)
    return center * inverse, inverse


def norm_back(grad, unit, inverse, gain):
    scaled = grad * gain
    first = jnp.mean(scaled, axis=-1, keepdims=True)
    second = jnp.mean(scaled * unit, axis=-1, keepdims=True)
    return inverse * (scaled - first - unit * second)


def gelu_parts(hidden):
    size = jnp.abs(hidden)
    bell = jnp.exp(hidden * hidden * -0.5)
    base = size * (0.3275911 * 0.7071067811865476) + 1.0
    inv = pl.reciprocal(base, approx=True)
    inv = inv * (2.0 - base * inv)
    poly = inv * (0.5 * 1.061405429) + (0.5 * -1.453152027)
    poly = poly * inv + (0.5 * 1.421413741)
    poly = poly * inv + (0.5 * -0.284496736)
    poly = poly * inv + (0.5 * 0.254829592)
    tail = poly * inv * bell
    phi = jnp.where(hidden < 0.0, tail, 1.0 - tail)
    return hidden * phi, phi + hidden * bell * 0.3989422804014327


def halves(pair, first_half):
    zero = jnp.zeros_like(pair)
    return jnp.concatenate([jnp.where(first_half, pair, zero), jnp.where(first_half, zero, pair)], axis=0)


def pair_forward(query, key, value, first_half, same=None):
    rows = query.shape[0]
    scores = dot_nt(key, halves(query * BF16(HEAD_DIM ** -0.5), first_half))
    if same is not None:
        scores = jnp.where(same, scores, NEGATIVE)
    raised = jnp.exp(scores - jnp.max(scores, axis=0, keepdims=True))
    probs = (raised * (1.0 / jnp.sum(raised, axis=0, keepdims=True))).astype(BF16)
    both = dot_tn(probs, value)
    return probs, jnp.where(first_half, both[:rows], both[rows:])


def pair_backward(query, key, value, probs, grad_mixed, first_half):
    rows = query.shape[0]
    grad_both = halves(grad_mixed, first_half)
    query_both = halves(query * BF16(HEAD_DIM ** -0.5), first_half)
    grad_probs = dot_nt(value, grad_both)
    wide = probs.astype(F32)
    grad_scores = (wide * (grad_probs - jnp.sum(grad_probs * wide, axis=0, keepdims=True))).astype(BF16)
    grad_value = dot_nn(probs, grad_both)
    grad_key = dot_nn(grad_scores, query_both)
    both = dot_tn(grad_scores, key)
    grad_query = jnp.where(first_half, both[:rows], both[rows:]) * (HEAD_DIM ** -0.5)
    return grad_query, grad_key, grad_value


def lane_half(shape):
    return lax.broadcasted_iota(jnp.int32, shape, 1) % PAIR < HEAD_DIM


def attention_kernel(seg_length, x_ref, wqo_ref, proj_ref, probs_ref, mixed_ref, pre_ref):
    rows, width = x_ref.shape
    pairs = width // PAIR
    for part in range(3):
        proj_ref[:, part * width : (part + 1) * width] = dot_nn(x_ref[...], square(wqo_ref[part])).astype(BF16)
    first_half = lane_half((seg_length, PAIR))
    for seg in range(rows // seg_length):
        span = slice(seg * seg_length, (seg + 1) * seg_length)
        for pair in range(pairs):
            cols = [slice(part * width + pair * PAIR, part * width + (pair + 1) * PAIR) for part in range(3)]
            probs, mixed = pair_forward(
                proj_ref[span, cols[0]], proj_ref[span, cols[1]], proj_ref[span, cols[2]], first_half
            )
            probs_ref[seg, pair] = probs
            mixed_ref[span, cols[0]] = mixed.astype(BF16)
    pre_ref[...] = x_ref[...].astype(F32) + dot_nn(mixed_ref[...], square(wqo_ref[3]))


def square(value):
    return value.reshape(-1, value.shape[-1])


def up_block(ref, part):
    return square(ref[:, part])


def down_block(ref, part):
    count = ref.shape[0] // 4
    return square(ref[part * count : (part + 1) * count])


def whole(shape):
    return pl.BlockSpec(shape, lambda i: (0,) * len(shape), pipeline_mode=pl.Buffered(1))


def by_rows(block, width):
    return pl.BlockSpec((block, width), lambda i: (i, 0))


def attention_forward(rows_in, w_qo, seg_length, block):
    rows, width = rows_in.shape
    pairs = width // PAIR
    segs = block // seg_length
    shapes = (
        jax.ShapeDtypeStruct((rows, 3 * width), BF16),
        jax.ShapeDtypeStruct((rows // seg_length, pairs, seg_length, 2 * seg_length), BF16),
        jax.ShapeDtypeStruct((rows, width), BF16),
        jax.ShapeDtypeStruct((rows, width), F32),
    )
    flops = 2 * rows * width * (4 * width + 4 * seg_length)
    return pl.pallas_call(
        partial(attention_kernel, seg_length),
        out_shape=shapes,
        grid=(rows // block,),
        in_specs=[by_rows(block, width), whole(w_qo.shape)],
        out_specs=[
            by_rows(block, 3 * width),
            pl.BlockSpec((segs, pairs, seg_length, 2 * seg_length), lambda i: (i, 0, 0, 0)),
            by_rows(block, width),
            by_rows(block, width),
        ],
        compiler_params=pltpu.CompilerParams(vmem_limit_bytes=56 * MIB),
        cost_estimate=pl.CostEstimate(flops=2 * flops, bytes_accessed=rows * width * 26, transcendentals=0),
        name="attention_forward",
    )(rows_in, w_qo)


def ffn_kernel(pre_ref, wup_ref, wdown_ref, gains_ref, shifts_ref, low_ref, act_ref, slope_ref, pre2_ref):
    rows, width = pre_ref.shape
    unit, unused = norm_parts(pre_ref[...])
    first = unit * gains_ref[0:1].astype(F32) + shifts_ref[0:1].astype(F32)
    low = first.astype(BF16)
    low_ref[...] = low
    total = first
    for part in range(4):
        cols = slice(part * width, (part + 1) * width)
        act, slope = gelu_parts(dot_nn(low, up_block(wup_ref, part)))
        act = act.astype(BF16)
        act_ref[:, cols] = act
        slope_ref[:, cols] = slope.astype(BF16)
        total = total + dot_nn(act, down_block(wdown_ref, part))
    pre2_ref[...] = total


def ffn_forward(pre_first, w_up, w_down, gains, shifts, block):
    rows, width = pre_first.shape
    hidden = 4 * width
    shapes = (
        jax.ShapeDtypeStruct((rows, width), BF16),
        jax.ShapeDtypeStruct((rows, hidden), BF16),
        jax.ShapeDtypeStruct((rows, hidden), BF16),
        jax.ShapeDtypeStruct((rows, width), F32),
    )
    return pl.pallas_call(
        ffn_kernel,
        out_shape=shapes,
        grid=(rows // block,),
        in_specs=[by_rows(block, width), w_up[1], w_down[1], whole(gains.shape), whole(shifts.shape)],
        out_specs=[
            by_rows(block, width),
            by_rows(block, hidden),
            by_rows(block, hidden),
            by_rows(block, width),
        ],
        compiler_params=pltpu.CompilerParams(vmem_limit_bytes=56 * MIB),
        cost_estimate=pl.CostEstimate(flops=8 * rows * width * hidden, bytes_accessed=rows * width * 28, transcendentals=0),
        name="ffn_forward",
    )(pre_first, w_up[0], w_down[0], gains, shifts)


def ffn_back_kernel(
    seg_length, cot_ref, edge_ref, cls_ref, pre1_ref, pre2_ref, slope_ref, wup_ref, wdown_ref, gains_ref, shifts_ref,
    out_ref, branch_ref, gradh_ref, grad1_ref, low1_ref, sums_ref,
):
    rows, width = cot_ref.shape
    segs = rows // seg_length
    step = pl.program_id(0)
    gain1 = gains_ref[1:2].astype(F32)
    gain0 = gains_ref[0:1].astype(F32)

    def with_edge(values, edge):
        parts = []
        top = lax.broadcasted_iota(jnp.int32, (seg_length, width), 0) == 0
        for seg in range(segs):
            parts.append(jnp.where(top, edge[seg], values[seg * seg_length : (seg + 1) * seg_length]))
        return jnp.concatenate(parts, axis=0) if segs > 1 else parts[0]

    unit2, inverse2 = norm_parts(pre2_ref[...])
    out_ref[...] = with_edge(unit2 * gain1 + shifts_ref[1:2].astype(F32), cls_ref).astype(BF16)
    grad2 = with_edge(cot_ref[...].astype(F32), edge_ref)
    sums = [jnp.sum(grad2 * unit2, axis=0, keepdims=True), jnp.sum(grad2, axis=0, keepdims=True)]
    pre_grad = norm_back(grad2, unit2, inverse2, gain1)
    branch = pre_grad.astype(BF16)
    branch_ref[...] = branch
    total = pre_grad
    for part in range(4):
        cols = slice(part * width, (part + 1) * width)
        grad_act = dot_nt(branch, down_block(wdown_ref, part))
        grad_hidden = (grad_act * slope_ref[:, cols].astype(F32)).astype(BF16)
        gradh_ref[:, cols] = grad_hidden
        total = total + dot_nt(grad_hidden, up_block(wup_ref, part))
    unit1, inverse1 = norm_parts(pre1_ref[...])
    sums += [jnp.sum(total * unit1, axis=0, keepdims=True), jnp.sum(total, axis=0, keepdims=True)]
    grad1 = norm_back(total, unit1, inverse1, gain0)
    grad1_ref[...] = grad1
    low1_ref[...] = grad1.astype(BF16)

    @pl.when(step == 0)
    def start_sums():
        sums_ref[...] = jnp.zeros_like(sums_ref)

    for row, part in zip((1, 4, 0, 3), sums):
        sums_ref[row : row + 1] += part


def ffn_backward(cot, edge, cls_new, pre_first, pre_second, slope, w_up, w_down, gains, shifts, seg_length, block):
    rows, width = cot.shape
    hidden = 4 * width
    segs = block // seg_length
    small = pl.BlockSpec((segs, 1, width), lambda i: (i, 0, 0))
    shapes = (
        jax.ShapeDtypeStruct((rows, width), BF16),
        jax.ShapeDtypeStruct((rows, width), BF16),
        jax.ShapeDtypeStruct((rows, hidden), BF16),
        jax.ShapeDtypeStruct((rows, width), F32),
        jax.ShapeDtypeStruct((rows, width), BF16),
        jax.ShapeDtypeStruct((8, width), F32),
    )
    return pl.pallas_call(
        partial(ffn_back_kernel, seg_length),
        out_shape=shapes,
        grid=(rows // block,),
        in_specs=[
            by_rows(block, width), small, small, by_rows(block, width), by_rows(block, width), by_rows(block, hidden),
            w_up[1], w_down[1], whole(gains.shape), whole(shifts.shape),
        ],
        out_specs=[
            by_rows(block, width), by_rows(block, width), by_rows(block, hidden), by_rows(block, width), by_rows(block, width),
            pl.BlockSpec((8, width), lambda i: (0, 0)),
        ],
        compiler_params=pltpu.CompilerParams(vmem_limit_bytes=56 * MIB),
        cost_estimate=pl.CostEstimate(flops=8 * rows * width * hidden, bytes_accessed=rows * width * 40, transcendentals=0),
        name="ffn_backward",
    )(cot, edge, cls_new, pre_first, pre_second, slope, w_up[0], w_down[0], gains, shifts)


def attention_back_kernel(seg_length, grad1_ref, low1_ref, proj_ref, probs_ref, wqo_ref, gradp_ref, input_ref, gradm_ref):
    rows, width = grad1_ref.shape
    pairs = width // PAIR
    gradm_ref[...] = dot_nt(low1_ref[...], square(wqo_ref[3])).astype(BF16)
    first_half = lane_half((seg_length, PAIR))
    for seg in range(rows // seg_length):
        span = slice(seg * seg_length, (seg + 1) * seg_length)
        for pair in range(pairs):
            cols = [slice(part * width + pair * PAIR, part * width + (pair + 1) * PAIR) for part in range(3)]
            grads = pair_backward(
                proj_ref[span, cols[0]], proj_ref[span, cols[1]], proj_ref[span, cols[2]],
                probs_ref[seg, pair], gradm_ref[span, cols[0]], first_half,
            )
            for place, grad in zip(cols, grads):
                gradp_ref[span, place] = grad.astype(BF16)
    total = grad1_ref[...]
    for part in range(3):
        total = total + dot_nt(gradp_ref[:, part * width : (part + 1) * width], square(wqo_ref[part]))
    input_ref[...] = total


def attention_backward(grad1, low1, proj, probs, w_qo, seg_length, block):
    rows, width = grad1.shape
    pairs = width // PAIR
    segs = block // seg_length
    return pl.pallas_call(
        partial(attention_back_kernel, seg_length),
        out_shape=(jax.ShapeDtypeStruct((rows, 3 * width), BF16), jax.ShapeDtypeStruct((rows, width), F32)),
        grid=(rows // block,),
        in_specs=[
            by_rows(block, width), by_rows(block, width), by_rows(block, 3 * width),
            pl.BlockSpec((segs, pairs, seg_length, 2 * seg_length), lambda i: (i, 0, 0, 0)),
            whole(w_qo.shape),
        ],
        out_specs=[by_rows(block, 3 * width), by_rows(block, width)],
        scratch_shapes=[pltpu.VMEM((block, width), BF16)],
        compiler_params=pltpu.CompilerParams(vmem_limit_bytes=56 * MIB),
        cost_estimate=pl.CostEstimate(flops=2 * rows * width * (8 * width), bytes_accessed=rows * width * 30, transcendentals=0),
        name="attention_backward",
    )(grad1, low1, proj, probs, w_qo)


def edge_kernel(pre_ref, wup_ref, wdown_ref, gains_ref, shifts_ref, out_ref):
    unit, unused = norm_parts(pre_ref[...])
    total = unit * gains_ref[0:1].astype(F32) + shifts_ref[0:1].astype(F32)
    low = total.astype(BF16)
    for part in range(4):
        act, unused = gelu_parts(dot_nn(low, up_block(wup_ref, part)))
        total = total + dot_nn(act.astype(BF16), down_block(wdown_ref, part))
    unit, unused = norm_parts(total)
    out_ref[...] = unit * gains_ref[1:2].astype(F32) + shifts_ref[1:2].astype(F32)


def edge_forward(pre_edge, w_up, w_down, gains, shifts):
    rows, width = pre_edge.shape
    return pl.pallas_call(
        edge_kernel,
        out_shape=jax.ShapeDtypeStruct((rows, width), F32),
        grid=(1,),
        in_specs=[by_rows(rows, width), w_up[1], w_down[1], whole(gains.shape), whole(shifts.shape)],
        out_specs=by_rows(rows, width),
        compiler_params=pltpu.CompilerParams(vmem_limit_bytes=56 * MIB),
        cost_estimate=pl.CostEstimate(flops=200 * rows * width * width, bytes_accessed=20 * width * width, transcendentals=0),
        name="edge_forward",
    )(pre_edge, w_up[0], w_down[0], gains, shifts)


def cross_kernel(
    local, rows_ref, cot_ref, keyc_ref, keyr_ref, place_ref, table_ref, wc_ref, gains_ref, shifts_ref,
    new_ref, edge_ref, low_ref, gradp_ref, mixed_ref, gradz_ref, sums_ref, table_grad_ref, proj_ref, probs_ref, gradm_ref,
):
    count, width = rows_ref.shape
    pairs = width // PAIR
    entries = table_ref.shape[0]
    picks = place_ref[...] == lax.broadcasted_iota(jnp.int32, (count, entries), 1)
    embedded = rows_ref[...] + dot_nn(picks.astype(BF16), table_ref[...])
    low = embedded.astype(BF16)
    low_ref[...] = low
    for part in range(3):
        proj_ref[:, part * width : (part + 1) * width] = dot_nn(low, up_block(wc_ref, part)).astype(BF16)
    first_half = lane_half((count, PAIR))
    same = keyc_ref[...] == keyr_ref[...]
    places = [
        [slice(part * width + pair * PAIR, part * width + (pair + 1) * PAIR) for part in range(3)] for pair in range(pairs)
    ]
    for pair, cols in enumerate(places):
        probs, mixed = pair_forward(proj_ref[:, cols[0]], proj_ref[:, cols[1]], proj_ref[:, cols[2]], first_half, same)
        probs_ref[pair] = probs
        mixed_ref[:, cols[0]] = mixed.astype(BF16)
    pre_third = embedded + dot_nn(mixed_ref[...], up_block(wc_ref, 3))
    unit, inverse = norm_parts(pre_third)
    gain = gains_ref[2:3].astype(F32)
    new_ref[...] = unit[:local] * gain + shifts_ref[2:3].astype(F32)
    grad_out = cot_ref[...]
    grad_third = norm_back(grad_out, unit, inverse, gain)
    sums_ref[...] = jnp.zeros_like(sums_ref)
    sums_ref[2:3] = jnp.sum(grad_out[:local] * unit[:local], axis=0, keepdims=True)
    sums_ref[5:6] = jnp.sum(grad_out[:local], axis=0, keepdims=True)
    gradz = grad_third.astype(BF16)
    gradz_ref[...] = gradz
    gradm_ref[...] = dot_nt(gradz, up_block(wc_ref, 3)).astype(BF16)
    for pair, cols in enumerate(places):
        grads = pair_backward(
            proj_ref[:, cols[0]], proj_ref[:, cols[1]], proj_ref[:, cols[2]], probs_ref[pair], gradm_ref[:, cols[0]], first_half
        )
        for place, grad in zip(cols, grads):
            gradp_ref[:, place] = grad.astype(BF16)
    grad_edge = grad_third[:local]
    for part in range(3):
        grad_edge = grad_edge + dot_nt(gradp_ref[:local, part * width : (part + 1) * width], up_block(wc_ref, part))
    edge_ref[...] = grad_edge
    table_grad_ref[...] = lax.dot_general(
        picks[:local].astype(F32), grad_edge, (((0,), (0,)), ((), ())),
        precision=lax.Precision.HIGHEST, preferred_element_type=F32,
    )


def cross_block(local, edge_rows, edge_cot, key_col, key_row, place, table, w_cross, gains, shifts):
    count, width = edge_rows.shape
    shapes = (
        jax.ShapeDtypeStruct((local, width), F32),
        jax.ShapeDtypeStruct((local, width), F32),
        jax.ShapeDtypeStruct((count, width), BF16),
        jax.ShapeDtypeStruct((count, 3 * width), BF16),
        jax.ShapeDtypeStruct((count, width), BF16),
        jax.ShapeDtypeStruct((count, width), BF16),
        jax.ShapeDtypeStruct((8, width), F32),
        jax.ShapeDtypeStruct(table.shape, F32),
    )
    return pl.pallas_call(
        partial(cross_kernel, local),
        out_shape=shapes,
        grid=(1,),
        in_specs=[
            whole(edge_rows.shape), whole(edge_cot.shape), whole(key_col.shape), whole(key_row.shape), whole(place.shape),
            whole(table.shape), w_cross[1], whole(gains.shape), whole(shifts.shape),
        ],
        out_specs=[whole(shape.shape) for shape in shapes],
        scratch_shapes=[
            pltpu.VMEM((count, 3 * width), BF16),
            pltpu.VMEM((width // PAIR, count, 2 * count), BF16),
            pltpu.VMEM((count, width), BF16),
        ],
        compiler_params=pltpu.CompilerParams(vmem_limit_bytes=56 * MIB),
        cost_estimate=pl.CostEstimate(flops=10_000_000_000, bytes_accessed=width * width * 8, transcendentals=0),
        name="cross_block",
    )(edge_rows, edge_cot, key_col, key_row, place, table, w_cross[0], gains, shifts)


def cols_grad_kernel(ids_ref, left_ref, right_ref, send_ref, keep_ref):
    step = pl.program_id(0)
    product = dot_tn(left_ref[...], right_ref[...]).astype(BF16)

    @pl.when(step < 2)
    def to_send():
        send_ref[0] = product

    @pl.when(step >= 2)
    def to_keep():
        keep_ref[0] = product


def joint_grad_kernel(ids_ref, left_ref, last_left_ref, right_ref, last_right_ref, send_ref, keep_ref):
    step = pl.program_id(0)
    block = step ^ (2 * (1 - (ids_ref[1] & 1)))

    def put(product):
        @pl.when(step < 2)
        def to_send():
            send_ref[0] = product

        @pl.when(step >= 2)
        def to_keep():
            keep_ref[0] = product

    @pl.when(block < 3)
    def main():
        put(dot_tn(left_ref[...], right_ref[...]).astype(BF16))

    @pl.when(block == 3)
    def last():
        put(dot_tn(last_left_ref[...], last_right_ref[...]).astype(BF16))


def send_keep_specs(width):
    return [
        pl.BlockSpec((1, width, width), lambda j, ids: (jnp.minimum(j, 1), 0, 0)),
        pl.BlockSpec((1, width, width), lambda j, ids: (jnp.maximum(j - 2, 0), 0, 0)),
    ]


def other_core_first(j, ids):
    return j ^ (2 * (1 - (ids[1] & 1)))


def cols_grads(ids, left, right):
    rows, width = left.shape
    fixed = pl.BlockSpec((rows, width), lambda j, ids: (0, 0), pipeline_mode=pl.Buffered(1))
    half = jax.ShapeDtypeStruct((2, width, width), BF16)
    return pl.pallas_call(
        cols_grad_kernel,
        out_shape=(half, half),
        grid_spec=pltpu.PrefetchScalarGridSpec(
            num_scalar_prefetch=1,
            grid=(4,),
            in_specs=[fixed, pl.BlockSpec((rows, width), lambda j, ids: (0, other_core_first(j, ids)))],
            out_specs=send_keep_specs(width),
        ),
        compiler_params=pltpu.CompilerParams(vmem_limit_bytes=56 * MIB),
        cost_estimate=pl.CostEstimate(flops=8 * rows * width * width, bytes_accessed=10 * rows * width, transcendentals=0),
        name="cols_grads",
    )(ids, left, right)


def joint_grads(ids, left, last_left, right, last_right):
    rows, width = left.shape
    fixed = pl.BlockSpec((rows, width), lambda j, ids: (0, 0), pipeline_mode=pl.Buffered(1))
    half = jax.ShapeDtypeStruct((2, width, width), BF16)
    return pl.pallas_call(
        joint_grad_kernel,
        out_shape=(half, half),
        grid_spec=pltpu.PrefetchScalarGridSpec(
            num_scalar_prefetch=1,
            grid=(4,),
            in_specs=[
                fixed, fixed,
                pl.BlockSpec((rows, width), lambda j, ids: (0, jnp.minimum(other_core_first(j, ids), 2))),
                fixed,
            ],
            out_specs=send_keep_specs(width),
        ),
        compiler_params=pltpu.CompilerParams(vmem_limit_bytes=56 * MIB),
        cost_estimate=pl.CostEstimate(flops=8 * rows * width * width, bytes_accessed=12 * rows * width, transcendentals=0),
        name="joint_grads",
    )(ids, left, last_left, right, last_right)


def rows_grad_kernel(ids_ref, left_ref, right_ref, send_ref, keep_ref, held_ref):
    core = ids_ref[1] & 1
    held_ref[...] = dot_tn(left_ref[...], right_ref[...]).reshape(held_ref.shape)
    for share in range(2):
        send_ref[share] = held_ref[:, 2 * (1 - core) + share].astype(BF16)
        keep_ref[share] = held_ref[:, 2 * core + share].astype(BF16)


def rows_grads(ids, left, right, count):
    rows, width = right.shape
    hidden = left.shape[1]
    shard_rows = hidden // count // 4
    owners = count // 4
    half = jax.ShapeDtypeStruct((2, count, shard_rows, width), BF16)
    out_spec = pl.BlockSpec((2, owners, shard_rows, width), lambda j, ids: (0, j, 0, 0))
    return pl.pallas_call(
        rows_grad_kernel,
        out_shape=(half, half),
        grid_spec=pltpu.PrefetchScalarGridSpec(
            num_scalar_prefetch=1,
            grid=(4,),
            in_specs=[
                pl.BlockSpec((rows, hidden // 4), lambda j, ids: (0, j)),
                pl.BlockSpec((rows, width), lambda j, ids: (0, 0), pipeline_mode=pl.Buffered(1)),
            ],
            out_specs=[out_spec, out_spec],
            scratch_shapes=[pltpu.VMEM((owners, 4, shard_rows, width), F32)],
        ),
        compiler_params=pltpu.CompilerParams(vmem_limit_bytes=56 * MIB),
        cost_estimate=pl.CostEstimate(flops=2 * rows * width * hidden, bytes_accessed=10 * rows * width, transcendentals=0),
        name="rows_grads",
    )(ids, left, right)


def seg_swap(value, mask):
    count = lax.axis_size("seg")
    return lax.ppermute(value, "seg", [(i, i ^ mask) for i in range(count)])


def rep_swap(value, mask):
    count = lax.axis_size("rep")
    return lax.ppermute(value, "rep", [(i, i ^ mask) for i in range(count)])


def both_swap(value, seg_mask, rep_mask):
    reps = lax.axis_size("rep")
    total = lax.axis_size("seg") * reps
    pairs = [(i, ((i // reps) ^ seg_mask) * reps + ((i % reps) ^ rep_mask)) for i in range(total)]
    return lax.ppermute(value, ("seg", "rep"), pairs)


def place_kernel(count, ids_ref, *refs):
    parts, out_ref, sems = refs[:-2], refs[-2], refs[-1]
    me, core = ids_ref[0], ids_ref[1] & 1
    copies = []
    for number, part in enumerate(parts):
        mask, side = number % count, number // count
        owner_core = core if side == 0 else 1 - core
        for share in range(2):
            target = out_ref.at[2 * owner_core + share, me ^ mask]
            copies.append(pltpu.make_async_copy(part.at[share], target, sems.at[2 * number + share]))
    for copy in copies:
        copy.start()
    for copy in copies:
        copy.wait()


def put_in_place(ids, parts, count):
    unused, rows, width = parts[0].shape
    return pl.pallas_call(
        partial(place_kernel, count),
        out_shape=jax.ShapeDtypeStruct((4, count, rows, width), parts[0].dtype),
        in_specs=[pl.BlockSpec(memory_space=pltpu.SMEM)] + [pl.BlockSpec(memory_space=pl.ANY)] * len(parts),
        out_specs=pl.BlockSpec(memory_space=pltpu.VMEM),
        scratch_shapes=[pltpu.SemaphoreType.DMA((2 * len(parts),))],
        compiler_params=pltpu.CompilerParams(vmem_limit_bytes=32 * MIB),
        cost_estimate=pl.CostEstimate(flops=0, bytes_accessed=16 * count * rows * width, transcendentals=0),
        name="put_in_place",
    )(ids, *parts)


def gather_halves(ids, blocks):
    count = lax.axis_size("seg")
    piece = lax.dynamic_slice_in_dim(blocks, 2 * (ids[1] & 1), 2, 0)
    held = {0: piece}
    for mask in range(2, count, 2):
        held[mask] = seg_swap(piece, mask)
    for mask in range(0, count, 2):
        held[mask + 1] = seg_swap(held[mask], 1)
    mine = [held[mask] for mask in range(count)]
    return put_in_place(ids, mine + [rep_swap(part, 1) for part in mine], count)


def spread_kernel(ids_ref, keep_ref, came_ref, stay_ref, x_ref, y_ref, xy_ref):
    near, across = ids_ref[0] & 1, ids_ref[1] >> 1

    def total(share, side):
        return (keep_ref[share, 0, side].astype(F32) + came_ref[share, 0, side].astype(F32)).astype(BF16)

    stay_ref[0] = total(across, near)
    x_ref[0] = total(across, 1 - near)
    y_ref[0] = total(1 - across, near)
    xy_ref[0] = total(1 - across, 1 - near)


def spread(ids, keep, came):
    unused, count, rows, width = keep.shape
    far = count // 2
    shape = (2, far, 2, rows, width)
    in_spec = pl.BlockSpec((2, 1, 2, rows, width), lambda j: (0, j, 0, 0, 0))
    out_spec = pl.BlockSpec((1, rows, width), lambda j: (j, 0, 0))
    out = jax.ShapeDtypeStruct((far, rows, width), BF16)
    return pl.pallas_call(
        spread_kernel,
        out_shape=(out,) * 4,
        grid=(far,),
        in_specs=[pl.BlockSpec(memory_space=pltpu.SMEM), in_spec, in_spec],
        out_specs=[out_spec] * 4,
        compiler_params=pltpu.CompilerParams(vmem_limit_bytes=32 * MIB),
        cost_estimate=pl.CostEstimate(flops=0, bytes_accessed=12 * count * rows * width, transcendentals=0),
        name="spread",
    )(ids, keep.reshape(shape), came.reshape(shape))


def settle_kernel(ids_ref, a_ref, b_ref, c_ref, d_ref, *outs):
    far = ids_ref[0] >> 1
    for mask, out in enumerate(outs):
        place = far ^ mask
        total = (a_ref[place].astype(F32) + b_ref[place].astype(F32)) + (c_ref[place].astype(F32) + d_ref[place].astype(F32))
        out[...] = total.astype(BF16)


def settle(ids, parts):
    far, rows, width = parts[0].shape
    whole_spec = pl.BlockSpec(memory_space=pltpu.VMEM)
    return pl.pallas_call(
        settle_kernel,
        out_shape=(jax.ShapeDtypeStruct((rows, width), BF16),) * far,
        in_specs=[pl.BlockSpec(memory_space=pltpu.SMEM)] + [whole_spec] * 4,
        out_specs=[whole_spec] * far,
        compiler_params=pltpu.CompilerParams(vmem_limit_bytes=32 * MIB),
        cost_estimate=pl.CostEstimate(flops=0, bytes_accessed=10 * far * rows * width, transcendentals=0),
        name="settle",
    )(ids, *parts)


def reduce_group(ids, send, keep):
    count = lax.axis_size("seg")
    width = send.shape[-1]
    shape = (2, count, send.shape[-2] if send.ndim == 4 else send.shape[1] // count, width)
    stay, to_x, to_y, to_xy = spread(ids, keep.reshape(shape), rep_swap(send, 1).reshape(shape))
    own, *others = settle(ids, [stay, seg_swap(to_x, 1), rep_swap(to_y, 2), both_swap(to_xy, 1, 2)])
    total = own.astype(F32)
    for mask, other in enumerate(others, 1):
        total = total + seg_swap(other, 2 * mask).astype(F32)
    return total.astype(BF16)


def share_out(ids, share):
    rep = ids[1]
    held = jnp.stack([share, rep_swap(share, 2)], axis=0)
    held = jnp.concatenate([held, rep_swap(held, 1)], axis=0)
    order = jnp.array([0, 2, 1, 3], jnp.int32)
    return [
        lax.dynamic_index_in_dim(held, order[rep ^ owner], 0, keepdims=False).astype(F32) for owner in (0, 2, 1, 3)
    ]


def halve(value, axis, bit):
    own = lax.dynamic_index_in_dim(value, bit, axis, keepdims=False)
    other = lax.dynamic_index_in_dim(value, 1 - bit, axis, keepdims=False)
    return own, other


def reduce_small(ids, value):
    mask = lax.axis_size("seg") // 2
    while mask:
        bit = (ids[0] // mask) & 1
        own, other = halve(value.reshape((2, mask) + value.shape[1:]), 0, bit)
        value = own + seg_swap(other, mask)
        mask //= 2
    value = value[0]
    for mask in (1, 2):
        value = value + rep_swap(value, mask)
    return value


def body(tokens, cotangent, doc_counts, w_qkv, w_out, w_up, w_down, c_qkv, c_out, pos_table, norm_gains, norm_shifts):
    micro_count, unused, seg_local, seg_length, width = tokens.shape
    count = lax.axis_size("seg")
    me = lax.axis_index("seg").astype(jnp.int32)
    rep = lax.axis_index("rep").astype(jnp.int32)
    ids = jnp.stack([me, rep])
    shard_rows = w_qkv.shape[0]
    local = micro_count * seg_local
    rows = local * seg_length
    table_rows = pos_table.shape[0]
    norm_cols = norm_gains.shape[1]

    def shares_of(matrix):
        return matrix.reshape(shard_rows, 4, width).transpose(1, 0, 2)

    def own_share(matrix):
        return lax.dynamic_slice_in_dim(matrix, rep * width, width, 1)

    packed = jnp.concatenate(
        [
            own_share(w_up),
            lax.dynamic_slice_in_dim(w_down, rep * shard_rows, shard_rows, 0),
            own_share(jnp.concatenate([c_qkv, c_out], axis=1)),
            pos_table,
            jnp.pad(jnp.concatenate([norm_gains, norm_shifts], axis=0), ((0, 2), (0, width - norm_cols))),
        ],
        axis=0,
    )
    gathered = lax.all_gather(packed, ("seg", "rep"), axis=0).reshape(count, 4, -1, width)
    small = gathered[:, 0, 3 * shard_rows :]
    table = small[:, :table_rows].reshape(count * table_rows, width)
    norms = small[:, table_rows : table_rows + 6, :norm_cols].transpose(1, 0, 2).reshape(6, width)
    gains, shifts = norms[:3], norms[3:]

    if shard_rows % 16 == 0:
        def part_of(place):
            spec = pl.BlockSpec(
                (count, 4, shard_rows, width), lambda i: (0, 0, place, 0), pipeline_mode=pl.Buffered(1)
            )
            return gathered, spec

        full_up, full_down, full_cross = part_of(0), part_of(1), part_of(2)
    else:
        def part_of(place):
            return gathered[:, :, place * shard_rows : (place + 1) * shard_rows]

        def joined(value):
            value = value.transpose(1, 0, 2, 3).reshape(1, 4, width, width)
            return value, whole(value.shape)

        full_up, full_cross = joined(part_of(0)), joined(part_of(2))
        full_down = part_of(1).reshape(4, 1, width, width)
        full_down = (full_down, whole(full_down.shape))
    full_qo = gather_halves(ids, shares_of(jnp.concatenate([w_qkv, w_out], axis=1))).reshape(4, width, width)

    counts = doc_counts[:, 0]
    ends = jnp.cumsum(counts, axis=1)
    owners = me ^ jnp.arange(count, dtype=jnp.int32)
    seg_ids = owners[:, None, None] * seg_local + jnp.arange(seg_local, dtype=jnp.int32)[None, None, :]
    seg_ids = jnp.broadcast_to(seg_ids, (count, micro_count, seg_local))
    past = seg_ids[..., None] >= ends[None, :, None, :]
    doc_ids = jnp.sum(past.astype(jnp.int32), axis=-1)
    starts = jnp.sum(jnp.where(past, counts[None, :, None, :], 0), axis=-1)
    places = (seg_ids - starts).reshape(-1, 1)
    keys = (doc_ids + (counts.shape[1] + 1) * jnp.arange(micro_count, dtype=jnp.int32)[None, :, None]).reshape(-1)

    flat = tokens.reshape(rows, width)
    cot = cotangent.reshape(rows, width)
    proj, probs, mixed, pre_first = attention_forward(flat, full_qo, seg_length, 2 * seg_length)
    pre_edge = pre_first.reshape(local, seg_length, width)[:, 0]
    edge = edge_forward(pre_edge, full_up, full_down, gains, shifts)
    edge_cot = cot.reshape(local, seg_length, width)[:, 0].astype(F32)
    edges = jnp.stack([edge, edge_cot], axis=0)
    edges = jnp.stack([edges] + [seg_swap(edges, mask) for mask in range(1, count)], axis=0)
    low, act, slope, pre_second = ffn_forward(pre_first, full_up, full_down, gains, shifts, 2 * seg_length)
    cls_new, grad_edge, c_low, c_gradp, c_mixed, c_gradz, c_sums, table_grad = cross_block(
        local, edges[:, 0].reshape(-1, width), edges[:, 1].reshape(-1, width),
        keys[:, None], jnp.concatenate([keys, keys])[None, :], places, table, full_cross, gains, shifts,
    )
    layer_out, branch, grad_hidden, grad1, low1, sums = ffn_backward(
        cot, grad_edge[:, None], cls_new[:, None], pre_first, pre_second, slope, full_up, full_down, gains, shifts,
        seg_length, 2 * seg_length,
    )
    down_share = reduce_group(ids, *rows_grads(ids, act, branch, count))
    up_share = reduce_group(ids, *cols_grads(ids, low, grad_hidden))
    grad_proj, input_grad = attention_backward(grad1, low1, proj, probs, full_qo, seg_length, 2 * seg_length)
    qo_share = reduce_group(ids, *joint_grads(ids, flat, mixed, grad_proj, low1))

    own_low = lax.dynamic_slice_in_dim(c_low, me * shard_rows, shard_rows, 1)
    own_mixed = lax.dynamic_slice_in_dim(c_mixed, me * shard_rows, shard_rows, 1)
    grad_c = shares_of(jnp.concatenate([dot_tn(own_low, c_gradp), dot_tn(own_mixed, c_gradz)], axis=1)).astype(BF16)
    own, other = halve(grad_c.reshape(2, 2, shard_rows, width), 0, rep & 1)
    own, other = halve(own.astype(F32) + rep_swap(other, 1).astype(F32), 0, rep >> 1)
    c_share = (own + rep_swap(other.astype(BF16), 2).astype(F32)).astype(BF16)

    norm_sums = (sums + c_sums).reshape(8, count, norm_cols).transpose(1, 0, 2)
    norm_sums = jnp.pad(norm_sums, ((0, 0), (0, 0), (0, width - norm_cols)))
    summed = reduce_small(ids, jnp.concatenate([norm_sums, table_grad.reshape(count, table_rows, width)], axis=1))

    early = share_out(ids, jnp.stack([down_share, up_share, c_share], axis=0))
    late = share_out(ids, qo_share)

    def side_by_side(parts):
        return jnp.concatenate(parts, axis=1)

    return (
        layer_out.reshape(tokens.shape),
        input_grad.reshape(tokens.shape),
        side_by_side(late[:3]),
        late[3],
        side_by_side([part[1] for part in early]),
        jnp.concatenate([part[0] for part in early], axis=0),
        side_by_side([part[2] for part in early[:3]]),
        early[3][2],
        summed[8:],
        summed[:3, :norm_cols],
        summed[3:6, :norm_cols],
    )


def solution(mesh):
    rows = P(None, "rep", "seg", None, None)
    split = P("seg", None)
    last = P(None, "seg")
    return jax.shard_map(
        body,
        mesh=mesh,
        in_specs=(rows, rows, P(None, "rep", None)) + (split,) * 7 + (last, last),
        out_specs=(rows, rows) + (split,) * 7 + (last, last),
        check_vma=False,
    )
```

```python
from functools import partial
import jax
import jax.numpy as jnp
from jax import lax
from jax.experimental import pallas as pl
from jax.experimental.pallas import tpu as pltpu
from jax.sharding import PartitionSpec as P

HEAD_DIM = 64
PAIR = 2 * HEAD_DIM
EPSILON = 1e-05
NEGATIVE = -1e30
F32 = jnp.float32
BF16 = jnp.bfloat16
MIB = 1 << 20
LONG, SHORT = 6.0, 0.001


def dot_nn(left, right):
    return lax.dot_general(left, right, (((1,), (0,)), ((), ())), preferred_element_type=F32)


def dot_nt(left, right):
    return lax.dot_general(left, right, (((1,), (1,)), ((), ())), preferred_element_type=F32)


def dot_tn(left, right):
    return lax.dot_general(left, right, (((0,), (0,)), ((), ())), preferred_element_type=F32)


def norm_parts(values):
    center = values - jnp.mean(values, axis=-1, keepdims=True)
    spread = jnp.mean(center * center, axis=-1, keepdims=True)
    inverse = lax.rsqrt(spread + EPSILON)
    return center * inverse, inverse


def norm_back(grad, unit, inverse, gain):
    scaled = grad * gain
    first = jnp.mean(scaled, axis=-1, keepdims=True)
    second = jnp.mean(scaled * unit, axis=-1, keepdims=True)
    return inverse * (scaled - first - unit * second)


def gelu_parts(hidden):
    phi = 0.5 + 0.5 * lax.erf(hidden * 0.5 ** 0.5)
    bell = jnp.exp(hidden * hidden * -0.5) * 0.3989422804014327
    return hidden * phi, phi + hidden * bell


def halves(pair, first_half):
    zero = jnp.zeros_like(pair)
    return jnp.concatenate([jnp.where(first_half, pair, zero), jnp.where(first_half, zero, pair)], axis=0)


def pair_forward(query, key, value, first_half, same=None):
    rows = query.shape[0]
    scores = dot_nt(key, halves(query * BF16(HEAD_DIM ** -0.5), first_half))
    if same is not None:
        scores = jnp.where(same, scores, NEGATIVE)
    raised = jnp.exp(scores - jnp.max(scores, axis=0, keepdims=True))
    probs = (raised * (1.0 / jnp.sum(raised, axis=0, keepdims=True))).astype(BF16)
    both = dot_tn(probs, value)
    return probs, jnp.where(first_half, both[:rows], both[rows:])


def pair_backward(query, key, value, probs, grad_mixed, first_half):
    rows = query.shape[0]
    grad_both = halves(grad_mixed, first_half)
    query_both = halves(query * BF16(HEAD_DIM ** -0.5), first_half)
    grad_probs = dot_nt(value, grad_both)
    wide = probs.astype(F32)
    grad_scores = (wide * (grad_probs - jnp.sum(grad_probs * wide, axis=0, keepdims=True))).astype(BF16)
    grad_value = dot_nn(probs, grad_both)
    grad_key = dot_nn(grad_scores, query_both)
    both = dot_tn(grad_scores, key)
    grad_query = jnp.where(first_half, both[:rows], both[rows:]) * (HEAD_DIM ** -0.5)
    return grad_query, grad_key, grad_value


def lane_half(shape):
    return lax.broadcasted_iota(jnp.int32, shape, 1) % PAIR < HEAD_DIM


def square(value):
    return value.reshape(-1, value.shape[-1])


def up_block(ref, part):
    return square(ref[:, part])


def down_block(ref, part):
    count = ref.shape[0] // 4
    return square(ref[part * count : (part + 1) * count])


def whole(shape):
    return pl.BlockSpec(shape, lambda *at: (0,) * len(shape), pipeline_mode=pl.Buffered(1))


ANYWHERE = pl.BlockSpec(memory_space=pl.ANY)


def cost(flops, moved, weight=1.0):
    return pl.CostEstimate(flops=int(flops * weight), bytes_accessed=int(moved * weight), transcendentals=0)


def rows_call(kernel, name, block, span, rowed, fixed, outs, flops, prior=(), after=(), extra=(), ids=None, scratch=(), weight=1.0):
    first, steps = span

    def cut(value):
        array, ratio = value if isinstance(value, tuple) else (value, 1)
        shape = (block // ratio,) + array.shape[1:]
        return array, pl.BlockSpec(shape, lambda i, *ids: (i + first,) + (0,) * (len(shape) - 1))

    ins = [cut(value) for value in rowed] + list(fixed)
    results = [cut(value) for value in outs] + [(shape, whole(shape.shape)) for shape in extra]
    unread = list(prior) + list(after)
    lead = 0 if ids is None else 1
    moved = sum(value.size * value.dtype.itemsize for value, unused in ins + results) // 2

    def run(*refs):
        start = lead + len(ins)
        kernel(*refs[:start], *refs[start + len(unread) :])

    return pl.pallas_call(
        run,
        out_shape=tuple(jax.ShapeDtypeStruct(shape.shape, shape.dtype) for shape, unused in results),
        grid_spec=pltpu.PrefetchScalarGridSpec(
            num_scalar_prefetch=lead,
            grid=(steps,),
            in_specs=[spec for unused, spec in ins] + [ANYWHERE] * len(unread),
            out_specs=[spec for unused, spec in results],
            scratch_shapes=list(scratch),
        ),
        input_output_aliases={lead + len(ins) + i: i for i in range(len(prior))},
        compiler_params=pltpu.CompilerParams(vmem_limit_bytes=58 * MIB),
        cost_estimate=cost(2 * flops * steps * block, moved, weight),
        name=name,
    )(*([] if ids is None else [ids]), *[array for array, unused in ins], *unread)


def shape_of(shape, dtype):
    return jax.ShapeDtypeStruct(shape, dtype)


def fetch_pieces(ids_ref, plan, parts, out_ref, sems, start=0, owner_first=False):
    me, core = ids_ref[0], ids_ref[1] & 1
    rows = out_ref.shape[2]
    base = 2 * len(plan) if owner_first else 0
    copies = []
    for number, (which, mask, side) in enumerate(plan):
        part = parts[which]
        owner_core = core if side == 0 else 1 - core
        for share in range(2):
            piece = part.at[share] if part.shape[-2] == rows else part.at[share, pl.ds(start, rows)]
            place = (2 * owner_core + share, me ^ mask)
            target = out_ref.at[place[::-1] if owner_first else place]
            copies.append(pltpu.make_async_copy(piece, target, sems.at[base + 2 * number + share]))
    for copy in copies:
        copy.start()
    return copies


def fetch_halves(ids_ref, parts, out_ref, sems, start=0, owner_first=False):
    core = ids_ref[1] & 1
    rows = out_ref.shape[2]
    base = 4 if owner_first else 0
    copies = []
    for side, part in enumerate(parts):
        owner_core = core if side == 0 else 1 - core
        for share in range(2):
            piece = part.at[:, share] if part.shape[-2] == rows else part.at[:, share, pl.ds(start, rows)]
            block = 2 * owner_core + share
            target = out_ref.at[:, block] if owner_first else out_ref.at[block]
            copies.append(pltpu.make_async_copy(piece, target, sems.at[base + 2 * side + share]))
    for copy in copies:
        copy.start()
    return copies


def attention_rows(seg_length, x_ref, wqo_ref, proj_ref, probs_ref, mixed_ref, pre_ref):
    rows, width = x_ref.shape
    pairs = width // PAIR
    for part in range(3):
        proj_ref[:, part * width : (part + 1) * width] = dot_nn(x_ref[...], square(wqo_ref[part])).astype(BF16)
    first_half = lane_half((seg_length, PAIR))
    for seg in range(rows // seg_length):
        span = slice(seg * seg_length, (seg + 1) * seg_length)
        for pair in range(pairs):
            cols = [slice(part * width + pair * PAIR, part * width + (pair + 1) * PAIR) for part in range(3)]
            probs, mixed = pair_forward(
                proj_ref[span, cols[0]], proj_ref[span, cols[1]], proj_ref[span, cols[2]], first_half
            )
            probs_ref[seg, pair] = probs
            mixed_ref[span, cols[0]] = mixed.astype(BF16)
    pre_ref[...] = x_ref[...].astype(F32) + dot_nn(mixed_ref[...], square(wqo_ref[3]))


def attention_first_kernel(seg_length, plan, count, ids_ref, x_ref, *refs):
    parts, (proj_ref, probs_ref, mixed_ref, pre_ref, wqo_ref, sems) = refs[:count], refs[count:]

    @pl.when(pl.program_id(0) == 0)
    def fetch():
        for copy in fetch_pieces(ids_ref, plan, parts, wqo_ref, sems):
            copy.wait()

    attention_rows(seg_length, x_ref, wqo_ref, proj_ref, probs_ref, mixed_ref, pre_ref)


def attention_shapes(rows, width, seg_length):
    probs = shape_of((rows // seg_length, width // PAIR, seg_length, 2 * seg_length), BF16)
    return [
        shape_of((rows, 3 * width), BF16), (probs, seg_length), shape_of((rows, width), BF16), shape_of((rows, width), F32),
    ]


def attention_forward(rows_in, weight, seg_length, block, span, prior=(), after=(), pieces=None, ids=None):
    rows, width = rows_in.shape
    outs = attention_shapes(rows, width, seg_length)
    flops = width * (4 * width + 8 * seg_length)
    if pieces is None:
        return rows_call(
            partial(attention_rows, seg_length), "attention_forward", block, span, [rows_in],
            [(weight, whole(weight.shape))], outs, flops, prior, after, weight=SHORT,
        )
    plan, parts, shape = pieces
    return rows_call(
        partial(attention_first_kernel, seg_length, plan, len(parts)), "attention_forward", block, span, [rows_in],
        [(part, ANYWHERE) for part in parts], outs, flops, prior, after, [shape], ids,
        [pltpu.SemaphoreType.DMA((2 * len(plan),))], SHORT,
    )


def ffn_rows(pre_ref, wup_ref, wdown_ref, gains_ref, shifts_ref, low_ref, act_ref, slope_ref, pre2_ref):
    width = pre_ref.shape[1]
    unit, unused = norm_parts(pre_ref[...])
    total = unit * gains_ref[0:1].astype(F32) + shifts_ref[0:1].astype(F32)
    low = total.astype(BF16)
    low_ref[...] = low
    held = dot_nn(low, square(wup_ref[0]))
    for part in range(4):
        cols = slice(part * width, (part + 1) * width)
        ahead = dot_nn(low, square(wup_ref[part + 1])) if part < 3 else None
        act, slope = gelu_parts(held)
        act_ref[:, cols] = act.astype(BF16)
        slope_ref[:, cols] = slope.astype(BF16)
        total = total + dot_nn(act_ref[:, cols], down_block(wdown_ref, part))
        held = ahead
    pre2_ref[...] = total


def ffn_forward(pre_first, w_up, w_down, gains, shifts, block, span, prior=(), after=()):
    rows, width = pre_first.shape
    wide = shape_of((rows, 4 * width), BF16)
    return rows_call(
        ffn_rows, "ffn_forward", block, span, [pre_first],
        [(value, whole(value.shape)) for value in (w_up, w_down, gains, shifts)],
        [shape_of((rows, width), BF16), wide, wide, shape_of((rows, width), F32)], 8 * width * width, prior, after,
    )


def edge_rows(pre_ref, wup_ref, wdown_ref, gains_ref, shifts_ref, out_ref):
    unit, unused = norm_parts(pre_ref[...])
    total = unit * gains_ref[0:1].astype(F32) + shifts_ref[0:1].astype(F32)
    low = total.astype(BF16)
    for part in range(4):
        act, unused = gelu_parts(dot_nn(low, square(wup_ref[part])))
        total = total + dot_nn(act.astype(BF16), down_block(wdown_ref, part))
    unit, unused = norm_parts(total)
    out_ref[...] = unit * gains_ref[1:2].astype(F32) + shifts_ref[1:2].astype(F32)


def edge_first_kernel(ids_ref, pre_ref, gains_ref, shifts_ref, half_ref, other_ref, out_ref, wup_ref, wdown_ref, sems):
    parts = (half_ref, other_ref)
    up = fetch_halves(ids_ref, parts, wup_ref, sems)
    down = fetch_halves(ids_ref, parts, wdown_ref, sems, wup_ref.shape[2], True)
    for copy in up + down:
        copy.wait()
    edge_rows(pre_ref, wup_ref, wdown_ref, gains_ref, shifts_ref, out_ref)


def edge_forward(pre_edge, weights, gains, shifts, pieces=None, ids=None):
    rows, width = pre_edge.shape
    norms = [(gains, whole(gains.shape)), (shifts, whole(shifts.shape))]
    outs = [shape_of((rows, width), F32)]
    if pieces is None:
        return rows_call(
            edge_rows, "edge_forward", rows, (0, 1), [pre_edge], [(value, whole(value.shape)) for value in weights] + norms,
            outs, 60 * width * width,
        )
    parts, shapes = pieces
    return rows_call(
        edge_first_kernel, "edge_forward", rows, (0, 1), [pre_edge], norms + [(part, ANYWHERE) for part in parts], outs,
        60 * width * width, extra=shapes, ids=ids, scratch=[pltpu.SemaphoreType.DMA((8,))],
    )


def norm_rows(seg_length, cot_ref, pre2_ref, edge_ref, cls_ref, gains_ref, shifts_ref, out_ref, branch_ref, grad_ref, sums_ref):
    rows, width = cot_ref.shape
    top = lax.broadcasted_iota(jnp.int32, (seg_length, width), 0) == 0

    def with_edge(values, edge):
        parts = [
            jnp.where(top, edge[seg], values[seg * seg_length : (seg + 1) * seg_length]) for seg in range(rows // seg_length)
        ]
        return jnp.concatenate(parts, axis=0) if len(parts) > 1 else parts[0]

    gain = gains_ref[1:2].astype(F32)
    unit, inverse = norm_parts(pre2_ref[...])
    out_ref[...] = with_edge(unit * gain + shifts_ref[1:2].astype(F32), cls_ref).astype(BF16)
    grad = with_edge(cot_ref[...].astype(F32), edge_ref)
    pre_grad = norm_back(grad, unit, inverse, gain)
    grad_ref[...] = pre_grad
    branch_ref[...] = pre_grad.astype(BF16)

    @pl.when(pl.program_id(0) == 0)
    def start_sums():
        sums_ref[...] = jnp.zeros_like(sums_ref)

    sums_ref[1:2] += jnp.sum(grad * unit, axis=0, keepdims=True)
    sums_ref[4:5] += jnp.sum(grad, axis=0, keepdims=True)


def norm_backward(cot, pre_second, edge, cls_new, gains, shifts, seg_length, block, after):
    rows, width = cot.shape
    return rows_call(
        partial(norm_rows, seg_length), "norm_backward", block, (0, rows // block),
        [cot, pre_second, (edge, seg_length), (cls_new, seg_length)],
        [(gains, whole(gains.shape)), (shifts, whole(shifts.shape))],
        [shape_of((rows, width), BF16), shape_of((rows, width), BF16), shape_of((rows, width), F32)], 2 * width,
        after=after, extra=[shape_of((8, width), F32)],
    )


def ffn_back_rows(branch_ref, grad2_ref, pre1_ref, slope_ref, wup_ref, wdown_ref, gains_ref, gradh_ref, grad1_ref, low1_ref, sums_ref):
    width = branch_ref.shape[1]
    total = grad2_ref[...]
    for part in range(4):
        cols = slice(part * width, (part + 1) * width)
        grad_act = dot_nt(branch_ref[...], down_block(wdown_ref, part))
        grad_hidden = (grad_act * slope_ref[:, cols].astype(F32)).astype(BF16)
        gradh_ref[:, cols] = grad_hidden
        total = total + dot_nt(grad_hidden, square(wup_ref[part]))
    unit, inverse = norm_parts(pre1_ref[...])
    grad1 = norm_back(total, unit, inverse, gains_ref[0:1].astype(F32))
    grad1_ref[...] = grad1
    low1_ref[...] = grad1.astype(BF16)

    @pl.when(pl.program_id(0) == 0)
    def start_sums():
        sums_ref[...] = jnp.zeros_like(sums_ref)

    sums_ref[0:1] += jnp.sum(total * unit, axis=0, keepdims=True)
    sums_ref[3:4] += jnp.sum(total, axis=0, keepdims=True)


def ffn_backward(branch, grad2, pre_first, slope, w_up, w_down, gains, block, span, weight, prior=(), after=()):
    rows, width = branch.shape
    return rows_call(
        ffn_back_rows, "ffn_backward", block, span, [branch, grad2, pre_first, slope],
        [(w_up, whole(w_up.shape)), (w_down, whole(w_down.shape)), (gains, whole(gains.shape))],
        [shape_of((rows, 4 * width), BF16), shape_of((rows, width), F32), shape_of((rows, width), BF16)],
        8 * width * width, prior, after, [shape_of((8, width), F32)], weight=weight,
    )


def attention_back_rows(seg_length, grad1_ref, low1_ref, proj_ref, probs_ref, wqo_ref, gradp_ref, input_ref, gradm_ref):
    rows, width = grad1_ref.shape
    pairs = width // PAIR
    gradm_ref[...] = dot_nt(low1_ref[...], square(wqo_ref[3])).astype(BF16)
    first_half = lane_half((seg_length, PAIR))
    for seg in range(rows // seg_length):
        span = slice(seg * seg_length, (seg + 1) * seg_length)
        for pair in range(pairs):
            cols = [slice(part * width + pair * PAIR, part * width + (pair + 1) * PAIR) for part in range(3)]
            grads = pair_backward(
                proj_ref[span, cols[0]], proj_ref[span, cols[1]], proj_ref[span, cols[2]],
                probs_ref[seg, pair], gradm_ref[span, cols[0]], first_half,
            )
            for place, grad in zip(cols, grads):
                gradp_ref[span, place] = grad.astype(BF16)
    total = grad1_ref[...]
    for part in range(3):
        total = total + dot_nt(gradp_ref[:, part * width : (part + 1) * width], square(wqo_ref[part]))
    input_ref[...] = total


def attention_backward(grad1, low1, proj, probs, w_qo, seg_length, block, span, prior=(), after=()):
    rows, width = grad1.shape
    return rows_call(
        partial(attention_back_rows, seg_length), "attention_backward", block, span,
        [grad1, low1, proj, (probs, seg_length)], [(w_qo, whole(w_qo.shape))],
        [shape_of((rows, 3 * width), BF16), shape_of((rows, width), F32)],
        width * (4 * width + 16 * seg_length), prior, after, scratch=[pltpu.VMEM((block, width), BF16)], weight=SHORT,
    )


def cross_kernel(
    local, fetch, ids_ref, rows_ref, cot_ref, keyc_ref, keyr_ref, place_ref, table_ref, gains_ref, shifts_ref, *refs
):
    parts, refs = (refs[:2], refs[2:]) if fetch else (refs[:1], refs[1:])
    new_ref, edge_ref, low_ref, gradp_ref, mixed_ref, gradz_ref, sums_ref, table_grad_ref, proj_ref, probs_ref, gradm_ref = refs[:11]
    wc_ref = parts[0]
    if fetch:
        wc_ref, sems = refs[11:]
        for copy in fetch_halves(ids_ref, parts, wc_ref, sems):
            copy.wait()
    count, width = rows_ref.shape
    pairs = width // PAIR
    entries = table_ref.shape[0]
    picks = place_ref[...] == lax.broadcasted_iota(jnp.int32, (count, entries), 1)
    embedded = rows_ref[...] + dot_nn(picks.astype(BF16), table_ref[...])
    low = embedded.astype(BF16)
    low_ref[...] = low
    for part in range(3):
        proj_ref[:, part * width : (part + 1) * width] = dot_nn(low, square(wc_ref[part])).astype(BF16)
    first_half = lane_half((count, PAIR))
    same = keyc_ref[...] == keyr_ref[...]
    places = [
        [slice(part * width + pair * PAIR, part * width + (pair + 1) * PAIR) for part in range(3)] for pair in range(pairs)
    ]
    for pair, cols in enumerate(places):
        probs, mixed = pair_forward(proj_ref[:, cols[0]], proj_ref[:, cols[1]], proj_ref[:, cols[2]], first_half, same)
        probs_ref[pair] = probs
        mixed_ref[:, cols[0]] = mixed.astype(BF16)
    pre_third = embedded + dot_nn(mixed_ref[...], square(wc_ref[3]))
    unit, inverse = norm_parts(pre_third)
    gain = gains_ref[2:3].astype(F32)
    new_ref[...] = unit[:local] * gain + shifts_ref[2:3].astype(F32)
    grad_out = cot_ref[...]
    grad_third = norm_back(grad_out, unit, inverse, gain)
    sums_ref[...] = jnp.zeros_like(sums_ref)
    sums_ref[2:3] = jnp.sum(grad_out[:local] * unit[:local], axis=0, keepdims=True)
    sums_ref[5:6] = jnp.sum(grad_out[:local], axis=0, keepdims=True)
    gradz = grad_third.astype(BF16)
    gradz_ref[...] = gradz
    gradm_ref[...] = dot_nt(gradz, square(wc_ref[3])).astype(BF16)
    for pair, cols in enumerate(places):
        grads = pair_backward(
            proj_ref[:, cols[0]], proj_ref[:, cols[1]], proj_ref[:, cols[2]], probs_ref[pair], gradm_ref[:, cols[0]], first_half
        )
        for place, grad in zip(cols, grads):
            gradp_ref[:, place] = grad.astype(BF16)
    grad_edge = grad_third[:local]
    for part in range(3):
        grad_edge = grad_edge + dot_nt(gradp_ref[:local, part * width : (part + 1) * width], square(wc_ref[part]))
    edge_ref[...] = grad_edge
    table_grad_ref[...] = lax.dot_general(
        picks[:local].astype(F32), grad_edge, (((0,), (0,)), ((), ())),
        precision=lax.Precision.HIGHEST, preferred_element_type=F32,
    )


def cross_block(ids, local, edge_rows, edge_cot, key_col, key_row, place, table, gains, shifts, parts, shape):
    count, width = edge_rows.shape
    read = [edge_rows, edge_cot, key_col, key_row, place, table, gains, shifts]
    part_specs, fetched = [whole(part.shape) for part in parts], []
    if shape is not None:
        part_specs = [ANYWHERE] * len(parts)
        fetched = [pltpu.VMEM(shape.shape, BF16), pltpu.SemaphoreType.DMA((4,))]
    shapes = (
        jax.ShapeDtypeStruct((local, width), F32),
        jax.ShapeDtypeStruct((local, width), F32),
        jax.ShapeDtypeStruct((count, width), BF16),
        jax.ShapeDtypeStruct((count, 3 * width), BF16),
        jax.ShapeDtypeStruct((count, width), BF16),
        jax.ShapeDtypeStruct((count, width), BF16),
        jax.ShapeDtypeStruct((8, width), F32),
        jax.ShapeDtypeStruct(table.shape, F32),
    )
    return pl.pallas_call(
        partial(cross_kernel, local, shape is not None),
        out_shape=shapes,
        grid_spec=pltpu.PrefetchScalarGridSpec(
            num_scalar_prefetch=1,
            grid=(1,),
            in_specs=[whole(value.shape) for value in read] + part_specs,
            out_specs=[whole(value.shape) for value in shapes],
            scratch_shapes=[
                pltpu.VMEM((count, 3 * width), BF16),
                pltpu.VMEM((width // PAIR, count, 2 * count), BF16),
                pltpu.VMEM((count, width), BF16),
            ] + fetched,
        ),
        compiler_params=pltpu.CompilerParams(vmem_limit_bytes=56 * MIB),
        cost_estimate=cost(10_000_000_000, width * width * 8),
        name="cross_block",
    )(ids, *read, *parts)


def cols_grad_kernel(ids_ref, left_ref, right_ref, *refs):
    refs[-1][0] = dot_tn(left_ref[...], right_ref[...]).astype(BF16)


def joint_grad_kernel(side, ids_ref, left_ref, last_left_ref, right_ref, last_right_ref, *refs):
    block = half_block(side, pl.program_id(0), ids_ref)

    @pl.when(block < 3)
    def main():
        refs[-1][0] = dot_tn(left_ref[...], right_ref[...]).astype(BF16)

    @pl.when(block == 3)
    def last():
        refs[-1][0] = dot_tn(last_left_ref[...], last_right_ref[...]).astype(BF16)


def half_block(side, step, ids):
    return 2 * ((ids[1] & 1) ^ side) + step


def half_grads(kernel, name, side, ids, operands, specs, after, weight):
    rows, width = operands[0].shape
    return pl.pallas_call(
        kernel,
        out_shape=jax.ShapeDtypeStruct((2, width, width), BF16),
        grid_spec=pltpu.PrefetchScalarGridSpec(
            num_scalar_prefetch=1,
            grid=(2,),
            in_specs=specs + [ANYWHERE] * len(after),
            out_specs=pl.BlockSpec((1, width, width), lambda j, ids: (j, 0, 0)),
        ),
        compiler_params=pltpu.CompilerParams(vmem_limit_bytes=56 * MIB),
        cost_estimate=cost(4 * rows * width * width, 10 * rows * width, weight),
        name=name,
    )(ids, *operands, *after)


def cols_grads(side, ids, left, right, after, weight):
    rows, width = left.shape
    specs = [
        whole(left.shape),
        pl.BlockSpec((rows, width), lambda j, ids: (0, half_block(side, j, ids))),
    ]
    return half_grads(cols_grad_kernel, "cols_grads", side, ids, [left, right], specs, after, weight)


def joint_grads(side, ids, left, last_left, right, last_right, after, weight):
    rows, width = left.shape
    specs = [
        whole(left.shape),
        whole(left.shape),
        pl.BlockSpec((rows, width), lambda j, ids: (0, jnp.minimum(half_block(side, j, ids), 2))),
        whole(left.shape),
    ]
    operands = [left, last_left, right, last_right]
    return half_grads(partial(joint_grad_kernel, side), "joint_grads", side, ids, operands, specs, after, weight)


def rows_grad_kernel(ids_ref, left_ref, right_ref, *refs):
    send_ref, keep_ref, held_ref = refs[-3:]
    core = ids_ref[1] & 1
    held_ref[...] = dot_tn(left_ref[...], right_ref[...]).reshape(held_ref.shape)
    for share in range(2):
        send_ref[share] = held_ref[:, 2 * (1 - core) + share].astype(BF16)
        keep_ref[share] = held_ref[:, 2 * core + share].astype(BF16)


def rows_grads(ids, left, right, count, after):
    rows, width = right.shape
    hidden = left.shape[1]
    shard_rows = hidden // count // 4
    owners = count // 4
    half = jax.ShapeDtypeStruct((2, count, shard_rows, width), BF16)
    out_spec = pl.BlockSpec((2, owners, shard_rows, width), lambda j, ids: (0, j, 0, 0))
    return pl.pallas_call(
        rows_grad_kernel,
        out_shape=(half, half),
        grid_spec=pltpu.PrefetchScalarGridSpec(
            num_scalar_prefetch=1,
            grid=(4,),
            in_specs=[
                pl.BlockSpec((rows, hidden // 4), lambda j, ids: (0, j)),
                pl.BlockSpec((rows, width), lambda j, ids: (0, 0), pipeline_mode=pl.Buffered(1)),
            ] + [ANYWHERE] * len(after),
            out_specs=[out_spec, out_spec],
            scratch_shapes=[pltpu.VMEM((owners, 4, shard_rows, width), F32)],
        ),
        compiler_params=pltpu.CompilerParams(vmem_limit_bytes=56 * MIB),
        cost_estimate=cost(2 * rows * width * hidden, 10 * rows * width),
        name="rows_grads",
    )(ids, left, right, *after)


def later(value, *first):
    return lax.optimization_barrier((value,) + first)[0]


def seg_swap(value, mask):
    count = lax.axis_size("seg")
    return lax.ppermute(value, "seg", [(i, i ^ mask) for i in range(count)])


def rep_swap(value, mask):
    count = lax.axis_size("rep")
    return lax.ppermute(value, "rep", [(i, i ^ mask) for i in range(count)])


def both_swap(value, seg_mask, rep_mask):
    reps = lax.axis_size("rep")
    total = lax.axis_size("seg") * reps
    pairs = [(i, ((i // reps) ^ seg_mask) * reps + ((i % reps) ^ rep_mask)) for i in range(total)]
    return lax.ppermute(value, ("seg", "rep"), pairs)


def place_kernel(plan, count, owner_first, ids_ref, *refs):
    for copy in fetch_pieces(ids_ref, plan, refs[:count], refs[count], refs[count + 1], 0, owner_first):
        copy.wait()


def put_in_place(ids, pieces, owner_first=False):
    plan, parts, shape = pieces
    return pl.pallas_call(
        partial(place_kernel, plan, len(parts), owner_first),
        out_shape=shape,
        in_specs=[pl.BlockSpec(memory_space=pltpu.SMEM)] + [ANYWHERE] * len(parts),
        out_specs=pl.BlockSpec(memory_space=pltpu.VMEM),
        scratch_shapes=[pltpu.SemaphoreType.DMA((4 * len(plan),))],
        compiler_params=pltpu.CompilerParams(vmem_limit_bytes=32 * MIB),
        cost_estimate=cost(0, 4 * shape.size),
        name="put_in_place",
    )(ids, *parts)


def own_half(ids, blocks):
    return lax.dynamic_slice_in_dim(blocks, 2 * (ids[1] & 1), 2, 0)


def far_pieces(piece):
    return [piece] + [seg_swap(piece, mask) for mask in range(2, lax.axis_size("seg"), 2)]


def after_all(value, first):
    return later(value, *first) if first else value


def gather_singly(piece, evens, firsts):
    held, crossed = [], []
    for number, even in enumerate(evens):
        before = held[-1:] + [rep_swap(part, 1) for part in held[-4:-2]]
        crossed += before[1:]
        held += [even, seg_swap(after_all(even, before + firsts.get(number, [])), 1)]
    crossed += [rep_swap(part, 1) for part in held[-4:-1]] + [rep_swap(after_all(held[-1], firsts.get(-1, [])), 1)]
    return held, crossed


def pieces_of(held, crossed, shapes):
    count = len(held)
    return [(i, i % count, i // count) for i in range(2 * count)], held + crossed, shapes


class Gather:
    def __init__(self, piece):
        self.piece, self.came = piece, far_pieces(piece)

    def across(self, *first):
        self.evens = jnp.stack(self.came[:1] + [later(value, *first) for value in self.came[1:]], axis=0)
        self.came = seg_swap(self.evens, 1)

    def finish(self, *first):
        return jnp.stack([self.evens, later(self.came, *first)], axis=1).reshape((-1,) + self.piece.shape)


def spread_kernel(ids_ref, keep_ref, came_ref, stay_ref, x_ref, y_ref, xy_ref):
    near, across = ids_ref[0] & 1, ids_ref[1] >> 1

    def total(share, side):
        return (keep_ref[share, 0, side].astype(F32) + came_ref[share, 0, side].astype(F32)).astype(BF16)

    stay_ref[0] = total(across, near)
    x_ref[0] = total(across, 1 - near)
    y_ref[0] = total(1 - across, near)
    xy_ref[0] = total(1 - across, 1 - near)


def spread(ids, keep, came):
    unused, count, rows, width = keep.shape
    far = count // 2
    shape = (2, far, 2, rows, width)
    in_spec = pl.BlockSpec((2, 1, 2, rows, width), lambda j: (0, j, 0, 0, 0))
    out_spec = pl.BlockSpec((1, rows, width), lambda j: (j, 0, 0))
    out = jax.ShapeDtypeStruct((far, rows, width), BF16)
    return pl.pallas_call(
        spread_kernel,
        out_shape=(out,) * 4,
        grid=(far,),
        in_specs=[pl.BlockSpec(memory_space=pltpu.SMEM), in_spec, in_spec],
        out_specs=[out_spec] * 4,
        compiler_params=pltpu.CompilerParams(vmem_limit_bytes=32 * MIB),
        cost_estimate=cost(0, 12 * count * rows * width),
        name="spread",
    )(ids, keep.reshape(shape), came.reshape(shape))


def settle_kernel(ids_ref, a_ref, b_ref, c_ref, d_ref, *outs):
    far = ids_ref[0] >> 1
    for mask, out in enumerate(outs):
        place = far ^ mask
        total = (a_ref[place].astype(F32) + b_ref[place].astype(F32)) + (c_ref[place].astype(F32) + d_ref[place].astype(F32))
        out[...] = total.astype(BF16)


def settle(ids, parts):
    far, rows, width = parts[0].shape
    whole_spec = pl.BlockSpec(memory_space=pltpu.VMEM)
    return pl.pallas_call(
        settle_kernel,
        out_shape=(jax.ShapeDtypeStruct((rows, width), BF16),) * far,
        in_specs=[pl.BlockSpec(memory_space=pltpu.SMEM)] + [whole_spec] * 4,
        out_specs=[whole_spec] * far,
        compiler_params=pltpu.CompilerParams(vmem_limit_bytes=32 * MIB),
        cost_estimate=cost(0, 10 * far * rows * width),
        name="settle",
    )(ids, *parts)


def halve(value, axis, bit):
    own = lax.dynamic_index_in_dim(value, bit, axis, keepdims=False)
    other = lax.dynamic_index_in_dim(value, 1 - bit, axis, keepdims=False)
    return own, other


class Reduction:
    def __init__(self, ids, send, keep):
        count = lax.axis_size("seg")
        self.ids = ids
        self.shape = (2, count, send.size // (2 * count * send.shape[-1]), send.shape[-1])
        self.keep = keep
        self.came = rep_swap(send, 1)

    def spread(self, *first):
        came = later(self.came, *first)
        self.stay, *sends = spread(self.ids, self.keep.reshape(self.shape), came.reshape(self.shape))
        self.came = [seg_swap(sends[0], 1), rep_swap(sends[1], 2), both_swap(sends[2], 1, 2)]

    def settle(self, *first):
        self.own, *others = settle(self.ids, [self.stay] + [later(value, *first) for value in self.came])
        self.came = [seg_swap(other, 2 * mask) for mask, other in enumerate(others, 1)]

    def finish(self, *first):
        total = self.own.astype(F32)
        for value in self.came:
            total = total + later(value, *first).astype(F32)
        return total.astype(BF16)


class Sharing:
    def __init__(self, ids, value):
        self.ids, self.value = ids, value
        self.came = rep_swap(value, 2)

    def step(self, *first):
        self.value = jnp.stack([self.value, later(self.came, *first)], axis=0)
        self.came = rep_swap(self.value, 1)

    def finish(self, *first):
        held = jnp.concatenate([self.value, later(self.came, *first)], axis=0)
        order = jnp.array([0, 2, 1, 3], jnp.int32)
        return [
            lax.dynamic_index_in_dim(held, order[self.ids[1] ^ owner], 0, keepdims=False).astype(F32)
            for owner in (0, 2, 1, 3)
        ]


class SmallReduction:
    def __init__(self, ids, value):
        self.ids, self.mask = ids, lax.axis_size("seg") // 2
        self.split(value)

    def split(self, value):
        bit = (self.ids[0] // self.mask) & 1
        self.own, self.other = halve(value.reshape((2, self.mask) + value.shape[1:]), 0, bit)
        self.came = seg_swap(self.other, self.mask)
        self.mask //= 2

    def step(self, *first):
        value = self.own + later(self.came, *first)
        if self.mask:
            self.split(value)
        elif value.ndim == 3:
            self.own = self.other = value[0]
            self.came = rep_swap(self.own, 1)
        else:
            self.own = self.other = value
            self.came = rep_swap(self.own, 2)
            self.last = True

    def finish(self, *first):
        while not getattr(self, "last", False):
            self.step(*first)
        return self.own + later(self.came, *first)


def body(tokens, cotangent, doc_counts, w_qkv, w_out, w_up, w_down, c_qkv, c_out, pos_table, norm_gains, norm_shifts):
    micro_count, unused, seg_local, seg_length, width = tokens.shape
    count = lax.axis_size("seg")
    me = lax.axis_index("seg").astype(jnp.int32)
    rep = lax.axis_index("rep").astype(jnp.int32)
    ids = jnp.stack([me, rep])
    shard_rows = w_qkv.shape[0]
    local = micro_count * seg_local
    rows = local * seg_length
    table_rows = pos_table.shape[0]
    norm_cols = norm_gains.shape[1]
    aligned = shard_rows % 16 == 0

    def shares_of(matrix):
        return matrix.reshape(shard_rows, 4, width).transpose(1, 0, 2)

    def own_share(matrix):
        return lax.dynamic_slice_in_dim(matrix, rep * width, width, 1)

    norms = jnp.pad(jnp.concatenate([norm_gains, norm_shifts], axis=0), ((0, 2), (0, width - norm_cols)))
    small = jnp.pad(jnp.stack([pos_table, norms], axis=0), ((0, 0), (0, 16 - table_rows), (0, 0)))
    ffn_piece = jnp.concatenate(
        [own_half(ids, shares_of(w_up)), own_half(ids, w_down.reshape(4, shard_rows, width)), small], axis=1
    )
    ffn_half = lax.all_gather(ffn_piece, "seg", axis=0)
    qo_piece = own_half(ids, shares_of(jnp.concatenate([w_qkv, w_out], axis=1)))
    qo_evens = far_pieces(qo_piece)
    shapes = [shape_of((4, count, shard_rows, width), BF16), shape_of((count, 4, shard_rows, width), BF16)]
    qo_pieces = pieces_of(*gather_singly(qo_piece, qo_evens, {}), shapes[0])
    cross_piece = own_half(ids, shares_of(jnp.concatenate([c_qkv, c_out], axis=1)))
    cross_half = lax.all_gather(later(cross_piece, qo_evens[1]), "seg", axis=0)

    counts = doc_counts[:, 0]
    ends = jnp.cumsum(counts, axis=1)
    owners = me ^ jnp.arange(count, dtype=jnp.int32)
    seg_ids = owners[:, None, None] * seg_local + jnp.arange(seg_local, dtype=jnp.int32)[None, None, :]
    seg_ids = jnp.broadcast_to(seg_ids, (count, micro_count, seg_local))
    past = seg_ids[..., None] >= ends[None, :, None, :]
    doc_ids = jnp.sum(past.astype(jnp.int32), axis=-1)
    starts = jnp.sum(jnp.where(past, counts[None, :, None, :], 0), axis=-1)
    places = (seg_ids - starts).reshape(-1, 1)
    keys = (doc_ids + (counts.shape[1] + 1) * jnp.arange(micro_count, dtype=jnp.int32)[None, :, None]).reshape(-1)

    flat = tokens.reshape(rows, width)
    cot = cotangent.reshape(rows, width)
    block = 4 * seg_length
    steps = rows // block
    halves_of = ((0, steps // 2), (steps // 2, steps - steps // 2))

    everything = (0, steps)
    if aligned:
        proj, probs, mixed, pre_first, full_qo = attention_forward(
            flat, None, seg_length, block, everything, pieces=qo_pieces, ids=ids
        )
    else:
        full_qo = put_in_place(ids, qo_pieces).reshape(4, 1, width, width)
        proj, probs, mixed, pre_first = attention_forward(flat, full_qo, seg_length, block, everything)
    ffn_half = later(ffn_half, proj)
    small = ffn_half[:, :, 2 * shard_rows :]
    table = small[:, 0, :table_rows].reshape(count * table_rows, width)
    norms = small[:, 1, :6, :norm_cols].transpose(1, 0, 2).reshape(6, width)
    gains, shifts = norms[:3], norms[3:]
    ffn_other = rep_swap(ffn_half, 1)

    def joined(parts, start, owner_first):
        own, other = [part[:, :, start : start + shard_rows] for part in parts]
        both = jnp.where((rep & 1) == 0, jnp.concatenate([own, other], axis=1), jnp.concatenate([other, own], axis=1))
        return (both if owner_first else both.transpose(1, 0, 2, 3)).reshape(4, 1, width, width)

    pre_edge = pre_first.reshape(local, seg_length, width)[:, 0]
    if aligned:
        edge, full_up, full_down = edge_forward(
            pre_edge, None, gains, shifts, ([ffn_half, ffn_other], shapes), ids
        )
    else:
        full_up = joined([ffn_half, ffn_other], 0, False)
        full_down = joined([ffn_half, ffn_other], shard_rows, True)
        edge = edge_forward(pre_edge, [full_up, full_down], gains, shifts)[0]
    edge_cot = cot.reshape(local, seg_length, width)[:, 0].astype(F32)
    edges = Gather(jnp.stack([edge, edge_cot], axis=0))
    kept = ffn_forward(pre_first, full_up, full_down, gains, shifts, block, halves_of[0], after=[edge])
    edges.across(kept[0])
    low, act, slope, pre_second = ffn_forward(
        pre_first, full_up, full_down, gains, shifts, block, halves_of[1], prior=kept, after=[edges.evens]
    )
    edges = edges.finish(pre_second)
    cross_half = later(cross_half, pre_second)
    cross_parts, cross_shape = [cross_half, rep_swap(cross_half, 1)], shapes[0]
    if not aligned:
        cross_parts, cross_shape = [joined(cross_parts, 0, False)], None
    cls_new, grad_edge, c_low, c_gradp, c_mixed, c_gradz, c_sums, table_grad = cross_block(
        ids, local, edges[:, 0].reshape(-1, width), edges[:, 1].reshape(-1, width),
        keys[:, None], jnp.concatenate([keys, keys])[None, :], places, table, gains, shifts, cross_parts, cross_shape,
    )
    own_low = lax.dynamic_slice_in_dim(c_low, me * shard_rows, shard_rows, 1)
    own_mixed = lax.dynamic_slice_in_dim(c_mixed, me * shard_rows, shard_rows, 1)
    grad_c = shares_of(jnp.concatenate([dot_tn(own_low, c_gradp), dot_tn(own_mixed, c_gradz)], axis=1)).astype(BF16)
    c_own, c_other = halve(grad_c.reshape(2, 2, shard_rows, width), 0, rep & 1)
    c_came = rep_swap(c_other, 1)
    layer_out, branch, grad2, sums2 = norm_backward(
        cot, pre_second, grad_edge[:, None], cls_new[:, None], gains, shifts, seg_length, block, [c_other]
    )
    c_own, c_other = halve(c_own.astype(F32) + later(c_came, branch).astype(F32), 0, rep >> 1)
    c_other = c_other.astype(BF16)
    c_came = rep_swap(c_other, 2)
    send_down, keep_down = rows_grads(ids, act, branch, count, [c_other])
    c_share = (c_own + later(c_came, send_down).astype(F32)).astype(BF16)
    down = Reduction(ids, send_down, keep_down)
    grad_hidden, grad1, low1, sums1 = ffn_backward(
        branch, grad2, pre_first, slope, full_up, full_down, gains, block, everything, LONG, after=[send_down, c_share]
    )
    down.spread(grad1)
    send_up = cols_grads(1, ids, low, grad_hidden, [down.stay], SHORT)
    norm_sums = (later(sums2, send_up) + sums1 + c_sums).reshape(8, count, norm_cols).transpose(1, 0, 2)
    norm_sums = jnp.pad(norm_sums, ((0, 0), (0, 0), (0, width - norm_cols)))
    tiny = SmallReduction(ids, jnp.concatenate([norm_sums, table_grad.reshape(count, table_rows, width)], axis=1))
    keep_up = cols_grads(0, ids, low, grad_hidden, [send_up, tiny.other], LONG)
    up = Reduction(ids, send_up, keep_up)
    up.spread(keep_up)
    grad_proj, input_grad = attention_backward(
        grad1, low1, proj, probs, full_qo, seg_length, block, everything, after=[up.stay]
    )
    down.settle(grad_proj)
    up.settle(grad_proj)
    send_qo = joint_grads(1, ids, flat, mixed, grad_proj, low1, [up.own, down.own], SHORT)
    keep_qo = joint_grads(0, ids, flat, mixed, grad_proj, low1, [send_qo], LONG)
    qo = Reduction(ids, send_qo, keep_qo)
    tiny.step(send_qo)
    early = Sharing(ids, jnp.stack([down.finish(keep_qo), up.finish(keep_qo), c_share], axis=0))
    tiny.step(keep_qo)
    qo.spread(early.value, tiny.other)
    early.step(qo.came[0])
    tiny.step(qo.came[0])
    qo.settle()
    early_shares = early.finish(qo.own)
    tiny.step(qo.own)
    qo_share = qo.finish()
    summed = tiny.finish(qo_share)
    late = Sharing(ids, qo_share)
    late.step()
    late_shares = late.finish()

    def side_by_side(parts):
        return jnp.concatenate(parts, axis=1)

    return (
        layer_out.reshape(tokens.shape),
        input_grad.reshape(tokens.shape),
        side_by_side(late_shares[:3]),
        late_shares[3],
        side_by_side([part[1] for part in early_shares]),
        jnp.concatenate([part[0] for part in early_shares], axis=0),
        side_by_side([part[2] for part in early_shares[:3]]),
        early_shares[3][2],
        summed[8:],
        summed[:3, :norm_cols],
        summed[3:6, :norm_cols],
    )


def solution(mesh):
    rows = P(None, "rep", "seg", None, None)
    split = P("seg", None)
    last = P(None, "seg")
    return jax.shard_map(
        body,
        mesh=mesh,
        in_specs=(rows, rows, P(None, "rep", None)) + (split,) * 7 + (last, last),
        out_specs=(rows, rows) + (split,) * 7 + (last, last),
        check_vma=False,
    )
```

```python
from functools import partial
import jax
import jax.numpy as jnp
from jax import lax
from jax.experimental import pallas as pl
from jax.experimental.pallas import tpu as pltpu
from jax.sharding import PartitionSpec as P

HEAD_DIM = 64
PAIR = 2 * HEAD_DIM
EPSILON = 1e-05
NEGATIVE = -1e30
F32 = jnp.float32
BF16 = jnp.bfloat16
MIB = 1 << 20
LONG, SHORT = 6.0, 0.001


def dot_nn(left, right):
    return lax.dot_general(left, right, (((1,), (0,)), ((), ())), preferred_element_type=F32)


def dot_nt(left, right):
    return lax.dot_general(left, right, (((1,), (1,)), ((), ())), preferred_element_type=F32)


def dot_tn(left, right):
    return lax.dot_general(left, right, (((0,), (0,)), ((), ())), preferred_element_type=F32)


def norm_parts(values):
    center = values - jnp.mean(values, axis=-1, keepdims=True)
    spread = jnp.mean(center * center, axis=-1, keepdims=True)
    inverse = lax.rsqrt(spread + EPSILON)
    return center * inverse, inverse


def norm_back(grad, unit, inverse, gain):
    scaled = grad * gain
    first = jnp.mean(scaled, axis=-1, keepdims=True)
    second = jnp.mean(scaled * unit, axis=-1, keepdims=True)
    return inverse * (scaled - first - unit * second)


def gelu_parts(hidden):
    phi = 0.5 + 0.5 * lax.erf(hidden * 0.5 ** 0.5)
    bell = jnp.exp(hidden * hidden * -0.5) * 0.3989422804014327
    return hidden * phi, phi + hidden * bell


def halves(pair, first_half):
    zero = jnp.zeros_like(pair)
    return jnp.concatenate([jnp.where(first_half, pair, zero), jnp.where(first_half, zero, pair)], axis=0)


def pair_forward(query, key, value, first_half, same=None):
    rows = query.shape[0]
    scores = dot_nt(key, halves(query * BF16(HEAD_DIM ** -0.5), first_half))
    if same is not None:
        scores = jnp.where(same, scores, NEGATIVE)
    raised = jnp.exp(scores - jnp.max(scores, axis=0, keepdims=True))
    probs = (raised * (1.0 / jnp.sum(raised, axis=0, keepdims=True))).astype(BF16)
    both = dot_tn(probs, value)
    return probs, jnp.where(first_half, both[:rows], both[rows:])


def pair_backward(query, key, value, probs, grad_mixed, first_half):
    rows = query.shape[0]
    grad_both = halves(grad_mixed, first_half)
    query_both = halves(query * BF16(HEAD_DIM ** -0.5), first_half)
    grad_probs = dot_nt(value, grad_both)
    wide = probs.astype(F32)
    grad_scores = (wide * (grad_probs - jnp.sum(grad_probs * wide, axis=0, keepdims=True))).astype(BF16)
    grad_value = dot_nn(probs, grad_both)
    grad_key = dot_nn(grad_scores, query_both)
    both = dot_tn(grad_scores, key)
    grad_query = jnp.where(first_half, both[:rows], both[rows:]) * (HEAD_DIM ** -0.5)
    return grad_query, grad_key, grad_value


def lane_half(shape):
    return lax.broadcasted_iota(jnp.int32, shape, 1) % PAIR < HEAD_DIM


def square(value):
    return value.reshape(-1, value.shape[-1])


def up_block(ref, part):
    return square(ref[:, part])


def down_block(ref, part):
    count = ref.shape[0] // 4
    return square(ref[part * count : (part + 1) * count])


def whole(shape):
    return pl.BlockSpec(shape, lambda *at: (0,) * len(shape), pipeline_mode=pl.Buffered(1))


ANYWHERE = pl.BlockSpec(memory_space=pl.ANY)


def cost(flops, moved, weight=1.0):
    return pl.CostEstimate(flops=int(flops * weight), bytes_accessed=int(moved * weight), transcendentals=0)


def rows_call(kernel, name, block, span, rowed, fixed, outs, flops, prior=(), after=(), extra=(), ids=None, scratch=(), weight=1.0):
    first, steps = span

    def cut(value):
        array, ratio = value if isinstance(value, tuple) else (value, 1)
        shape = (block // ratio,) + array.shape[1:]
        return array, pl.BlockSpec(shape, lambda i, *ids: (i + first,) + (0,) * (len(shape) - 1))

    ins = [cut(value) for value in rowed] + list(fixed)
    results = [cut(value) for value in outs] + [(shape, whole(shape.shape)) for shape in extra]
    unread = list(prior) + list(after)
    lead = 0 if ids is None else 1
    moved = sum(value.size * value.dtype.itemsize for value, unused in ins + results) // 2

    def run(*refs):
        start = lead + len(ins)
        kernel(*refs[:start], *refs[start + len(unread) :])

    return pl.pallas_call(
        run,
        out_shape=tuple(jax.ShapeDtypeStruct(shape.shape, shape.dtype) for shape, unused in results),
        grid_spec=pltpu.PrefetchScalarGridSpec(
            num_scalar_prefetch=lead,
            grid=(steps,),
            in_specs=[spec for unused, spec in ins] + [ANYWHERE] * len(unread),
            out_specs=[spec for unused, spec in results],
            scratch_shapes=list(scratch),
        ),
        input_output_aliases={lead + len(ins) + i: i for i in range(len(prior))},
        compiler_params=pltpu.CompilerParams(vmem_limit_bytes=58 * MIB),
        cost_estimate=cost(2 * flops * steps * block, moved, weight),
        name=name,
    )(*([] if ids is None else [ids]), *[array for array, unused in ins], *unread)


def shape_of(shape, dtype):
    return jax.ShapeDtypeStruct(shape, dtype)


def fetch_pieces(ids_ref, plan, parts, out_ref, sems, start=0, owner_first=False):
    me, core = ids_ref[0], ids_ref[1] & 1
    rows = out_ref.shape[2]
    base = 2 * len(plan) if owner_first else 0
    copies = []
    for number, (which, mask, side) in enumerate(plan):
        part = parts[which]
        owner_core = core if side == 0 else 1 - core
        for share in range(2):
            piece = part.at[share] if part.shape[-2] == rows else part.at[share, pl.ds(start, rows)]
            place = (2 * owner_core + share, me ^ mask)
            target = out_ref.at[place[::-1] if owner_first else place]
            copies.append(pltpu.make_async_copy(piece, target, sems.at[base + 2 * number + share]))
    for copy in copies:
        copy.start()
    return copies


def fetch_halves(ids_ref, parts, out_ref, sems, start=0, owner_first=False):
    core = ids_ref[1] & 1
    rows = out_ref.shape[2]
    base = 4 if owner_first else 0
    copies = []
    for side, part in enumerate(parts):
        owner_core = core if side == 0 else 1 - core
        for share in range(2):
            piece = part.at[:, share] if part.shape[-2] == rows else part.at[:, share, pl.ds(start, rows)]
            block = 2 * owner_core + share
            target = out_ref.at[:, block] if owner_first else out_ref.at[block]
            copies.append(pltpu.make_async_copy(piece, target, sems.at[base + 2 * side + share]))
    for copy in copies:
        copy.start()
    return copies


def attention_rows(seg_length, x_ref, wqo_ref, proj_ref, probs_ref, mixed_ref, pre_ref):
    rows, width = x_ref.shape
    pairs = width // PAIR
    for part in range(3):
        proj_ref[:, part * width : (part + 1) * width] = dot_nn(x_ref[...], square(wqo_ref[part])).astype(BF16)
    first_half = lane_half((seg_length, PAIR))
    for seg in range(rows // seg_length):
        span = slice(seg * seg_length, (seg + 1) * seg_length)
        for pair in range(pairs):
            cols = [slice(part * width + pair * PAIR, part * width + (pair + 1) * PAIR) for part in range(3)]
            probs, mixed = pair_forward(
                proj_ref[span, cols[0]], proj_ref[span, cols[1]], proj_ref[span, cols[2]], first_half
            )
            probs_ref[seg, pair] = probs
            mixed_ref[span, cols[0]] = mixed.astype(BF16)
    pre_ref[...] = x_ref[...].astype(F32) + dot_nn(mixed_ref[...], square(wqo_ref[3]))


def attention_first_kernel(seg_length, plan, count, ids_ref, x_ref, *refs):
    parts, (proj_ref, probs_ref, mixed_ref, pre_ref, wqo_ref, sems) = refs[:count], refs[count:]

    @pl.when(pl.program_id(0) == 0)
    def fetch():
        for copy in fetch_pieces(ids_ref, plan, parts, wqo_ref, sems):
            copy.wait()

    attention_rows(seg_length, x_ref, wqo_ref, proj_ref, probs_ref, mixed_ref, pre_ref)


def attention_shapes(rows, width, seg_length):
    probs = shape_of((rows // seg_length, width // PAIR, seg_length, 2 * seg_length), BF16)
    return [
        shape_of((rows, 3 * width), BF16), (probs, seg_length), shape_of((rows, width), BF16), shape_of((rows, width), F32),
    ]


def attention_forward(rows_in, weight, seg_length, block, span, prior=(), after=(), pieces=None, ids=None):
    rows, width = rows_in.shape
    outs = attention_shapes(rows, width, seg_length)
    flops = width * (4 * width + 8 * seg_length)
    if pieces is None:
        return rows_call(
            partial(attention_rows, seg_length), "attention_forward", block, span, [rows_in],
            [(weight, whole(weight.shape))], outs, flops, prior, after, weight=SHORT,
        )
    plan, parts, shape = pieces
    return rows_call(
        partial(attention_first_kernel, seg_length, plan, len(parts)), "attention_forward", block, span, [rows_in],
        [(part, ANYWHERE) for part in parts], outs, flops, prior, after, [shape], ids,
        [pltpu.SemaphoreType.DMA((2 * len(plan),))], SHORT,
    )


def ffn_rows(
    seg_length, pre_ref, cot_ref, wup_ref, wdown_ref, gains_ref, shifts_ref,
    low_ref, act_ref, slope_ref, out_ref, branch_ref, grad_ref, sums_ref,
):
    rows, width = pre_ref.shape
    unit, unused = norm_parts(pre_ref[...])
    total = unit * gains_ref[0:1].astype(F32) + shifts_ref[0:1].astype(F32)
    low = total.astype(BF16)
    low_ref[...] = low
    held = dot_nn(low, square(wup_ref[0]))
    for part in range(4):
        cols = slice(part * width, (part + 1) * width)
        ahead = dot_nn(low, square(wup_ref[part + 1])) if part < 3 else None
        act, slope = gelu_parts(held)
        act_ref[:, cols] = act.astype(BF16)
        slope_ref[:, cols] = slope.astype(BF16)
        total = total + dot_nn(act_ref[:, cols], down_block(wdown_ref, part))
        held = ahead
    gain = gains_ref[1:2].astype(F32)
    unit, inverse = norm_parts(total)
    out_ref[...] = (unit * gain + shifts_ref[1:2].astype(F32)).astype(BF16)
    grad = cot_ref[...].astype(F32)
    pre_grad = norm_back(grad, unit, inverse, gain)
    grad_ref[...] = pre_grad
    branch_ref[...] = pre_grad.astype(BF16)

    @pl.when(pl.program_id(0) == 0)
    def start_sums():
        sums_ref[...] = jnp.zeros_like(sums_ref)

    inner = jnp.where(lax.broadcasted_iota(jnp.int32, grad.shape, 0) % seg_length == 0, 0.0, grad)
    sums_ref[1:2] += jnp.sum(inner * unit, axis=0, keepdims=True)
    sums_ref[4:5] += jnp.sum(inner, axis=0, keepdims=True)


def ffn_forward(pre_first, cot, w_up, w_down, gains, shifts, seg_length, block, span, prior=(), after=()):
    rows, width = pre_first.shape
    wide, low = shape_of((rows, 4 * width), BF16), shape_of((rows, width), BF16)
    return rows_call(
        partial(ffn_rows, seg_length), "ffn_forward", block, span, [pre_first, cot],
        [(value, whole(value.shape)) for value in (w_up, w_down, gains, shifts)],
        [low, wide, wide, low, low, shape_of((rows, width), F32)], 8 * width * width, prior, after,
        extra=[shape_of((8, width), F32)],
    )


def edge_rows(pre_ref, wup_ref, wdown_ref, gains_ref, shifts_ref, out_ref, total_ref):
    unit, unused = norm_parts(pre_ref[...])
    total = unit * gains_ref[0:1].astype(F32) + shifts_ref[0:1].astype(F32)
    low = total.astype(BF16)
    for part in range(4):
        act, unused = gelu_parts(dot_nn(low, square(wup_ref[part])))
        total = total + dot_nn(act.astype(BF16), down_block(wdown_ref, part))
    total_ref[...] = total
    unit, unused = norm_parts(total)
    out_ref[...] = unit * gains_ref[1:2].astype(F32) + shifts_ref[1:2].astype(F32)


def edge_first_kernel(ids_ref, pre_ref, gains_ref, shifts_ref, half_ref, other_ref, out_ref, total_ref, wup_ref, wdown_ref, sems):
    parts = (half_ref, other_ref)
    up = fetch_halves(ids_ref, parts, wup_ref, sems)
    down = fetch_halves(ids_ref, parts, wdown_ref, sems, wup_ref.shape[2], True)
    for copy in up + down:
        copy.wait()
    edge_rows(pre_ref, wup_ref, wdown_ref, gains_ref, shifts_ref, out_ref, total_ref)


def edge_forward(pre_edge, weights, gains, shifts, pieces=None, ids=None):
    rows, width = pre_edge.shape
    norms = [(gains, whole(gains.shape)), (shifts, whole(shifts.shape))]
    outs = [shape_of((rows, width), F32)] * 2
    if pieces is None:
        return rows_call(
            edge_rows, "edge_forward", rows, (0, 1), [pre_edge], [(value, whole(value.shape)) for value in weights] + norms,
            outs, 60 * width * width,
        )
    parts, shapes = pieces
    return rows_call(
        edge_first_kernel, "edge_forward", rows, (0, 1), [pre_edge], norms + [(part, ANYWHERE) for part in parts], outs,
        60 * width * width, extra=shapes, ids=ids, scratch=[pltpu.SemaphoreType.DMA((8,))],
    )


def ffn_back_rows(branch_ref, grad2_ref, pre1_ref, slope_ref, wup_ref, wdown_ref, gains_ref, gradh_ref, grad1_ref, low1_ref, sums_ref):
    width = branch_ref.shape[1]
    total = grad2_ref[...]
    for part in range(4):
        cols = slice(part * width, (part + 1) * width)
        grad_act = dot_nt(branch_ref[...], down_block(wdown_ref, part))
        grad_hidden = (grad_act * slope_ref[:, cols].astype(F32)).astype(BF16)
        gradh_ref[:, cols] = grad_hidden
        total = total + dot_nt(grad_hidden, square(wup_ref[part]))
    unit, inverse = norm_parts(pre1_ref[...])
    grad1 = norm_back(total, unit, inverse, gains_ref[0:1].astype(F32))
    grad1_ref[...] = grad1
    low1_ref[...] = grad1.astype(BF16)

    @pl.when(pl.program_id(0) == 0)
    def start_sums():
        sums_ref[...] = jnp.zeros_like(sums_ref)

    sums_ref[0:1] += jnp.sum(total * unit, axis=0, keepdims=True)
    sums_ref[3:4] += jnp.sum(total, axis=0, keepdims=True)


def ffn_backward(branch, grad2, pre_first, slope, w_up, w_down, gains, block, span, weight, prior=(), after=()):
    rows, width = branch.shape
    return rows_call(
        ffn_back_rows, "ffn_backward", block, span, [branch, grad2, pre_first, slope],
        [(w_up, whole(w_up.shape)), (w_down, whole(w_down.shape)), (gains, whole(gains.shape))],
        [shape_of((rows, 4 * width), BF16), shape_of((rows, width), F32), shape_of((rows, width), BF16)],
        8 * width * width, prior, after, [shape_of((8, width), F32)], weight=weight,
    )


def attention_back_rows(seg_length, low1_ref, proj_ref, probs_ref, wqo_ref, gradp_ref, gradm_ref):
    rows, width = low1_ref.shape
    pairs = width // PAIR
    gradm_ref[...] = dot_nt(low1_ref[...], square(wqo_ref[3])).astype(BF16)
    first_half = lane_half((seg_length, PAIR))
    for seg in range(rows // seg_length):
        span = slice(seg * seg_length, (seg + 1) * seg_length)
        for pair in range(pairs):
            cols = [slice(part * width + pair * PAIR, part * width + (pair + 1) * PAIR) for part in range(3)]
            grads = pair_backward(
                proj_ref[span, cols[0]], proj_ref[span, cols[1]], proj_ref[span, cols[2]],
                probs_ref[seg, pair], gradm_ref[span, cols[0]], first_half,
            )
            for place, grad in zip(cols, grads):
                gradp_ref[span, place] = grad.astype(BF16)


def attention_backward(low1, proj, probs, w_qo, seg_length, block, after=()):
    rows, width = low1.shape
    return rows_call(
        partial(attention_back_rows, seg_length), "attention_backward", block, (0, rows // block),
        [low1, proj, (probs, seg_length)], [(w_qo, whole(w_qo.shape))],
        [shape_of((rows, 3 * width), BF16)],
        width * (width + 16 * seg_length), (), after, scratch=[pltpu.VMEM((block, width), BF16)], weight=SHORT,
    )[0]


def input_rows(grad1_ref, gradp_ref, wqo_ref, input_ref):
    width = grad1_ref.shape[1]
    total = grad1_ref[...]
    for part in range(3):
        total = total + dot_nt(gradp_ref[:, part * width : (part + 1) * width], square(wqo_ref[part]))
    input_ref[...] = total


def input_gradient(grad1, gradp, w_qo, block, after):
    rows, width = grad1.shape
    return rows_call(
        input_rows, "input_gradient", block, (0, rows // block), [grad1, gradp], [(w_qo, whole(w_qo.shape))],
        [shape_of((rows, width), F32)], 3 * width * width, (), after, weight=LONG,
    )[0]


def cross_kernel(
    local, fetch, ids_ref, rows_ref, cot_ref, total_ref, keyc_ref, keyr_ref, place_ref, table_ref, gains_ref, shifts_ref, *refs
):
    parts, refs = (refs[:2], refs[2:]) if fetch else (refs[:1], refs[1:])
    new_ref, branch_ref, edge_ref, low_ref, gradp_ref, mixed_ref, gradz_ref, sums_ref, table_grad_ref = refs[:9]
    proj_ref, probs_ref, gradm_ref = refs[9:12]
    wc_ref = parts[0]
    if fetch:
        wc_ref, sems = refs[12:]
        for copy in fetch_halves(ids_ref, parts, wc_ref, sems):
            copy.wait()
    count, width = rows_ref.shape
    pairs = width // PAIR
    entries = table_ref.shape[0]
    picks = place_ref[...] == lax.broadcasted_iota(jnp.int32, (count, entries), 1)
    embedded = rows_ref[...] + dot_nn(picks.astype(BF16), table_ref[...])
    low = embedded.astype(BF16)
    low_ref[...] = low
    for part in range(3):
        proj_ref[:, part * width : (part + 1) * width] = dot_nn(low, square(wc_ref[part])).astype(BF16)
    first_half = lane_half((count, PAIR))
    same = keyc_ref[...] == keyr_ref[...]
    places = [
        [slice(part * width + pair * PAIR, part * width + (pair + 1) * PAIR) for part in range(3)] for pair in range(pairs)
    ]
    for pair, cols in enumerate(places):
        probs, mixed = pair_forward(proj_ref[:, cols[0]], proj_ref[:, cols[1]], proj_ref[:, cols[2]], first_half, same)
        probs_ref[pair] = probs
        mixed_ref[:, cols[0]] = mixed.astype(BF16)
    pre_third = embedded + dot_nn(mixed_ref[...], square(wc_ref[3]))
    unit, inverse = norm_parts(pre_third)
    gain = gains_ref[2:3].astype(F32)
    new_ref[...] = (unit[:local] * gain + shifts_ref[2:3].astype(F32)).astype(BF16)
    grad_out = cot_ref[...]
    grad_third = norm_back(grad_out, unit, inverse, gain)
    sums_ref[...] = jnp.zeros_like(sums_ref)
    sums_ref[2:3] = jnp.sum(grad_out[:local] * unit[:local], axis=0, keepdims=True)
    sums_ref[5:6] = jnp.sum(grad_out[:local], axis=0, keepdims=True)
    gradz = grad_third.astype(BF16)
    gradz_ref[...] = gradz
    gradm_ref[...] = dot_nt(gradz, square(wc_ref[3])).astype(BF16)
    for pair, cols in enumerate(places):
        grads = pair_backward(
            proj_ref[:, cols[0]], proj_ref[:, cols[1]], proj_ref[:, cols[2]], probs_ref[pair], gradm_ref[:, cols[0]], first_half
        )
        for place, grad in zip(cols, grads):
            gradp_ref[:, place] = grad.astype(BF16)
    grad_edge = grad_third[:local]
    for part in range(3):
        grad_edge = grad_edge + dot_nt(gradp_ref[:local, part * width : (part + 1) * width], square(wc_ref[part]))
    unit, inverse = norm_parts(total_ref[...])
    sums_ref[1:2] = jnp.sum(grad_edge * unit, axis=0, keepdims=True)
    sums_ref[4:5] = jnp.sum(grad_edge, axis=0, keepdims=True)
    pre_grad = norm_back(grad_edge, unit, inverse, gains_ref[1:2].astype(F32))
    edge_ref[...] = pre_grad
    branch_ref[...] = pre_grad.astype(BF16)
    table_grad_ref[...] = lax.dot_general(
        picks[:local].astype(F32), grad_edge, (((0,), (0,)), ((), ())),
        precision=lax.Precision.HIGHEST, preferred_element_type=F32,
    )


def cross_block(ids, local, edge_rows, edge_cot, edge_total, key_col, key_row, place, table, gains, shifts, parts, shape):
    count, width = edge_rows.shape
    read = [edge_rows, edge_cot, edge_total, key_col, key_row, place, table, gains, shifts]
    part_specs, fetched = [whole(part.shape) for part in parts], []
    if shape is not None:
        part_specs = [ANYWHERE] * len(parts)
        fetched = [pltpu.VMEM(shape.shape, BF16), pltpu.SemaphoreType.DMA((4,))]
    shapes = (
        jax.ShapeDtypeStruct((local, width), BF16),
        jax.ShapeDtypeStruct((local, width), BF16),
        jax.ShapeDtypeStruct((local, width), F32),
        jax.ShapeDtypeStruct((count, width), BF16),
        jax.ShapeDtypeStruct((count, 3 * width), BF16),
        jax.ShapeDtypeStruct((count, width), BF16),
        jax.ShapeDtypeStruct((count, width), BF16),
        jax.ShapeDtypeStruct((8, width), F32),
        jax.ShapeDtypeStruct(table.shape, F32),
    )
    return pl.pallas_call(
        partial(cross_kernel, local, shape is not None),
        out_shape=shapes,
        grid_spec=pltpu.PrefetchScalarGridSpec(
            num_scalar_prefetch=1,
            grid=(1,),
            in_specs=[whole(value.shape) for value in read] + part_specs,
            out_specs=[whole(value.shape) for value in shapes],
            scratch_shapes=[
                pltpu.VMEM((count, 3 * width), BF16),
                pltpu.VMEM((width // PAIR, count, 2 * count), BF16),
                pltpu.VMEM((count, width), BF16),
            ] + fetched,
        ),
        compiler_params=pltpu.CompilerParams(vmem_limit_bytes=56 * MIB),
        cost_estimate=cost(10_000_000_000, width * width * 8),
        name="cross_block",
    )(ids, *read, *parts)


def cols_grad_kernel(side, ids_ref, left_ref, right_ref, rider_ref, *refs):
    out_ref = refs[-1]
    owners, rows = rider_ref.shape[0], left_ref.shape[1] // rider_ref.shape[0]
    block = half_block(side, pl.program_id(0), ids_ref)
    product = dot_tn(left_ref[...], right_ref[...]).astype(BF16)
    out_ref[0, :, :rows] = product.reshape(owners, rows, product.shape[1])
    rider = rider_ref[...]
    out_ref[0, :, rows:] = jnp.where(block == 0, rider, jnp.zeros_like(rider))


def joint_grad_kernel(side, ids_ref, left_ref, last_left_ref, right_ref, last_right_ref, *refs):
    block = half_block(side, pl.program_id(0), ids_ref)

    @pl.when(block < 3)
    def main():
        refs[-1][0] = dot_tn(left_ref[...], right_ref[...]).astype(BF16)

    @pl.when(block == 3)
    def last():
        refs[-1][0] = dot_tn(last_left_ref[...], last_right_ref[...]).astype(BF16)


def half_block(side, step, ids):
    return 2 * ((ids[1] & 1) ^ side) + step


def half_grads(kernel, name, ids, operands, specs, shape, after, weight):
    rows, width = operands[0].shape
    return pl.pallas_call(
        kernel,
        out_shape=jax.ShapeDtypeStruct((2,) + shape, BF16),
        grid_spec=pltpu.PrefetchScalarGridSpec(
            num_scalar_prefetch=1,
            grid=(2,),
            in_specs=specs + [ANYWHERE] * len(after),
            out_specs=pl.BlockSpec((1,) + shape, lambda j, ids: (j,) + (0,) * len(shape)),
        ),
        compiler_params=pltpu.CompilerParams(vmem_limit_bytes=56 * MIB),
        cost_estimate=cost(4 * rows * width * width, 10 * rows * width, weight),
        name=name,
    )(ids, *operands, *after)


def plain_cols_kernel(ids_ref, left_ref, right_ref, *refs):
    refs[-1][0] = dot_tn(left_ref[...], right_ref[...]).astype(BF16)


def cols_grads(side, ids, left, right, rider, after, weight):
    rows, width = left.shape
    owners, extra, unused = rider.shape
    specs = [
        whole(left.shape),
        pl.BlockSpec((rows, width), lambda j, ids: (0, half_block(side, j, ids))),
    ]
    if width // owners % 16 == 0:
        return half_grads(
            partial(cols_grad_kernel, side), "cols_grads", ids, [left, right, rider], specs + [whole(rider.shape)],
            (owners, width // owners + extra, width), after, weight,
        )
    product = half_grads(plain_cols_kernel, "cols_grads", ids, [left, right], specs, (width, width), after, weight)
    first = half_block(side, 0, ids) == 0
    rider = jnp.where(first, rider, jnp.zeros_like(rider))
    rider = jnp.stack([rider, jnp.zeros_like(rider)], axis=0)
    return jnp.concatenate([product.reshape(2, owners, width // owners, width), rider], axis=2)


def joint_grads(side, ids, left, last_left, right, last_right, after, weight):
    rows, width = left.shape
    specs = [
        whole(left.shape),
        whole(left.shape),
        pl.BlockSpec((rows, width), lambda j, ids: (0, jnp.minimum(half_block(side, j, ids), 2))),
        whole(left.shape),
    ]
    operands = [left, last_left, right, last_right]
    return half_grads(partial(joint_grad_kernel, side), "joint_grads", ids, operands, specs, (width, width), after, weight)


def rows_grad_kernel(ids_ref, left_ref, right_ref, *refs):
    send_ref, keep_ref, held_ref = refs[-3:]
    core = ids_ref[1] & 1
    held_ref[...] = dot_tn(left_ref[...], right_ref[...]).reshape(held_ref.shape)
    for share in range(2):
        send_ref[share] = held_ref[:, 2 * (1 - core) + share].astype(BF16)
        keep_ref[share] = held_ref[:, 2 * core + share].astype(BF16)


def rows_grads(ids, left, right, count, after):
    rows, width = right.shape
    hidden = left.shape[1]
    shard_rows = hidden // count // 4
    owners = count // 4
    half = jax.ShapeDtypeStruct((2, count, shard_rows, width), BF16)
    out_spec = pl.BlockSpec((2, owners, shard_rows, width), lambda j, ids: (0, j, 0, 0))
    return pl.pallas_call(
        rows_grad_kernel,
        out_shape=(half, half),
        grid_spec=pltpu.PrefetchScalarGridSpec(
            num_scalar_prefetch=1,
            grid=(4,),
            in_specs=[
                pl.BlockSpec((rows, hidden // 4), lambda j, ids: (0, j)),
                pl.BlockSpec((rows, width), lambda j, ids: (0, 0), pipeline_mode=pl.Buffered(1)),
            ] + [ANYWHERE] * len(after),
            out_specs=[out_spec, out_spec],
            scratch_shapes=[pltpu.VMEM((owners, 4, shard_rows, width), F32)],
        ),
        compiler_params=pltpu.CompilerParams(vmem_limit_bytes=56 * MIB),
        cost_estimate=cost(2 * rows * width * hidden, 10 * rows * width),
        name="rows_grads",
    )(ids, left, right, *after)


def later(value, *first):
    return lax.optimization_barrier((value,) + first)[0]


def seg_swap(value, mask):
    count = lax.axis_size("seg")
    return lax.ppermute(value, "seg", [(i, i ^ mask) for i in range(count)])


def rep_swap(value, mask):
    count = lax.axis_size("rep")
    return lax.ppermute(value, "rep", [(i, i ^ mask) for i in range(count)])


def both_swap(value, seg_mask, rep_mask):
    reps = lax.axis_size("rep")
    total = lax.axis_size("seg") * reps
    pairs = [(i, ((i // reps) ^ seg_mask) * reps + ((i % reps) ^ rep_mask)) for i in range(total)]
    return lax.ppermute(value, ("seg", "rep"), pairs)


def place_kernel(plan, count, owner_first, ids_ref, *refs):
    for copy in fetch_pieces(ids_ref, plan, refs[:count], refs[count], refs[count + 1], 0, owner_first):
        copy.wait()


def put_in_place(ids, pieces, owner_first=False):
    plan, parts, shape = pieces
    return pl.pallas_call(
        partial(place_kernel, plan, len(parts), owner_first),
        out_shape=shape,
        in_specs=[pl.BlockSpec(memory_space=pltpu.SMEM)] + [ANYWHERE] * len(parts),
        out_specs=pl.BlockSpec(memory_space=pltpu.VMEM),
        scratch_shapes=[pltpu.SemaphoreType.DMA((4 * len(plan),))],
        compiler_params=pltpu.CompilerParams(vmem_limit_bytes=32 * MIB),
        cost_estimate=cost(0, 4 * shape.size),
        name="put_in_place",
    )(ids, *parts)


def own_half(ids, blocks):
    return lax.dynamic_slice_in_dim(blocks, 2 * (ids[1] & 1), 2, 0)


def far_pieces(piece):
    return [piece] + [seg_swap(piece, mask) for mask in range(2, lax.axis_size("seg"), 2)]


def after_all(value, first):
    return later(value, *first) if first else value


def gather_singly(piece, evens, firsts):
    held, crossed = [], []
    for number, even in enumerate(evens):
        before = held[-1:] + [rep_swap(part, 1) for part in held[-4:-2]]
        crossed += before[1:]
        held += [even, seg_swap(after_all(even, before + firsts.get(number, [])), 1)]
    crossed += [rep_swap(part, 1) for part in held[-4:-1]] + [rep_swap(after_all(held[-1], firsts.get(-1, [])), 1)]
    return held, crossed


def pieces_of(held, crossed, shapes):
    count = len(held)
    return [(i, i % count, i // count) for i in range(2 * count)], held + crossed, shapes


class Gather:
    def __init__(self, piece):
        self.piece, self.came = piece, far_pieces(piece)

    def across(self, *first):
        self.evens = jnp.stack(self.came[:1] + [later(value, *first) for value in self.came[1:]], axis=0)
        self.came = seg_swap(self.evens, 1)

    def finish(self, *first):
        return jnp.stack([self.evens, later(self.came, *first)], axis=1).reshape((-1,) + self.piece.shape)


def spread_kernel(ids_ref, keep_ref, came_ref, stay_ref, x_ref, y_ref, xy_ref):
    near, across = ids_ref[0] & 1, ids_ref[1] >> 1

    def total(share, side):
        return (keep_ref[share, 0, side].astype(F32) + came_ref[share, 0, side].astype(F32)).astype(BF16)

    stay_ref[0] = total(across, near)
    x_ref[0] = total(across, 1 - near)
    y_ref[0] = total(1 - across, near)
    xy_ref[0] = total(1 - across, 1 - near)


def spread(ids, keep, came):
    unused, count, rows, width = keep.shape
    far = count // 2
    shape = (2, far, 2, rows, width)
    in_spec = pl.BlockSpec((2, 1, 2, rows, width), lambda j: (0, j, 0, 0, 0))
    out_spec = pl.BlockSpec((1, rows, width), lambda j: (j, 0, 0))
    out = jax.ShapeDtypeStruct((far, rows, width), BF16)
    return pl.pallas_call(
        spread_kernel,
        out_shape=(out,) * 4,
        grid=(far,),
        in_specs=[pl.BlockSpec(memory_space=pltpu.SMEM), in_spec, in_spec],
        out_specs=[out_spec] * 4,
        compiler_params=pltpu.CompilerParams(vmem_limit_bytes=32 * MIB),
        cost_estimate=cost(0, 12 * count * rows * width),
        name="spread",
    )(ids, keep.reshape(shape), came.reshape(shape))


def settle_kernel(ids_ref, *refs):
    far = refs[0].shape[0]
    parts, outs = refs[:-far], refs[-far:]
    start = 0
    for first in range(0, len(parts), 4):
        rows = parts[first].shape[1]
        for mask, out in enumerate(outs):
            a, b, c, d = (part[(ids_ref[0] >> 1) ^ mask].astype(F32) for part in parts[first : first + 4])
            out[start : start + rows] = ((a + b) + (c + d)).astype(BF16)
        start += rows


def settle(ids, *groups):
    far, unused, width = groups[0][0].shape
    heights = [group[0].shape[1] for group in groups]
    if len(groups) > 1 and any(rows % 16 for rows in heights):
        return [jnp.concatenate(parts, axis=0) for parts in zip(*[settle(ids, group) for group in groups])]
    whole_spec = pl.BlockSpec(memory_space=pltpu.VMEM)
    return pl.pallas_call(
        settle_kernel,
        out_shape=(jax.ShapeDtypeStruct((sum(heights), width), BF16),) * far,
        in_specs=[pl.BlockSpec(memory_space=pltpu.SMEM)] + [whole_spec] * (4 * len(groups)),
        out_specs=[whole_spec] * far,
        compiler_params=pltpu.CompilerParams(vmem_limit_bytes=32 * MIB),
        cost_estimate=cost(0, 10 * far * sum(heights) * width),
        name="settle",
    )(ids, *[part for group in groups for part in group])


def halve(value, axis, bit):
    own = lax.dynamic_index_in_dim(value, bit, axis, keepdims=False)
    other = lax.dynamic_index_in_dim(value, 1 - bit, axis, keepdims=False)
    return own, other


class Reduction:
    def __init__(self, ids, send, keep):
        count = lax.axis_size("seg")
        self.ids = ids
        self.shape = (2, count, send.size // (2 * count * send.shape[-1]), send.shape[-1])
        self.keep = keep
        self.came = rep_swap(send, 1)

    def spread(self, *first):
        came = after_all(self.came, first)
        self.stay, *sends = spread(self.ids, self.keep.reshape(self.shape), came.reshape(self.shape))
        self.came = [seg_swap(sends[0], 1), rep_swap(sends[1], 2), both_swap(sends[2], 1, 2)]

    def parts(self, *first):
        return [self.stay] + [after_all(value, first) for value in self.came]


def swap_far(others):
    return [seg_swap(other, 2 * mask) for mask, other in enumerate(others, 1)]


def add_up(own, came, *first):
    total = own.astype(F32)
    for value in came:
        total = total + after_all(value, first).astype(F32)
    return total.astype(BF16)


class Sharing:
    def __init__(self, ids, value):
        self.ids, self.value = ids, value
        self.came = rep_swap(value, 2)

    def step(self, *first):
        self.value = jnp.stack([self.value, later(self.came, *first)], axis=0)
        self.came = rep_swap(self.value, 1)

    def finish(self, *first):
        held = jnp.concatenate([self.value, later(self.came, *first)], axis=0)
        order = jnp.array([0, 2, 1, 3], jnp.int32)
        return [
            lax.dynamic_index_in_dim(held, order[self.ids[1] ^ owner], 0, keepdims=False).astype(F32)
            for owner in (0, 2, 1, 3)
        ]


def body(tokens, cotangent, doc_counts, w_qkv, w_out, w_up, w_down, c_qkv, c_out, pos_table, norm_gains, norm_shifts):
    micro_count, unused, seg_local, seg_length, width = tokens.shape
    count = lax.axis_size("seg")
    me = lax.axis_index("seg").astype(jnp.int32)
    rep = lax.axis_index("rep").astype(jnp.int32)
    ids = jnp.stack([me, rep])
    shard_rows = w_qkv.shape[0]
    local = micro_count * seg_local
    rows = local * seg_length
    table_rows = pos_table.shape[0]
    norm_cols = norm_gains.shape[1]
    aligned = shard_rows % 16 == 0

    def shares_of(matrix):
        return matrix.reshape(shard_rows, 4, width).transpose(1, 0, 2)

    def own_share(matrix):
        return lax.dynamic_slice_in_dim(matrix, rep * width, width, 1)

    norms = jnp.pad(jnp.concatenate([norm_gains, norm_shifts], axis=0), ((0, 2), (0, width - norm_cols)))
    small = jnp.pad(jnp.stack([pos_table, norms], axis=0), ((0, 0), (0, 16 - table_rows), (0, 0)))
    ffn_piece = jnp.concatenate(
        [own_half(ids, shares_of(w_up)), own_half(ids, w_down.reshape(4, shard_rows, width)), small], axis=1
    )
    ffn_half = lax.all_gather(ffn_piece, "seg", axis=0)
    qo_piece = own_half(ids, shares_of(jnp.concatenate([w_qkv, w_out], axis=1)))
    qo_evens = far_pieces(qo_piece)
    shapes = [shape_of((4, count, shard_rows, width), BF16), shape_of((count, 4, shard_rows, width), BF16)]
    qo_pieces = pieces_of(*gather_singly(qo_piece, qo_evens, {}), shapes[0])
    cross_piece = own_half(ids, shares_of(jnp.concatenate([c_qkv, c_out], axis=1)))
    cross_half = lax.all_gather(later(cross_piece, qo_evens[1]), "seg", axis=0)

    counts = doc_counts[:, 0]
    ends = jnp.cumsum(counts, axis=1)
    owners = me ^ jnp.arange(count, dtype=jnp.int32)
    seg_ids = owners[:, None, None] * seg_local + jnp.arange(seg_local, dtype=jnp.int32)[None, None, :]
    seg_ids = jnp.broadcast_to(seg_ids, (count, micro_count, seg_local))
    past = seg_ids[..., None] >= ends[None, :, None, :]
    doc_ids = jnp.sum(past.astype(jnp.int32), axis=-1)
    starts = jnp.sum(jnp.where(past, counts[None, :, None, :], 0), axis=-1)
    places = (seg_ids - starts).reshape(-1, 1)
    keys = (doc_ids + (counts.shape[1] + 1) * jnp.arange(micro_count, dtype=jnp.int32)[None, :, None]).reshape(-1)

    flat = tokens.reshape(rows, width)
    cot = cotangent.reshape(rows, width)
    block = 4 * seg_length
    steps = rows // block
    halves_of = ((0, steps // 2), (steps // 2, steps - steps // 2))

    everything = (0, steps)
    if aligned:
        proj, probs, mixed, pre_first, full_qo = attention_forward(
            flat, None, seg_length, block, everything, after=[keys, places], pieces=qo_pieces, ids=ids
        )
    else:
        full_qo = put_in_place(ids, qo_pieces).reshape(4, 1, width, width)
        proj, probs, mixed, pre_first = attention_forward(flat, full_qo, seg_length, block, everything)
    ffn_half = later(ffn_half, proj)
    small = ffn_half[:, :, 2 * shard_rows :]
    table = small[:, 0, :table_rows].reshape(count * table_rows, width)
    norms = small[:, 1, :6, :norm_cols].transpose(1, 0, 2).reshape(6, width)
    gains, shifts = norms[:3], norms[3:]
    ffn_other = rep_swap(ffn_half, 1)

    def joined(parts, start, owner_first):
        own, other = [part[:, :, start : start + shard_rows] for part in parts]
        both = jnp.where((rep & 1) == 0, jnp.concatenate([own, other], axis=1), jnp.concatenate([other, own], axis=1))
        return (both if owner_first else both.transpose(1, 0, 2, 3)).reshape(4, 1, width, width)

    pre_edge = pre_first.reshape(local, seg_length, width)[:, 0]
    if aligned:
        edge, edge_total, full_up, full_down = edge_forward(
            pre_edge, None, gains, shifts, ([ffn_half, ffn_other], shapes), ids
        )
    else:
        full_up = joined([ffn_half, ffn_other], 0, False)
        full_down = joined([ffn_half, ffn_other], shard_rows, True)
        edge, edge_total = edge_forward(pre_edge, [full_up, full_down], gains, shifts)
    edge_cot = cot.reshape(local, seg_length, width)[:, 0].astype(F32)
    edges = Gather(jnp.stack([edge, edge_cot], axis=0))
    small_block, small_steps = block // 2, steps
    *kept, sums2a = ffn_forward(
        pre_first, cot, full_up, full_down, gains, shifts, seg_length, small_block, (0, small_steps), after=[edge]
    )
    edges.across(kept[0])
    low, act, slope, out, branch, grad2, sums2b = ffn_forward(
        pre_first, cot, full_up, full_down, gains, shifts, seg_length, small_block, (small_steps, small_steps), prior=kept,
        after=[edges.evens],
    )
    edges = edges.finish(low)
    cross_half = later(cross_half, low)
    cross_parts, cross_shape = [cross_half, rep_swap(cross_half, 1)], shapes[0]
    if not aligned:
        cross_parts, cross_shape = [joined(cross_parts, 0, False)], None
    cls_new, cls_branch, cls_grad, c_low, c_gradp, c_mixed, c_gradz, c_sums, table_grad = cross_block(
        ids, local, edges[:, 0].reshape(-1, width), edges[:, 1].reshape(-1, width), edge_total,
        keys[:, None], jnp.concatenate([keys, keys])[None, :], places, table, gains, shifts, cross_parts, cross_shape,
    )

    def with_edge(values, edge):
        whole_rows = values.reshape(local, seg_length, width)
        return lax.dynamic_update_slice(whole_rows, edge[:, None], (0, 0, 0)).reshape(rows, width)

    branch, grad2 = with_edge(branch, cls_branch), with_edge(grad2, cls_grad)
    send_down, keep_down = rows_grads(ids, act, branch, count, [])
    down = Reduction(ids, send_down, keep_down)
    *kept, sums1a = ffn_backward(
        branch, grad2, pre_first, slope, full_up, full_down, gains, block, halves_of[0], LONG, after=[send_down]
    )
    down.spread(kept[0])
    grad_hidden, grad1, low1, sums1b = ffn_backward(
        branch, grad2, pre_first, slope, full_up, full_down, gains, block, halves_of[1], SHORT, prior=kept, after=[down.stay]
    )
    norm_sums = (sums2a + sums2b + sums1a + sums1b + c_sums).reshape(8, count, norm_cols).transpose(1, 0, 2)
    norm_sums = jnp.pad(norm_sums, ((0, 0), (0, 0), (0, width - norm_cols)))
    rider = jnp.concatenate([norm_sums, table_grad.reshape(count, table_rows, width)], axis=1).astype(BF16)
    send_up = cols_grads(1, ids, low, grad_hidden, rider, [], SHORT)
    own_down, *others = settle(ids, down.parts(send_up))
    came_down = swap_far(others)
    keep_up = cols_grads(0, ids, low, grad_hidden, rider, [send_up, own_down], LONG)
    up = Reduction(ids, send_up, keep_up)
    up.spread(keep_up, *came_down[:1])
    grad_proj = attention_backward(low1, proj, probs, full_qo, seg_length, block, after=[up.stay])
    down_share = add_up(own_down, came_down, grad_proj)
    send_qo = joint_grads(1, ids, flat, mixed, grad_proj, low1, [], SHORT)
    own_up, *others = settle(ids, up.parts(send_qo))
    came_up = swap_far(others)
    keep_qo = joint_grads(0, ids, flat, mixed, grad_proj, low1, [send_qo, own_up], LONG)
    qo = Reduction(ids, send_qo, keep_qo)
    qo.spread(keep_qo, *came_up[:2])
    input_grad = input_gradient(grad1, grad_proj, full_qo, block, [qo.stay])
    own, *others = settle(ids, qo.parts(input_grad))
    came = swap_far(others)
    early = Sharing(ids, jnp.concatenate([down_share, add_up(own_up, came_up, own)], axis=0))
    own_low = lax.dynamic_slice_in_dim(later(c_low, own), me * shard_rows, shard_rows, 1)
    own_mixed = lax.dynamic_slice_in_dim(later(c_mixed, own), me * shard_rows, shard_rows, 1)
    grad_c = shares_of(jnp.concatenate([dot_tn(own_low, c_gradp), dot_tn(own_mixed, c_gradz)], axis=1)).astype(BF16)
    c_own, c_other = halve(grad_c.reshape(2, 2, shard_rows, width), 0, rep & 1)
    c_own, c_other = halve(c_own.astype(F32) + rep_swap(c_other, 1).astype(F32), 0, rep >> 1)
    c_came = rep_swap(c_other.astype(BF16), 2)
    late = Sharing(ids, add_up(own, came))
    early.step(late.value)
    crossing = Sharing(ids, (c_own + later(c_came, late.value).astype(F32)).astype(BF16))
    layer_out = with_edge(later(out, crossing.value), cls_new)
    late.step(layer_out)
    crossing.step(late.value)
    early_shares = early.finish(late.value)
    starts = (0, shard_rows, 2 * shard_rows, 2 * shard_rows + 16)
    down_parts, up_parts, riders = [[part[first:last] for part in early_shares] for first, last in zip(starts, starts[1:])]
    grad_up, grad_down, summed = jnp.concatenate(up_parts, axis=1), jnp.concatenate(down_parts, axis=0), riders[0]
    qo_parts, c_parts = late.finish(), crossing.finish()

    return (
        layer_out.reshape(tokens.shape),
        input_grad.reshape(tokens.shape),
        jnp.concatenate(qo_parts[:3], axis=1),
        qo_parts[3],
        grad_up,
        grad_down,
        jnp.concatenate(c_parts[:3], axis=1),
        c_parts[3],
        summed[8 : 8 + table_rows],
        summed[:3, :norm_cols],
        summed[3:6, :norm_cols],
    )


def solution(mesh):
    rows = P(None, "rep", "seg", None, None)
    split = P("seg", None)
    last = P(None, "seg")
    return jax.shard_map(
        body,
        mesh=mesh,
        in_specs=(rows, rows, P(None, "rep", None)) + (split,) * 7 + (last, last),
        out_specs=(rows, rows) + (split,) * 7 + (last, last),
        check_vma=False,
    )
```

```python
from functools import partial
import jax
import jax.numpy as jnp
from jax import lax
from jax.experimental import pallas as pl
from jax.experimental.pallas import tpu as pltpu
from jax.sharding import PartitionSpec as P

HEAD_DIM = 64
PAIR = 2 * HEAD_DIM
EPSILON = 1e-05
NEGATIVE = -1e30
F32 = jnp.float32
BF16 = jnp.bfloat16
MIB = 1 << 20
LONG, SHORT = 6.0, 0.001
CLS_ACT, CLS_SLOPE, CLS_LOW, CLS_PRE, CLS_TOTAL, CLS_OUT, CLS_COT, CLS_BLOCKS = 0, 4, 8, 9, 10, 11, 12, 13


def dot_nn(left, right):
    return lax.dot_general(left, right, (((1,), (0,)), ((), ())), preferred_element_type=F32)


def dot_nt(left, right):
    return lax.dot_general(left, right, (((1,), (1,)), ((), ())), preferred_element_type=F32)


def dot_tn(left, right):
    return lax.dot_general(left, right, (((0,), (0,)), ((), ())), preferred_element_type=F32)


def norm_parts(values):
    center = values - jnp.mean(values, axis=-1, keepdims=True)
    spread = jnp.mean(center * center, axis=-1, keepdims=True)
    inverse = lax.rsqrt(spread + EPSILON)
    return center * inverse, inverse


def norm_back(grad, unit, inverse, gain):
    scaled = grad * gain
    first = jnp.mean(scaled, axis=-1, keepdims=True)
    second = jnp.mean(scaled * unit, axis=-1, keepdims=True)
    return inverse * (scaled - first - unit * second)


def gelu_parts(hidden):
    phi = 0.5 + 0.5 * lax.erf(hidden * 0.5 ** 0.5)
    bell = jnp.exp(hidden * hidden * -0.5) * 0.3989422804014327
    return hidden * phi, phi + hidden * bell


def halves(pair, first_half):
    zero = jnp.zeros_like(pair)
    return jnp.concatenate([jnp.where(first_half, pair, zero), jnp.where(first_half, zero, pair)], axis=0)


def pair_forward(query, key, value, first_half, same=None):
    rows = query.shape[0]
    scores = dot_nt(key, halves(query * BF16(HEAD_DIM ** -0.5), first_half))
    if same is not None:
        scores = jnp.where(same, scores, NEGATIVE)
    raised = jnp.exp(scores - jnp.max(scores, axis=0, keepdims=True))
    probs = (raised * (1.0 / jnp.sum(raised, axis=0, keepdims=True))).astype(BF16)
    both = dot_tn(probs, value)
    return probs, jnp.where(first_half, both[:rows], both[rows:])


def pair_backward(query, key, value, probs, grad_mixed, first_half):
    rows = query.shape[0]
    grad_both = halves(grad_mixed, first_half)
    query_both = halves(query * BF16(HEAD_DIM ** -0.5), first_half)
    grad_probs = dot_nt(value, grad_both)
    wide = probs.astype(F32)
    grad_scores = (wide * (grad_probs - jnp.sum(grad_probs * wide, axis=0, keepdims=True))).astype(BF16)
    grad_value = dot_nn(probs, grad_both)
    grad_key = dot_nn(grad_scores, query_both)
    both = dot_tn(grad_scores, key)
    grad_query = jnp.where(first_half, both[:rows], both[rows:]) * (HEAD_DIM ** -0.5)
    return grad_query, grad_key, grad_value


def lane_half(shape):
    return lax.broadcasted_iota(jnp.int32, shape, 1) % PAIR < HEAD_DIM


def square(value):
    return value.reshape(-1, value.shape[-1])


def up_block(ref, part):
    return square(ref[:, part])


def down_block(ref, part):
    count = ref.shape[0] // 4
    return square(ref[part * count : (part + 1) * count])


def whole(shape):
    return pl.BlockSpec(shape, lambda *at: (0,) * len(shape), pipeline_mode=pl.Buffered(1))


ANYWHERE = pl.BlockSpec(memory_space=pl.ANY)


def cost(flops, moved, weight=1.0):
    return pl.CostEstimate(flops=int(flops * weight), bytes_accessed=int(moved * weight), transcendentals=0)


def rows_call(kernel, name, block, span, rowed, fixed, outs, flops, prior=(), after=(), extra=(), ids=None, scratch=(), weight=1.0):
    first, steps = span

    def cut(value):
        array, ratio = value if isinstance(value, tuple) else (value, 1)
        shape = (block // ratio,) + array.shape[1:]
        return array, pl.BlockSpec(shape, lambda i, *ids: (i + first,) + (0,) * (len(shape) - 1))

    ins = [cut(value) for value in rowed] + list(fixed)
    results = [cut(value) for value in outs] + [(shape, whole(shape.shape)) for shape in extra]
    unread = list(prior) + list(after)
    lead = 0 if ids is None else 1
    moved = sum(value.size * value.dtype.itemsize for value, unused in ins + results) // 2

    def run(*refs):
        start = lead + len(ins)
        kernel(*refs[:start], *refs[start + len(unread) :])

    return pl.pallas_call(
        run,
        out_shape=tuple(jax.ShapeDtypeStruct(shape.shape, shape.dtype) for shape, unused in results),
        grid_spec=pltpu.PrefetchScalarGridSpec(
            num_scalar_prefetch=lead,
            grid=(steps,),
            in_specs=[spec for unused, spec in ins] + [ANYWHERE] * len(unread),
            out_specs=[spec for unused, spec in results],
            scratch_shapes=list(scratch),
        ),
        input_output_aliases={lead + len(ins) + i: i for i in range(len(prior))},
        compiler_params=pltpu.CompilerParams(vmem_limit_bytes=58 * MIB),
        cost_estimate=cost(2 * flops * steps * block, moved, weight),
        name=name,
    )(*([] if ids is None else [ids]), *[array for array, unused in ins], *unread)


def shape_of(shape, dtype):
    return jax.ShapeDtypeStruct(shape, dtype)


def fetch_pieces(ids_ref, plan, parts, out_ref, sems, start=0, owner_first=False):
    me, core = ids_ref[0], ids_ref[1] & 1
    rows = out_ref.shape[2]
    base = 2 * len(plan) if owner_first else 0
    copies = []
    for number, (which, mask, side) in enumerate(plan):
        part = parts[which]
        owner_core = core if side == 0 else 1 - core
        for share in range(2):
            piece = part.at[share] if part.shape[-2] == rows else part.at[share, pl.ds(start, rows)]
            place = (2 * owner_core + share, me ^ mask)
            target = out_ref.at[place[::-1] if owner_first else place]
            copies.append(pltpu.make_async_copy(piece, target, sems.at[base + 2 * number + share]))
    for copy in copies:
        copy.start()
    return copies


def fetch_halves(ids_ref, parts, out_ref, sems, start=0, owner_first=False):
    core = ids_ref[1] & 1
    rows = out_ref.shape[2]
    base = 4 if owner_first else 0
    copies = []
    for side, part in enumerate(parts):
        owner_core = core if side == 0 else 1 - core
        for share in range(2):
            piece = part.at[:, share] if part.shape[-2] == rows else part.at[:, share, pl.ds(start, rows)]
            block = 2 * owner_core + share
            target = out_ref.at[:, block] if owner_first else out_ref.at[block]
            copies.append(pltpu.make_async_copy(piece, target, sems.at[base + 2 * side + share]))
    for copy in copies:
        copy.start()
    return copies


def attention_rows(seg_length, x_ref, wqo_ref, proj_ref, probs_ref, mixed_ref, pre_ref):
    rows, width = x_ref.shape
    pairs = width // PAIR
    for part in range(3):
        proj_ref[:, part * width : (part + 1) * width] = dot_nn(x_ref[...], square(wqo_ref[part])).astype(BF16)
    first_half = lane_half((seg_length, PAIR))
    for seg in range(rows // seg_length):
        span = slice(seg * seg_length, (seg + 1) * seg_length)
        for pair in range(pairs):
            cols = [slice(part * width + pair * PAIR, part * width + (pair + 1) * PAIR) for part in range(3)]
            probs, mixed = pair_forward(
                proj_ref[span, cols[0]], proj_ref[span, cols[1]], proj_ref[span, cols[2]], first_half
            )
            probs_ref[seg, pair] = probs
            mixed_ref[span, cols[0]] = mixed.astype(BF16)
    pre_ref[...] = x_ref[...].astype(F32) + dot_nn(mixed_ref[...], square(wqo_ref[3]))


def attention_first_kernel(seg_length, plan, count, ids_ref, x_ref, *refs):
    parts, (proj_ref, probs_ref, mixed_ref, pre_ref, wqo_ref, sems) = refs[:count], refs[count:]

    @pl.when(pl.program_id(0) == 0)
    def fetch():
        for copy in fetch_pieces(ids_ref, plan, parts, wqo_ref, sems):
            copy.wait()

    attention_rows(seg_length, x_ref, wqo_ref, proj_ref, probs_ref, mixed_ref, pre_ref)


def attention_shapes(rows, width, seg_length):
    probs = shape_of((rows // seg_length, width // PAIR, seg_length, 2 * seg_length), BF16)
    return [
        shape_of((rows, 3 * width), BF16), (probs, seg_length), shape_of((rows, width), BF16), shape_of((rows, width), F32),
    ]


def attention_forward(rows_in, weight, seg_length, block, span, prior=(), after=(), pieces=None, ids=None):
    rows, width = rows_in.shape
    outs = attention_shapes(rows, width, seg_length)
    flops = width * (4 * width + 8 * seg_length)
    if pieces is None:
        return rows_call(
            partial(attention_rows, seg_length), "attention_forward", block, span, [rows_in],
            [(weight, whole(weight.shape))], outs, flops, prior, after, weight=SHORT,
        )
    plan, parts, shape = pieces
    return rows_call(
        partial(attention_first_kernel, seg_length, plan, len(parts)), "attention_forward", block, span, [rows_in],
        [(part, ANYWHERE) for part in parts], outs, flops, prior, after, [shape], ids,
        [pltpu.SemaphoreType.DMA((2 * len(plan),))], SHORT,
    )


def ffn_rows(
    seg_length, pre_ref, cot_ref, wup_ref, wdown_ref, gains_ref, shifts_ref,
    low_ref, act_ref, slope_ref, out_ref, branch_ref, grad_ref, sums_ref, cls_ref,
):
    rows, width = pre_ref.shape
    segs = rows // seg_length

    def keep_cls(block, values):
        for seg in range(segs):
            row = values[seg * seg_length : seg * seg_length + 1].astype(F32)
            cls_ref[pl.ds(pl.program_id(0) * segs + seg, 1), block * width : (block + 1) * width] = row

    unit, unused = norm_parts(pre_ref[...])
    total = unit * gains_ref[0:1].astype(F32) + shifts_ref[0:1].astype(F32)
    low = total.astype(BF16)
    low_ref[...] = low
    held = dot_nn(low, square(wup_ref[0]))
    for part in range(4):
        cols = slice(part * width, (part + 1) * width)
        ahead = dot_nn(low, square(wup_ref[part + 1])) if part < 3 else None
        act, slope = gelu_parts(held)
        act, slope = act.astype(BF16), slope.astype(BF16)
        act_ref[:, cols] = act
        slope_ref[:, cols] = slope
        keep_cls(CLS_ACT + part, act)
        keep_cls(CLS_SLOPE + part, slope)
        total = total + dot_nn(act_ref[:, cols], down_block(wdown_ref, part))
        held = ahead
    gain = gains_ref[1:2].astype(F32)
    unit, inverse = norm_parts(total)
    out = unit * gain + shifts_ref[1:2].astype(F32)
    out_ref[...] = out.astype(BF16)
    keep_cls(CLS_LOW, low)
    keep_cls(CLS_PRE, pre_ref)
    keep_cls(CLS_TOTAL, total)
    keep_cls(CLS_OUT, out)
    keep_cls(CLS_COT, cot_ref)
    is_cls = lax.broadcasted_iota(jnp.int32, total.shape, 0) % seg_length == 0
    grad = jnp.where(is_cls, 0.0, cot_ref[...].astype(F32))
    pre_grad = norm_back(grad, unit, inverse, gain)
    grad_ref[...] = pre_grad
    branch_ref[...] = pre_grad.astype(BF16)

    @pl.when(pl.program_id(0) == 0)
    def start_sums():
        sums_ref[...] = jnp.zeros_like(sums_ref)

    sums_ref[1:2] += jnp.sum(grad * unit, axis=0, keepdims=True)
    sums_ref[4:5] += jnp.sum(grad, axis=0, keepdims=True)


def ffn_first_kernel(seg_length, ids_ref, pre_ref, cot_ref, gains_ref, shifts_ref, half_ref, other_ref, *refs):
    *outs, wup_ref, wdown_ref, sems = refs

    @pl.when(pl.program_id(0) == 0)
    def fetch():
        parts = (half_ref, other_ref)
        up = fetch_halves(ids_ref, parts, wup_ref, sems)
        down = fetch_halves(ids_ref, parts, wdown_ref, sems, wup_ref.shape[2], True)
        for copy in up + down:
            copy.wait()

    ffn_rows(seg_length, pre_ref, cot_ref, wup_ref, wdown_ref, gains_ref, shifts_ref, *outs)


def ffn_forward(pre_first, cot, weights, gains, shifts, seg_length, block, pieces=None, ids=None):
    rows, width = pre_first.shape
    span = (0, rows // block)
    wide, low = shape_of((rows, 4 * width), BF16), shape_of((rows, width), BF16)
    outs = [low, wide, wide, low, low, shape_of((rows, width), F32)]
    extra = [shape_of((8, width), F32), shape_of((rows // seg_length, CLS_BLOCKS * width), F32)]
    if pieces is None:
        return rows_call(
            partial(ffn_rows, seg_length), "ffn_forward", block, span, [pre_first, cot],
            [(value, whole(value.shape)) for value in (*weights, gains, shifts)], outs, 8 * width * width, extra=extra,
        )
    parts, shapes = pieces
    return rows_call(
        partial(ffn_first_kernel, seg_length), "ffn_forward", block, span, [pre_first, cot],
        [(gains, whole(gains.shape)), (shifts, whole(shifts.shape))] + [(part, ANYWHERE) for part in parts], outs,
        8 * width * width, extra=extra + shapes, ids=ids, scratch=[pltpu.SemaphoreType.DMA((8,))],
    )


def ffn_back_rows(branch_ref, grad2_ref, pre1_ref, slope_ref, wup_ref, wdown_ref, gains_ref, gradh_ref, grad1_ref, low1_ref, sums_ref):
    width = branch_ref.shape[1]
    total = grad2_ref[...]
    for part in range(4):
        cols = slice(part * width, (part + 1) * width)
        grad_act = dot_nt(branch_ref[...], down_block(wdown_ref, part))
        grad_hidden = (grad_act * slope_ref[:, cols].astype(F32)).astype(BF16)
        gradh_ref[:, cols] = grad_hidden
        total = total + dot_nt(grad_hidden, square(wup_ref[part]))
    unit, inverse = norm_parts(pre1_ref[...])
    grad1 = norm_back(total, unit, inverse, gains_ref[0:1].astype(F32))
    grad1_ref[...] = grad1
    low1_ref[...] = grad1.astype(BF16)

    @pl.when(pl.program_id(0) == 0)
    def start_sums():
        sums_ref[...] = jnp.zeros_like(sums_ref)

    sums_ref[0:1] += jnp.sum(total * unit, axis=0, keepdims=True)
    sums_ref[3:4] += jnp.sum(total, axis=0, keepdims=True)


def ffn_backward(branch, grad2, pre_first, slope, w_up, w_down, gains, block, span, weight, prior=(), after=()):
    rows, width = branch.shape
    return rows_call(
        ffn_back_rows, "ffn_backward", block, span, [branch, grad2, pre_first, slope],
        [(w_up, whole(w_up.shape)), (w_down, whole(w_down.shape)), (gains, whole(gains.shape))],
        [shape_of((rows, 4 * width), BF16), shape_of((rows, width), F32), shape_of((rows, width), BF16)],
        8 * width * width, prior, after, [shape_of((8, width), F32)], weight=weight,
    )


def attention_back_rows(seg_length, low1_ref, proj_ref, probs_ref, wqo_ref, gradp_ref, gradm_ref):
    rows, width = low1_ref.shape
    pairs = width // PAIR
    gradm_ref[...] = dot_nt(low1_ref[...], square(wqo_ref[3])).astype(BF16)
    first_half = lane_half((seg_length, PAIR))
    for seg in range(rows // seg_length):
        span = slice(seg * seg_length, (seg + 1) * seg_length)
        for pair in range(pairs):
            cols = [slice(part * width + pair * PAIR, part * width + (pair + 1) * PAIR) for part in range(3)]
            grads = pair_backward(
                proj_ref[span, cols[0]], proj_ref[span, cols[1]], proj_ref[span, cols[2]],
                probs_ref[seg, pair], gradm_ref[span, cols[0]], first_half,
            )
            for place, grad in zip(cols, grads):
                gradp_ref[span, place] = grad.astype(BF16)


def attention_backward(low1, proj, probs, w_qo, seg_length, block, after=()):
    rows, width = low1.shape
    return rows_call(
        partial(attention_back_rows, seg_length), "attention_backward", block, (0, rows // block),
        [low1, proj, (probs, seg_length)], [(w_qo, whole(w_qo.shape))],
        [shape_of((rows, 3 * width), BF16)],
        width * (width + 16 * seg_length), (), after, scratch=[pltpu.VMEM((block, width), BF16)], weight=SHORT,
    )[0]


def input_rows(grad1_ref, gradp_ref, wqo_ref, input_ref):
    width = grad1_ref.shape[1]
    total = grad1_ref[...]
    for part in range(3):
        total = total + dot_nt(gradp_ref[:, part * width : (part + 1) * width], square(wqo_ref[part]))
    input_ref[...] = total


def input_gradient(grad1, gradp, w_qo, block, after):
    rows, width = grad1.shape
    return rows_call(
        input_rows, "input_gradient", block, (0, rows // block), [grad1, gradp], [(w_qo, whole(w_qo.shape))],
        [shape_of((rows, width), F32)], 3 * width * width, (), after, weight=LONG,
    )[0]


def cross_kernel(
    local, fetch, ids_ref, rows_ref, cls_ref, keyc_ref, keyr_ref, place_ref, table_ref, gains_ref, shifts_ref,
    wup_hbm, wdown_hbm, *refs
):
    parts, refs = (refs[:2], refs[2:]) if fetch else (refs[:1], refs[1:])
    new_ref, branch_ref, grad_c_ref, sums_ref, table_grad_ref, hidden_ref, grad1_ref, low1_ref, turned_ref = refs[:9]
    proj_ref, probs_ref, gradm_ref, mixed_ref, gradp_ref, lying_ref, wup_ref, wdown_ref, ffn_sems = refs[9:18]
    ffn_copies = [
        pltpu.make_async_copy(wdown_hbm, wdown_ref, ffn_sems.at[0]), pltpu.make_async_copy(wup_hbm, wup_ref, ffn_sems.at[1]),
    ]
    wc_ref = parts[0]
    if fetch:
        wc_ref, sems = refs[18:]
        copies = fetch_halves(ids_ref, parts, wc_ref, sems)
    for copy in ffn_copies:
        copy.start()
    if fetch:
        for copy in copies:
            copy.wait()
    count, width = rows_ref.shape[0], rows_ref.shape[1] // 2

    def cls(block):
        return cls_ref[:, block * width : (block + 1) * width]

    pairs = width // PAIR
    entries = table_ref.shape[0]
    picks = place_ref[...] == lax.broadcasted_iota(jnp.int32, (count, entries), 1)
    embedded = rows_ref[:, :width] + dot_nn(picks.astype(BF16), table_ref[...])
    low = embedded.astype(BF16)
    for part in range(3):
        proj_ref[:, part * width : (part + 1) * width] = dot_nn(low, square(wc_ref[part])).astype(BF16)
    first_half = lane_half((count, PAIR))
    same = keyc_ref[...] == keyr_ref[...]
    places = [
        [slice(part * width + pair * PAIR, part * width + (pair + 1) * PAIR) for part in range(3)] for pair in range(pairs)
    ]
    for pair, cols in enumerate(places):
        probs, mixed = pair_forward(proj_ref[:, cols[0]], proj_ref[:, cols[1]], proj_ref[:, cols[2]], first_half, same)
        probs_ref[pair] = probs
        mixed_ref[:, cols[0]] = mixed.astype(BF16)
    pre_third = embedded + dot_nn(mixed_ref[...], square(wc_ref[3]))
    unit, inverse = norm_parts(pre_third)
    gain = gains_ref[2:3].astype(F32)
    new_ref[...] = (unit[:local] * gain + shifts_ref[2:3].astype(F32)).astype(BF16)
    grad_out = rows_ref[:, width:]
    grad_third = norm_back(grad_out, unit, inverse, gain)
    sums_ref[...] = jnp.zeros_like(sums_ref)
    sums_ref[2:3] = jnp.sum(grad_out[:local] * unit[:local], axis=0, keepdims=True)
    sums_ref[5:6] = jnp.sum(grad_out[:local], axis=0, keepdims=True)
    gradz = grad_third.astype(BF16)
    gradm_ref[...] = dot_nt(gradz, square(wc_ref[3])).astype(BF16)
    for pair, cols in enumerate(places):
        grads = pair_backward(
            proj_ref[:, cols[0]], proj_ref[:, cols[1]], proj_ref[:, cols[2]], probs_ref[pair], gradm_ref[:, cols[0]], first_half
        )
        for place, grad in zip(cols, grads):
            gradp_ref[:, place] = grad.astype(BF16)
    grad_edge = grad_third[:local]
    for part in range(3):
        grad_edge = grad_edge + dot_nt(gradp_ref[:local, part * width : (part + 1) * width], square(wc_ref[part]))
    rows = grad_c_ref.shape[1]
    own = pl.ds(pl.multiple_of(ids_ref[0] * rows, 8), rows)
    lying_ref[...] = low.astype(F32).T
    own_low = lying_ref[own, :].astype(BF16)
    for part in range(3):
        grad_c_ref[part] = dot_nn(own_low, gradp_ref[:, part * width : (part + 1) * width]).astype(BF16)
    lying_ref[...] = mixed_ref[...].astype(F32).T
    grad_c_ref[3] = dot_nn(lying_ref[own, :].astype(BF16), gradz).astype(BF16)
    unit, inverse = norm_parts(cls(CLS_TOTAL))
    sums_ref[1:2] = jnp.sum(grad_edge * unit, axis=0, keepdims=True)
    sums_ref[4:5] = jnp.sum(grad_edge, axis=0, keepdims=True)
    total = norm_back(grad_edge, unit, inverse, gains_ref[1:2].astype(F32))
    branch = total.astype(BF16)
    branch_ref[...] = branch
    for part in range(4):
        turned_ref[part * width : (part + 1) * width] = cls(CLS_ACT + part).T.astype(BF16)
    for copy in ffn_copies:
        copy.wait()
    for part in range(4):
        grad_act = dot_nt(branch, down_block(wdown_ref, part))
        grad_hidden = (grad_act * cls(CLS_SLOPE + part)).astype(BF16)
        hidden_ref[:, part * width : (part + 1) * width] = grad_hidden
        total = total + dot_nt(grad_hidden, square(wup_ref[part]))
    unit, inverse = norm_parts(cls(CLS_PRE))
    grad1 = norm_back(total, unit, inverse, gains_ref[0:1].astype(F32))
    grad1_ref[...] = grad1
    low1_ref[...] = grad1.astype(BF16)
    sums_ref[0:1] = jnp.sum(total * unit, axis=0, keepdims=True)
    sums_ref[3:4] = jnp.sum(total, axis=0, keepdims=True)
    table_grad_ref[...] = lax.dot_general(
        picks[:local].astype(F32), grad_edge, (((0,), (0,)), ((), ())),
        precision=lax.Precision.HIGHEST, preferred_element_type=F32,
    )


def cross_block(ids, edges, cls, key_col, key_row, place, table, gains, shifts, w_up, w_down, parts, shape):
    local, count, width = cls.shape[0], edges.shape[0], table.shape[1]
    read = [edges, cls, key_col, key_row, place, table, gains, shifts]
    part_specs, fetched = [whole(part.shape) for part in parts], []
    if shape is not None:
        part_specs = [ANYWHERE] * len(parts)
        fetched = [pltpu.VMEM(shape.shape, BF16), pltpu.SemaphoreType.DMA((4,))]
    shapes = (
        jax.ShapeDtypeStruct((local, width), BF16),
        jax.ShapeDtypeStruct((local, width), BF16),
        jax.ShapeDtypeStruct((4, width // lax.axis_size("seg"), width), BF16),
        jax.ShapeDtypeStruct((8, width), F32),
        jax.ShapeDtypeStruct(table.shape, F32),
        jax.ShapeDtypeStruct((local, 4 * width), BF16),
        jax.ShapeDtypeStruct((local, width), F32),
        jax.ShapeDtypeStruct((local, width), BF16),
        jax.ShapeDtypeStruct((4 * width, local), BF16),
    )
    return pl.pallas_call(
        partial(cross_kernel, local, shape is not None),
        out_shape=shapes,
        grid_spec=pltpu.PrefetchScalarGridSpec(
            num_scalar_prefetch=1,
            grid=(1,),
            in_specs=[whole(value.shape) for value in read] + [ANYWHERE] * 2 + part_specs,
            out_specs=[whole(value.shape) for value in shapes],
            scratch_shapes=[
                pltpu.VMEM((count, 3 * width), BF16),
                pltpu.VMEM((width // PAIR, count, 2 * count), BF16),
                pltpu.VMEM((count, width), BF16),
                pltpu.VMEM((count, width), BF16),
                pltpu.VMEM((count, 3 * width), BF16),
                pltpu.VMEM((width, count), F32),
                pltpu.VMEM(w_up.shape, BF16),
                pltpu.VMEM(w_down.shape, BF16),
                pltpu.SemaphoreType.DMA((2,)),
            ] + fetched,
        ),
        compiler_params=pltpu.CompilerParams(vmem_limit_bytes=56 * MIB),
        cost_estimate=cost(10_000_000_000, width * width * 8),
        name="cross_block",
    )(ids, *read, w_up, w_down, *parts)


def with_cls(left_ref, right_ref, cls_left_ref, cls_right_ref):
    cls_product = dot_tn(cls_left_ref[...].astype(BF16), cls_right_ref[...])
    return (dot_tn(left_ref[...], right_ref[...]) + cls_product).astype(BF16)


def cols_grad_kernel(side, ids_ref, left_ref, right_ref, cls_left_ref, cls_right_ref, rider_ref, *refs):
    out_ref = refs[-1]
    owners, rows = rider_ref.shape[0], left_ref.shape[1] // rider_ref.shape[0]
    block = half_block(side, pl.program_id(0), ids_ref)
    product = with_cls(left_ref, right_ref, cls_left_ref, cls_right_ref)
    out_ref[0, :, :rows] = product.reshape(owners, rows, product.shape[1])
    rider = rider_ref[...]
    out_ref[0, :, rows:] = jnp.where(block == 0, rider, jnp.zeros_like(rider))


def joint_grad_kernel(side, ids_ref, left_ref, last_left_ref, right_ref, last_right_ref, *refs):
    block = half_block(side, pl.program_id(0), ids_ref)

    @pl.when(block < 3)
    def main():
        refs[-1][0] = dot_tn(left_ref[...], right_ref[...]).astype(BF16)

    @pl.when(block == 3)
    def last():
        refs[-1][0] = dot_tn(last_left_ref[...], last_right_ref[...]).astype(BF16)


def half_block(side, step, ids):
    return 2 * ((ids[1] & 1) ^ side) + step


def half_grads(kernel, name, ids, operands, specs, shape, after, weight):
    rows, width = operands[0].shape
    return pl.pallas_call(
        kernel,
        out_shape=jax.ShapeDtypeStruct((2,) + shape, BF16),
        grid_spec=pltpu.PrefetchScalarGridSpec(
            num_scalar_prefetch=1,
            grid=(2,),
            in_specs=specs + [ANYWHERE] * len(after),
            out_specs=pl.BlockSpec((1,) + shape, lambda j, ids: (j,) + (0,) * len(shape)),
        ),
        compiler_params=pltpu.CompilerParams(vmem_limit_bytes=56 * MIB),
        cost_estimate=cost(4 * rows * width * width, 10 * rows * width, weight),
        name=name,
    )(ids, *operands, *after)


def plain_cols_kernel(ids_ref, left_ref, right_ref, cls_left_ref, cls_right_ref, *refs):
    refs[-1][0] = with_cls(left_ref, right_ref, cls_left_ref, cls_right_ref)


def cols_grads(side, ids, left, right, cls_left, cls_right, rider, after, weight):
    rows, width = left.shape
    owners, extra, unused = rider.shape
    specs = [
        whole(left.shape),
        pl.BlockSpec((rows, width), lambda j, ids: (0, half_block(side, j, ids))),
        pl.BlockSpec((cls_left.shape[0], width), lambda j, ids: (0, CLS_LOW), pipeline_mode=pl.Buffered(1)),
        pl.BlockSpec((cls_left.shape[0], width), lambda j, ids: (0, half_block(side, j, ids))),
    ]
    operands = [left, right, cls_left, cls_right]
    if width // owners % 16 == 0:
        return half_grads(
            partial(cols_grad_kernel, side), "cols_grads", ids, operands + [rider], specs + [whole(rider.shape)],
            (owners, width // owners + extra, width), after, weight,
        )
    product = half_grads(plain_cols_kernel, "cols_grads", ids, operands, specs, (width, width), after, weight)
    first = half_block(side, 0, ids) == 0
    rider = jnp.where(first, rider, jnp.zeros_like(rider))
    rider = jnp.stack([rider, jnp.zeros_like(rider)], axis=0)
    return jnp.concatenate([product.reshape(2, owners, width // owners, width), rider], axis=2)


def joint_grads(side, ids, left, last_left, right, last_right, after, weight):
    rows, width = left.shape
    specs = [
        whole(left.shape),
        whole(left.shape),
        pl.BlockSpec((rows, width), lambda j, ids: (0, jnp.minimum(half_block(side, j, ids), 2))),
        whole(left.shape),
    ]
    operands = [left, last_left, right, last_right]
    return half_grads(partial(joint_grad_kernel, side), "joint_grads", ids, operands, specs, (width, width), after, weight)


def rows_grad_kernel(ids_ref, left_ref, right_ref, *refs):
    send_ref, keep_ref, held_ref = refs[-3:]
    core = ids_ref[1] & 1
    held_ref[...] = dot_tn(left_ref[...], right_ref[...]).reshape(held_ref.shape)
    for share in range(2):
        send_ref[share] = held_ref[:, 2 * (1 - core) + share].astype(BF16)
        keep_ref[share] = held_ref[:, 2 * core + share].astype(BF16)


def rows_grads(ids, left, right, count, after):
    rows, width = right.shape
    hidden = left.shape[1]
    shard_rows = hidden // count // 4
    owners = count // 4
    half = jax.ShapeDtypeStruct((2, count, shard_rows, width), BF16)
    out_spec = pl.BlockSpec((2, owners, shard_rows, width), lambda j, ids: (0, j, 0, 0))
    return pl.pallas_call(
        rows_grad_kernel,
        out_shape=(half, half),
        grid_spec=pltpu.PrefetchScalarGridSpec(
            num_scalar_prefetch=1,
            grid=(4,),
            in_specs=[
                pl.BlockSpec((rows, hidden // 4), lambda j, ids: (0, j)),
                pl.BlockSpec((rows, width), lambda j, ids: (0, 0), pipeline_mode=pl.Buffered(1)),
            ] + [ANYWHERE] * len(after),
            out_specs=[out_spec, out_spec],
            scratch_shapes=[pltpu.VMEM((owners, 4, shard_rows, width), F32)],
        ),
        compiler_params=pltpu.CompilerParams(vmem_limit_bytes=56 * MIB),
        cost_estimate=cost(2 * rows * width * hidden, 10 * rows * width),
        name="rows_grads",
    )(ids, left, right, *after)


def later(value, *first):
    return lax.optimization_barrier((value,) + first)[0]


def seg_swap(value, mask):
    count = lax.axis_size("seg")
    return lax.ppermute(value, "seg", [(i, i ^ mask) for i in range(count)])


def rep_swap(value, mask):
    count = lax.axis_size("rep")
    return lax.ppermute(value, "rep", [(i, i ^ mask) for i in range(count)])


def both_swap(value, seg_mask, rep_mask):
    reps = lax.axis_size("rep")
    total = lax.axis_size("seg") * reps
    pairs = [(i, ((i // reps) ^ seg_mask) * reps + ((i % reps) ^ rep_mask)) for i in range(total)]
    return lax.ppermute(value, ("seg", "rep"), pairs)


def place_kernel(plan, count, owner_first, ids_ref, *refs):
    for copy in fetch_pieces(ids_ref, plan, refs[:count], refs[count], refs[count + 1], 0, owner_first):
        copy.wait()


def put_in_place(ids, pieces, owner_first=False):
    plan, parts, shape = pieces
    return pl.pallas_call(
        partial(place_kernel, plan, len(parts), owner_first),
        out_shape=shape,
        in_specs=[pl.BlockSpec(memory_space=pltpu.SMEM)] + [ANYWHERE] * len(parts),
        out_specs=pl.BlockSpec(memory_space=pltpu.VMEM),
        scratch_shapes=[pltpu.SemaphoreType.DMA((4 * len(plan),))],
        compiler_params=pltpu.CompilerParams(vmem_limit_bytes=32 * MIB),
        cost_estimate=cost(0, 4 * shape.size),
        name="put_in_place",
    )(ids, *parts)


def own_half(ids, blocks):
    return lax.dynamic_slice_in_dim(blocks, 2 * (ids[1] & 1), 2, 0)


def far_pieces(piece):
    return [piece] + [seg_swap(piece, mask) for mask in range(2, lax.axis_size("seg"), 2)]


def after_all(value, first):
    return later(value, *first) if first else value


def gather_singly(piece, evens, firsts):
    held, crossed = [], []
    for number, even in enumerate(evens):
        before = held[-1:] + [rep_swap(part, 1) for part in held[-4:-2]]
        crossed += before[1:]
        held += [even, seg_swap(after_all(even, before + firsts.get(number, [])), 1)]
    crossed += [rep_swap(part, 1) for part in held[-4:-1]] + [rep_swap(after_all(held[-1], firsts.get(-1, [])), 1)]
    return held, crossed


def pieces_of(held, crossed, shapes):
    count = len(held)
    return [(i, i % count, i // count) for i in range(2 * count)], held + crossed, shapes


class Gather:
    def __init__(self, piece):
        self.piece, self.came = piece, far_pieces(piece)

    def across(self, *first):
        self.evens = jnp.stack(self.came[:1] + [later(value, *first) for value in self.came[1:]], axis=0)
        self.came = seg_swap(self.evens, 1)

    def finish(self, *first):
        return jnp.stack([self.evens, later(self.came, *first)], axis=1).reshape((-1,) + self.piece.shape)


def spread_kernel(ids_ref, keep_ref, came_ref, *refs):
    stay_ref, x_ref, y_ref, xy_ref = refs[-4:]
    near, across, core = ids_ref[0] & 1, ids_ref[1] >> 1, ids_ref[1] & 1

    def total(share, side):
        value = keep_ref[share, 0, side].astype(F32) + came_ref[share, 0, side].astype(F32)
        if len(refs) > 4:
            for left_ref, right_ref in (refs[:2], refs[2:4]):
                value = value + dot_nn(left_ref[0, side, 2 * core + share], right_ref[...])
        return value.astype(BF16)

    stay_ref[0] = total(across, near)
    x_ref[0] = total(across, 1 - near)
    y_ref[0] = total(1 - across, near)
    xy_ref[0] = total(1 - across, 1 - near)


def spread(ids, keep, came, product=()):
    unused, count, rows, width = keep.shape
    far = count // 2
    shape = (2, far, 2, rows, width)
    in_spec = pl.BlockSpec((2, 1, 2, rows, width), lambda j: (0, j, 0, 0, 0))
    out_spec = pl.BlockSpec((1, rows, width), lambda j: (j, 0, 0))
    out = jax.ShapeDtypeStruct((far, rows, width), BF16)
    specs = [pl.BlockSpec(memory_space=pltpu.SMEM), in_spec, in_spec]
    if product:
        depth = product[1].shape[0]
        product = [value.reshape(far, 2, 4, rows, depth) if i % 2 == 0 else value for i, value in enumerate(product)]
        specs += [pl.BlockSpec((1, 2, 4, rows, depth), lambda j: (j, 0, 0, 0, 0)), whole(product[1].shape)] * 2
    return pl.pallas_call(
        spread_kernel,
        out_shape=(out,) * 4,
        grid=(far,),
        in_specs=specs,
        out_specs=[out_spec] * 4,
        compiler_params=pltpu.CompilerParams(vmem_limit_bytes=32 * MIB),
        cost_estimate=cost(0, 12 * count * rows * width),
        name="spread",
    )(ids, keep.reshape(shape), came.reshape(shape), *product)


def settle_kernel(ids_ref, *refs):
    far = refs[0].shape[0]
    parts, outs = refs[:-far], refs[-far:]
    start = 0
    for first in range(0, len(parts), 4):
        rows = parts[first].shape[1]
        for mask, out in enumerate(outs):
            a, b, c, d = (part[(ids_ref[0] >> 1) ^ mask].astype(F32) for part in parts[first : first + 4])
            out[start : start + rows] = ((a + b) + (c + d)).astype(BF16)
        start += rows


def settle(ids, *groups):
    far, unused, width = groups[0][0].shape
    heights = [group[0].shape[1] for group in groups]
    if len(groups) > 1 and any(rows % 16 for rows in heights):
        return [jnp.concatenate(parts, axis=0) for parts in zip(*[settle(ids, group) for group in groups])]
    whole_spec = pl.BlockSpec(memory_space=pltpu.VMEM)
    return pl.pallas_call(
        settle_kernel,
        out_shape=(jax.ShapeDtypeStruct((sum(heights), width), BF16),) * far,
        in_specs=[pl.BlockSpec(memory_space=pltpu.SMEM)] + [whole_spec] * (4 * len(groups)),
        out_specs=[whole_spec] * far,
        compiler_params=pltpu.CompilerParams(vmem_limit_bytes=32 * MIB),
        cost_estimate=cost(0, 10 * far * sum(heights) * width),
        name="settle",
    )(ids, *[part for group in groups for part in group])


def halve(value, axis, bit):
    own = lax.dynamic_index_in_dim(value, bit, axis, keepdims=False)
    other = lax.dynamic_index_in_dim(value, 1 - bit, axis, keepdims=False)
    return own, other


class Reduction:
    def __init__(self, ids, send, keep):
        count = lax.axis_size("seg")
        self.ids = ids
        self.shape = (2, count, send.size // (2 * count * send.shape[-1]), send.shape[-1])
        self.keep = keep
        self.came = rep_swap(send, 1)

    def spread(self, *first, product=()):
        came = after_all(self.came, first)
        self.stay, *sends = spread(self.ids, self.keep.reshape(self.shape), came.reshape(self.shape), product)
        self.came = [seg_swap(sends[0], 1), rep_swap(sends[1], 2), both_swap(sends[2], 1, 2)]

    def parts(self, *first):
        return [self.stay] + [after_all(value, first) for value in self.came]


def swap_far(others):
    return [seg_swap(other, 2 * mask) for mask, other in enumerate(others, 1)]


def add_up(own, came, *first):
    total = own.astype(F32)
    for value in came:
        total = total + after_all(value, first).astype(F32)
    return total.astype(BF16)


class Sharing:
    def __init__(self, ids, value):
        self.ids, self.value = ids, value
        self.came = rep_swap(value, 2)

    def step(self, *first):
        self.value = jnp.stack([self.value, later(self.came, *first)], axis=0)
        self.came = rep_swap(self.value, 1)

    def finish(self, *first):
        held = jnp.concatenate([self.value, later(self.came, *first)], axis=0)
        places = [self.ids[1] ^ owner for owner in (0, 2, 1, 3)]
        return [
            lax.dynamic_index_in_dim(held, 2 * (place & 1) + place // 2, 0, keepdims=False).astype(F32) for place in places
        ]


def body(tokens, cotangent, doc_counts, w_qkv, w_out, w_up, w_down, c_qkv, c_out, pos_table, norm_gains, norm_shifts):
    micro_count, unused, seg_local, seg_length, width = tokens.shape
    count = lax.axis_size("seg")
    me = lax.axis_index("seg").astype(jnp.int32)
    rep = lax.axis_index("rep").astype(jnp.int32)
    ids = jnp.stack([me, rep])
    shard_rows = w_qkv.shape[0]
    local = micro_count * seg_local
    rows = local * seg_length
    table_rows = pos_table.shape[0]
    norm_cols = norm_gains.shape[1]
    aligned = shard_rows % 16 == 0

    def shares_of(matrix):
        return matrix.reshape(shard_rows, 4, width).transpose(1, 0, 2)

    def own_share(matrix):
        return lax.dynamic_slice_in_dim(matrix, rep * width, width, 1)

    norms = jnp.pad(jnp.concatenate([norm_gains, norm_shifts], axis=0), ((0, 2), (0, width - norm_cols)))
    small = jnp.pad(jnp.stack([pos_table, norms], axis=0), ((0, 0), (0, 16 - table_rows), (0, 0)))
    ffn_piece = jnp.concatenate(
        [own_half(ids, shares_of(w_up)), own_half(ids, w_down.reshape(4, shard_rows, width)), small], axis=1
    )
    ffn_half = lax.all_gather(ffn_piece, "seg", axis=0)
    qo_piece = own_half(ids, shares_of(jnp.concatenate([w_qkv, w_out], axis=1)))
    qo_evens = far_pieces(qo_piece)
    shapes = [shape_of((4, count, shard_rows, width), BF16), shape_of((count, 4, shard_rows, width), BF16)]
    qo_pieces = pieces_of(*gather_singly(qo_piece, qo_evens, {}), shapes[0])
    cross_piece = own_half(ids, shares_of(jnp.concatenate([c_qkv, c_out], axis=1)))
    cross_half = lax.all_gather(later(cross_piece, qo_evens[1]), "seg", axis=0)

    counts = doc_counts[:, 0]
    ends = jnp.cumsum(counts, axis=1)
    owners = me ^ jnp.arange(count, dtype=jnp.int32)
    seg_ids = owners[:, None, None] * seg_local + jnp.arange(seg_local, dtype=jnp.int32)[None, None, :]
    seg_ids = jnp.broadcast_to(seg_ids, (count, micro_count, seg_local))
    past = seg_ids[..., None] >= ends[None, :, None, :]
    doc_ids = jnp.sum(past.astype(jnp.int32), axis=-1)
    starts = jnp.sum(jnp.where(past, counts[None, :, None, :], 0), axis=-1)
    places = (seg_ids - starts).reshape(-1, 1)
    keys = (doc_ids + (counts.shape[1] + 1) * jnp.arange(micro_count, dtype=jnp.int32)[None, :, None]).reshape(-1)

    flat = tokens.reshape(rows, width)
    cot = cotangent.reshape(rows, width)
    block = 4 * seg_length
    steps = rows // block
    halves_of = ((0, steps // 2), (steps // 2, steps - steps // 2))

    everything = (0, steps)
    if aligned:
        proj, probs, mixed, pre_first, full_qo = attention_forward(
            flat, None, seg_length, block, everything, after=[keys, places], pieces=qo_pieces, ids=ids
        )
    else:
        full_qo = put_in_place(ids, qo_pieces).reshape(4, 1, width, width)
        proj, probs, mixed, pre_first = attention_forward(flat, full_qo, seg_length, block, everything)
    ffn_half = later(ffn_half, proj)
    small = ffn_half[:, :, 2 * shard_rows :]
    table = small[:, 0, :table_rows].reshape(count * table_rows, width)
    norms = small[:, 1, :6, :norm_cols].transpose(1, 0, 2).reshape(6, width)
    gains, shifts = norms[:3], norms[3:]
    ffn_other = rep_swap(ffn_half, 1)

    def joined(parts, start, owner_first):
        own, other = [part[:, :, start : start + shard_rows] for part in parts]
        both = jnp.where((rep & 1) == 0, jnp.concatenate([own, other], axis=1), jnp.concatenate([other, own], axis=1))
        return (both if owner_first else both.transpose(1, 0, 2, 3)).reshape(4, 1, width, width)

    small_block = 2 * seg_length
    if aligned:
        low, act, slope, out, branch, grad2, sums2, cls, full_up, full_down = ffn_forward(
            pre_first, cot, None, gains, shifts, seg_length, small_block, ([ffn_half, ffn_other], shapes), ids
        )
    else:
        full_up = joined([ffn_half, ffn_other], 0, False)
        full_down = joined([ffn_half, ffn_other], shard_rows, True)
        low, act, slope, out, branch, grad2, sums2, cls = ffn_forward(
            pre_first, cot, [full_up, full_down], gains, shifts, seg_length, small_block
        )

    def with_edge(values, edge):
        whole_rows = values.reshape(local, seg_length, values.shape[1])
        return lax.dynamic_update_slice(whole_rows, edge[:, None], (0, 0, 0)).reshape(values.shape)

    edges = Gather(cls[:, CLS_OUT * width : (CLS_COT + 1) * width])
    send_down, keep_down = rows_grads(ids, act, branch, count, [edges.piece])
    down = Reduction(ids, send_down, keep_down)
    edges.across(send_down)
    cross_half = later(cross_half, send_down)
    cross_other = rep_swap(cross_half, 1)
    *kept, sums1a = ffn_backward(
        branch, grad2, pre_first, slope, full_up, full_down, gains, block, halves_of[0], LONG, after=[edges.evens, cross_half]
    )
    edges = edges.finish(kept[0]).reshape(-1, 2 * width)
    cross_parts, cross_shape = [cross_half, later(cross_other, kept[0])], shapes[0]
    if not aligned:
        cross_parts, cross_shape = [joined(cross_parts, 0, False)], None
    cls_new, cls_branch, grad_c, c_sums, table_grad, *cls_back = cross_block(
        ids, edges, cls, keys[:, None], jnp.concatenate([keys, keys])[None, :], places, table, gains, shifts, full_up,
        full_down, cross_parts, cross_shape,
    )
    cls_hidden, cls_grad1, cls_low1, cls_turned = cls_back
    operands = [cls_turned, cls_branch]
    c_own, c_other = halve(grad_c.reshape(2, 2, shard_rows, width), 0, rep & 1)
    c_came = rep_swap(c_other, 1)
    down.spread(kept[0], product=operands + [rep_swap(value, 1) for value in operands])
    grad_hidden, grad1, low1, sums1b = ffn_backward(
        branch, grad2, pre_first, slope, full_up, full_down, gains, block, halves_of[1], SHORT, prior=kept, after=[down.stay]
    )
    low1 = with_edge(low1, cls_low1)
    norm_sums = (sums2 + sums1a + sums1b + c_sums).reshape(8, count, norm_cols).transpose(1, 0, 2)
    norm_sums = jnp.pad(norm_sums, ((0, 0), (0, 0), (0, width - norm_cols)))
    rider = jnp.concatenate([norm_sums, table_grad.reshape(count, table_rows, width)], axis=1).astype(BF16)
    send_up = cols_grads(1, ids, low, grad_hidden, cls, cls_hidden, rider, [], SHORT)
    own_down, *others = settle(ids, down.parts(send_up))
    came_down = swap_far(others)
    keep_up = cols_grads(0, ids, low, grad_hidden, cls, cls_hidden, rider, [send_up, own_down], LONG)
    up = Reduction(ids, send_up, keep_up)
    up.spread(keep_up, *came_down[:1])
    grad_proj = attention_backward(low1, proj, probs, full_qo, seg_length, block, after=[up.stay])
    down_share = add_up(own_down, came_down, grad_proj)
    c_own, c_other = halve(c_own.astype(F32) + later(c_came, grad_proj).astype(F32), 0, rep >> 1)
    c_came = rep_swap(c_other.astype(BF16), 2)
    send_qo = joint_grads(1, ids, flat, mixed, grad_proj, low1, [], SHORT)
    own_up, *others = settle(ids, up.parts(send_qo))
    came_up = swap_far(others)
    keep_qo = joint_grads(0, ids, flat, mixed, grad_proj, low1, [send_qo, own_up], LONG)
    qo = Reduction(ids, send_qo, keep_qo)
    qo.spread(keep_qo, *came_up[:2])
    input_grad = input_gradient(with_edge(later(grad1, qo.stay), cls_grad1), grad_proj, full_qo, block, [qo.stay])
    own, *others = settle(ids, qo.parts(input_grad))
    came = swap_far(others)
    c_share = (c_own + later(c_came, own).astype(F32)).astype(BF16)
    early = Sharing(ids, jnp.concatenate([down_share, add_up(own_up, came_up, own), c_share], axis=0))
    late = Sharing(ids, add_up(own, came))
    early.step(late.value)
    layer_out = with_edge(later(out, late.value), cls_new)
    early_shares = early.finish(layer_out)
    starts = (0, shard_rows, 2 * shard_rows, 2 * shard_rows + 16, 3 * shard_rows + 16)
    down_parts, up_parts, riders, c_parts = [
        [part[first:last] for part in early_shares] for first, last in zip(starts, starts[1:])
    ]
    done = [
        jnp.concatenate(up_parts, axis=1),
        jnp.concatenate(down_parts, axis=0),
        jnp.concatenate(c_parts[:3], axis=1),
        c_parts[3],
    ]
    summed = riders[0]
    late.step(layer_out, *done)
    qo_parts = late.finish()

    return (
        layer_out.reshape(tokens.shape),
        input_grad.reshape(tokens.shape),
        jnp.concatenate(qo_parts[:3], axis=1),
        qo_parts[3],
        *done,
        summed[8 : 8 + table_rows],
        summed[:3, :norm_cols],
        summed[3:6, :norm_cols],
    )


def solution(mesh):
    rows = P(None, "rep", "seg", None, None)
    split = P("seg", None)
    last = P(None, "seg")
    return jax.shard_map(
        body,
        mesh=mesh,
        in_specs=(rows, rows, P(None, "rep", None)) + (split,) * 7 + (last, last),
        out_specs=(rows, rows) + (split,) * 7 + (last, last),
        check_vma=False,
    )
```

```python
from functools import partial
import jax
import jax.numpy as jnp
from jax import lax
from jax.experimental import pallas as pl
from jax.experimental.pallas import tpu as pltpu
from jax.sharding import PartitionSpec as P

HEAD_DIM = 64
PAIR = 2 * HEAD_DIM
EPSILON = 1e-05
NEGATIVE = -1e30
F32 = jnp.float32
BF16 = jnp.bfloat16
MIB = 1 << 20
LONG, SHORT = 6.0, 0.001
CLS_ACT, CLS_SLOPE, CLS_LOW, CLS_PRE, CLS_TOTAL, CLS_OUT, CLS_COT, CLS_BLOCKS = 0, 4, 8, 9, 10, 11, 12, 13


def dot_nn(left, right):
    return lax.dot_general(left, right, (((1,), (0,)), ((), ())), preferred_element_type=F32)


def dot_nt(left, right):
    return lax.dot_general(left, right, (((1,), (1,)), ((), ())), preferred_element_type=F32)


def dot_tn(left, right):
    return lax.dot_general(left, right, (((0,), (0,)), ((), ())), preferred_element_type=F32)


def norm_parts(values):
    center = values - jnp.mean(values, axis=-1, keepdims=True)
    spread = jnp.mean(center * center, axis=-1, keepdims=True)
    inverse = lax.rsqrt(spread + EPSILON)
    return center * inverse, inverse


def norm_back(grad, unit, inverse, gain):
    scaled = grad * gain
    first = jnp.mean(scaled, axis=-1, keepdims=True)
    second = jnp.mean(scaled * unit, axis=-1, keepdims=True)
    return inverse * (scaled - first - unit * second)


def gelu_parts(hidden):
    phi = 0.5 + 0.5 * lax.erf(hidden * 0.5 ** 0.5)
    bell = jnp.exp(hidden * hidden * -0.5) * 0.3989422804014327
    return hidden * phi, phi + hidden * bell


def halves(pair, first_half):
    zero = jnp.zeros_like(pair)
    return jnp.concatenate([jnp.where(first_half, pair, zero), jnp.where(first_half, zero, pair)], axis=0)


def pair_forward(query, key, value, first_half, same=None):
    rows = query.shape[0]
    scores = dot_nt(key, halves(query * BF16(HEAD_DIM ** -0.5), first_half))
    if same is not None:
        scores = jnp.where(same, scores, NEGATIVE)
    raised = jnp.exp(scores - jnp.max(scores, axis=0, keepdims=True))
    probs = (raised * (1.0 / jnp.sum(raised, axis=0, keepdims=True))).astype(BF16)
    both = dot_tn(probs, value)
    return probs, jnp.where(first_half, both[:rows], both[rows:])


def pair_backward(query, key, value, probs, grad_mixed, first_half):
    rows = query.shape[0]
    grad_both = halves(grad_mixed, first_half)
    query_both = halves(query * BF16(HEAD_DIM ** -0.5), first_half)
    grad_probs = dot_nt(value, grad_both)
    wide = probs.astype(F32)
    grad_scores = (wide * (grad_probs - jnp.sum(grad_probs * wide, axis=0, keepdims=True))).astype(BF16)
    grad_value = dot_nn(probs, grad_both)
    grad_key = dot_nn(grad_scores, query_both)
    both = dot_tn(grad_scores, key)
    grad_query = jnp.where(first_half, both[:rows], both[rows:]) * (HEAD_DIM ** -0.5)
    return grad_query, grad_key, grad_value


def lane_half(shape):
    return lax.broadcasted_iota(jnp.int32, shape, 1) % PAIR < HEAD_DIM


def square(value):
    return value.reshape(-1, value.shape[-1])


def up_block(ref, part):
    return square(ref[:, part])


def down_block(ref, part):
    count = ref.shape[0] // 4
    return square(ref[part * count : (part + 1) * count])


def whole(shape):
    return pl.BlockSpec(shape, lambda *at: (0,) * len(shape), pipeline_mode=pl.Buffered(1))


ANYWHERE = pl.BlockSpec(memory_space=pl.ANY)


def cost(flops, moved, weight=1.0):
    return pl.CostEstimate(flops=int(flops * weight), bytes_accessed=int(moved * weight), transcendentals=0)


def rows_call(kernel, name, block, span, rowed, fixed, outs, flops, prior=(), after=(), extra=(), ids=None, scratch=(), weight=1.0):
    first, steps = span

    def cut(value):
        array, ratio = value if isinstance(value, tuple) else (value, 1)
        shape = (block // ratio,) + array.shape[1:]
        return array, pl.BlockSpec(shape, lambda i, *ids: (i + first,) + (0,) * (len(shape) - 1))

    ins = [cut(value) for value in rowed] + list(fixed)
    results = [cut(value) for value in outs] + [(shape, whole(shape.shape)) for shape in extra]
    unread = list(prior) + list(after)
    lead = 0 if ids is None else 1
    moved = sum(value.size * value.dtype.itemsize for value, unused in ins + results) // 2

    def run(*refs):
        start = lead + len(ins)
        kernel(*refs[:start], *refs[start + len(unread) :])

    return pl.pallas_call(
        run,
        out_shape=tuple(jax.ShapeDtypeStruct(shape.shape, shape.dtype) for shape, unused in results),
        grid_spec=pltpu.PrefetchScalarGridSpec(
            num_scalar_prefetch=lead,
            grid=(steps,),
            in_specs=[spec for unused, spec in ins] + [ANYWHERE] * len(unread),
            out_specs=[spec for unused, spec in results],
            scratch_shapes=list(scratch),
        ),
        input_output_aliases={lead + len(ins) + i: i for i in range(len(prior))},
        compiler_params=pltpu.CompilerParams(vmem_limit_bytes=58 * MIB),
        cost_estimate=cost(2 * flops * steps * block, moved, weight),
        name=name,
    )(*([] if ids is None else [ids]), *[array for array, unused in ins], *unread)


def shape_of(shape, dtype):
    return jax.ShapeDtypeStruct(shape, dtype)


def fetch_pieces(ids_ref, parts, out_ref, sems):
    me, rep = ids_ref[0], ids_ref[1]
    copies = []
    for number, part in enumerate(parts):
        for slot in range(part.shape[0]):
            target = out_ref.at[rep ^ (number // 2), me ^ (2 * slot + number % 2)]
            copies.append(pltpu.make_async_copy(part.at[slot], target, sems.at[number * part.shape[0] + slot]))
    for copy in copies:
        copy.start()
    return copies


def fetch_halves(ids_ref, parts, out_ref, sems, start=0, owner_first=False):
    core = ids_ref[1] & 1
    rows = out_ref.shape[2]
    base = 4 if owner_first else 0
    copies = []
    for side, part in enumerate(parts):
        owner_core = core if side == 0 else 1 - core
        for share in range(2):
            piece = part.at[:, share] if part.shape[-2] == rows else part.at[:, share, pl.ds(start, rows)]
            block = 2 * owner_core + share
            target = out_ref.at[:, block] if owner_first else out_ref.at[block]
            copies.append(pltpu.make_async_copy(piece, target, sems.at[base + 2 * side + share]))
    for copy in copies:
        copy.start()
    return copies


def attention_rows(seg_length, x_ref, wqo_ref, proj_ref, probs_ref, mixed_ref, pre_ref):
    rows, width = x_ref.shape
    pairs = width // PAIR
    for part in range(3):
        proj_ref[:, part * width : (part + 1) * width] = dot_nn(x_ref[...], square(wqo_ref[part])).astype(BF16)
    first_half = lane_half((seg_length, PAIR))
    for seg in range(rows // seg_length):
        span = slice(seg * seg_length, (seg + 1) * seg_length)
        for pair in range(pairs):
            cols = [slice(part * width + pair * PAIR, part * width + (pair + 1) * PAIR) for part in range(3)]
            probs, mixed = pair_forward(
                proj_ref[span, cols[0]], proj_ref[span, cols[1]], proj_ref[span, cols[2]], first_half
            )
            probs_ref[seg, pair] = probs
            mixed_ref[span, cols[0]] = mixed.astype(BF16)
    pre_ref[...] = x_ref[...].astype(F32) + dot_nn(mixed_ref[...], square(wqo_ref[3]))


def attention_first_kernel(seg_length, count, ids_ref, x_ref, *refs):
    parts, (proj_ref, probs_ref, mixed_ref, pre_ref, wqo_ref, sems) = refs[:count], refs[count:]

    @pl.when(pl.program_id(0) == 0)
    def fetch():
        for copy in fetch_pieces(ids_ref, parts, wqo_ref, sems):
            copy.wait()

    attention_rows(seg_length, x_ref, wqo_ref, proj_ref, probs_ref, mixed_ref, pre_ref)


def attention_shapes(rows, width, seg_length):
    probs = shape_of((rows // seg_length, width // PAIR, seg_length, 2 * seg_length), BF16)
    return [
        shape_of((rows, 3 * width), BF16), (probs, seg_length), shape_of((rows, width), BF16), shape_of((rows, width), F32),
    ]


def attention_forward(rows_in, weight, seg_length, block, span, prior=(), after=(), pieces=None, ids=None):
    rows, width = rows_in.shape
    outs = attention_shapes(rows, width, seg_length)
    flops = width * (4 * width + 8 * seg_length)
    if pieces is None:
        return rows_call(
            partial(attention_rows, seg_length), "attention_forward", block, span, [rows_in],
            [(weight, whole(weight.shape))], outs, flops, prior, after, weight=SHORT,
        )
    parts, shape = pieces
    return rows_call(
        partial(attention_first_kernel, seg_length, len(parts)), "attention_forward", block, span, [rows_in],
        [(part, ANYWHERE) for part in parts], outs, flops, prior, after, [shape], ids,
        [pltpu.SemaphoreType.DMA((len(parts) * parts[0].shape[0],))], SHORT,
    )


def ffn_rows(
    seg_length, pre_ref, cot_ref, wup_ref, wdown_ref, gains_ref, shifts_ref,
    low_ref, act_ref, slope_ref, out_ref, branch_ref, grad_ref, sums_ref, cls_ref,
):
    rows, width = pre_ref.shape
    segs = rows // seg_length

    def keep_cls(block, values):
        for seg in range(segs):
            row = values[seg * seg_length : seg * seg_length + 1].astype(F32)
            cls_ref[pl.ds(pl.program_id(0) * segs + seg, 1), block * width : (block + 1) * width] = row

    unit, unused = norm_parts(pre_ref[...])
    total = unit * gains_ref[0:1].astype(F32) + shifts_ref[0:1].astype(F32)
    low = total.astype(BF16)
    low_ref[...] = low
    held = dot_nn(low, square(wup_ref[0]))
    for part in range(4):
        cols = slice(part * width, (part + 1) * width)
        ahead = dot_nn(low, square(wup_ref[part + 1])) if part < 3 else None
        act, slope = gelu_parts(held)
        act, slope = act.astype(BF16), slope.astype(BF16)
        act_ref[:, cols] = act
        slope_ref[:, cols] = slope
        keep_cls(CLS_ACT + part, act)
        keep_cls(CLS_SLOPE + part, slope)
        total = total + dot_nn(act_ref[:, cols], down_block(wdown_ref, part))
        held = ahead
    gain = gains_ref[1:2].astype(F32)
    unit, inverse = norm_parts(total)
    out = unit * gain + shifts_ref[1:2].astype(F32)
    out_ref[...] = out.astype(BF16)
    keep_cls(CLS_LOW, low)
    keep_cls(CLS_PRE, pre_ref)
    keep_cls(CLS_TOTAL, total)
    keep_cls(CLS_OUT, out)
    keep_cls(CLS_COT, cot_ref)
    is_cls = lax.broadcasted_iota(jnp.int32, total.shape, 0) % seg_length == 0
    grad = jnp.where(is_cls, 0.0, cot_ref[...].astype(F32))
    pre_grad = norm_back(grad, unit, inverse, gain)
    grad_ref[...] = pre_grad
    branch_ref[...] = pre_grad.astype(BF16)

    @pl.when(pl.program_id(0) == 0)
    def start_sums():
        sums_ref[...] = jnp.zeros_like(sums_ref)

    sums_ref[1:2] += jnp.sum(grad * unit, axis=0, keepdims=True)
    sums_ref[4:5] += jnp.sum(grad, axis=0, keepdims=True)


def ffn_first_kernel(seg_length, ids_ref, pre_ref, cot_ref, gains_ref, shifts_ref, half_ref, other_ref, *refs):
    *outs, wup_ref, wdown_ref, sems = refs

    @pl.when(pl.program_id(0) == 0)
    def fetch():
        parts = (half_ref, other_ref)
        up = fetch_halves(ids_ref, parts, wup_ref, sems)
        down = fetch_halves(ids_ref, parts, wdown_ref, sems, wup_ref.shape[2], True)
        for copy in up + down:
            copy.wait()

    ffn_rows(seg_length, pre_ref, cot_ref, wup_ref, wdown_ref, gains_ref, shifts_ref, *outs)


def ffn_forward(pre_first, cot, weights, gains, shifts, seg_length, block, pieces=None, ids=None):
    rows, width = pre_first.shape
    span = (0, rows // block)
    wide, low = shape_of((rows, 4 * width), BF16), shape_of((rows, width), BF16)
    outs = [low, wide, wide, low, low, shape_of((rows, width), F32)]
    extra = [shape_of((8, width), F32), shape_of((rows // seg_length, CLS_BLOCKS * width), F32)]
    if pieces is None:
        return rows_call(
            partial(ffn_rows, seg_length), "ffn_forward", block, span, [pre_first, cot],
            [(value, whole(value.shape)) for value in (*weights, gains, shifts)], outs, 8 * width * width, extra=extra,
        )
    parts, shapes = pieces
    return rows_call(
        partial(ffn_first_kernel, seg_length), "ffn_forward", block, span, [pre_first, cot],
        [(gains, whole(gains.shape)), (shifts, whole(shifts.shape))] + [(part, ANYWHERE) for part in parts], outs,
        8 * width * width, extra=extra + shapes, ids=ids, scratch=[pltpu.SemaphoreType.DMA((8,))],
    )


def ffn_back_rows(
    branch_ref, grad2_ref, pre1_ref, slope_ref, wup_hbm, wdown_hbm, gains_ref, gradh_ref, grad1_ref, low1_ref, sums_ref,
    wup_ref, wdown_ref, sems,
):
    width = branch_ref.shape[1]
    owners = wdown_ref.shape[0] // 4
    copies = []
    for part in range(4):
        place = pl.ds(part * owners, owners)
        copies += [
            pltpu.make_async_copy(wdown_hbm.at[place], wdown_ref.at[place], sems.at[2 * part]),
            pltpu.make_async_copy(wup_hbm.at[part], wup_ref.at[part], sems.at[2 * part + 1]),
        ]
    first_step = pl.program_id(0) == 0

    @pl.when(first_step)
    def fetch():
        sums_ref[...] = jnp.zeros_like(sums_ref)
        for copy in copies:
            copy.start()

    total = grad2_ref[...]
    for part in range(4):
        cols = slice(part * width, (part + 1) * width)

        @pl.when(first_step)
        def arrive():
            copies[2 * part].wait()
            copies[2 * part + 1].wait()

        grad_act = dot_nt(branch_ref[...], down_block(wdown_ref, part))
        grad_hidden = (grad_act * slope_ref[:, cols].astype(F32)).astype(BF16)
        gradh_ref[:, cols] = grad_hidden
        total = total + dot_nt(grad_hidden, square(wup_ref[part]))
    unit, inverse = norm_parts(pre1_ref[...])
    grad1 = norm_back(total, unit, inverse, gains_ref[0:1].astype(F32))
    grad1_ref[...] = grad1
    low1_ref[...] = grad1.astype(BF16)
    sums_ref[0:1] += jnp.sum(total * unit, axis=0, keepdims=True)
    sums_ref[3:4] += jnp.sum(total, axis=0, keepdims=True)


def ffn_backward(branch, grad2, pre_first, slope, w_up, w_down, gains, block, span, weight, prior=(), after=()):
    rows, width = branch.shape
    return rows_call(
        ffn_back_rows, "ffn_backward", block, span, [branch, grad2, pre_first, slope],
        [(w_up, ANYWHERE), (w_down, ANYWHERE), (gains, whole(gains.shape))],
        [shape_of((rows, 4 * width), BF16), shape_of((rows, width), F32), shape_of((rows, width), BF16)],
        8 * width * width, prior, after, [shape_of((8, width), F32)], weight=weight,
        scratch=[pltpu.VMEM(w_up.shape, BF16), pltpu.VMEM(w_down.shape, BF16), pltpu.SemaphoreType.DMA((8,))],
    )


def attention_back_rows(seg_length, low1_ref, proj_ref, probs_ref, wqo_ref, gradp_ref, gradm_ref):
    rows, width = low1_ref.shape
    pairs = width // PAIR
    gradm_ref[...] = dot_nt(low1_ref[...], square(wqo_ref[3])).astype(BF16)
    first_half = lane_half((seg_length, PAIR))
    for seg in range(rows // seg_length):
        span = slice(seg * seg_length, (seg + 1) * seg_length)
        for pair in range(pairs):
            cols = [slice(part * width + pair * PAIR, part * width + (pair + 1) * PAIR) for part in range(3)]
            grads = pair_backward(
                proj_ref[span, cols[0]], proj_ref[span, cols[1]], proj_ref[span, cols[2]],
                probs_ref[seg, pair], gradm_ref[span, cols[0]], first_half,
            )
            for place, grad in zip(cols, grads):
                gradp_ref[span, place] = grad.astype(BF16)


def attention_backward(low1, proj, probs, w_qo, seg_length, block, after=()):
    rows, width = low1.shape
    return rows_call(
        partial(attention_back_rows, seg_length), "attention_backward", block, (0, rows // block),
        [low1, proj, (probs, seg_length)], [(w_qo, whole(w_qo.shape))],
        [shape_of((rows, 3 * width), BF16)],
        width * (width + 16 * seg_length), (), after, scratch=[pltpu.VMEM((block, width), BF16)], weight=SHORT,
    )[0]


def input_rows(grad1_ref, gradp_ref, wqo_ref, input_ref):
    width = grad1_ref.shape[1]
    total = grad1_ref[...]
    for part in range(3):
        total = total + dot_nt(gradp_ref[:, part * width : (part + 1) * width], square(wqo_ref[part]))
    input_ref[...] = total


def input_gradient(grad1, gradp, w_qo, block, after):
    rows, width = grad1.shape
    return rows_call(
        input_rows, "input_gradient", block, (0, rows // block), [grad1, gradp], [(w_qo, whole(w_qo.shape))],
        [shape_of((rows, width), F32)], 3 * width * width, (), after, weight=LONG,
    )[0]


def cross_kernel(
    local, fetch, ids_ref, rows_ref, cls_ref, keyc_ref, keyr_ref, place_ref, table_ref, gains_ref, shifts_ref,
    wup_hbm, wdown_hbm, *refs
):
    parts, refs = (refs[:2], refs[2:]) if fetch else (refs[:1], refs[1:])
    new_ref, branch_ref, grad_c_ref, sums_ref, table_grad_ref, hidden_ref, grad1_ref, low1_ref, turned_ref = refs[:9]
    proj_ref, probs_ref, gradm_ref, mixed_ref, gradp_ref, lying_ref, wup_ref, wdown_ref, ffn_sems = refs[9:18]
    ffn_copies = [
        pltpu.make_async_copy(wdown_hbm, wdown_ref, ffn_sems.at[0]), pltpu.make_async_copy(wup_hbm, wup_ref, ffn_sems.at[1]),
    ]
    wc_ref = parts[0]
    if fetch:
        wc_ref, sems = refs[18:]
        copies = fetch_halves(ids_ref, parts, wc_ref, sems)
    for copy in ffn_copies:
        copy.start()
    if fetch:
        for copy in copies:
            copy.wait()
    count, width = rows_ref.shape[0], rows_ref.shape[1] // 2

    def cls(block):
        return cls_ref[:, block * width : (block + 1) * width]

    pairs = width // PAIR
    entries = table_ref.shape[0]
    picks = place_ref[...] == lax.broadcasted_iota(jnp.int32, (count, entries), 1)
    embedded = rows_ref[:, :width] + dot_nn(picks.astype(BF16), table_ref[...])
    low = embedded.astype(BF16)
    for part in range(3):
        proj_ref[:, part * width : (part + 1) * width] = dot_nn(low, square(wc_ref[part])).astype(BF16)
    first_half = lane_half((count, PAIR))
    same = keyc_ref[...] == keyr_ref[...]
    places = [
        [slice(part * width + pair * PAIR, part * width + (pair + 1) * PAIR) for part in range(3)] for pair in range(pairs)
    ]
    for pair, cols in enumerate(places):
        probs, mixed = pair_forward(proj_ref[:, cols[0]], proj_ref[:, cols[1]], proj_ref[:, cols[2]], first_half, same)
        probs_ref[pair] = probs
        mixed_ref[:, cols[0]] = mixed.astype(BF16)
    pre_third = embedded + dot_nn(mixed_ref[...], square(wc_ref[3]))
    unit, inverse = norm_parts(pre_third)
    gain = gains_ref[2:3].astype(F32)
    new_ref[...] = (unit[:local] * gain + shifts_ref[2:3].astype(F32)).astype(BF16)
    grad_out = rows_ref[:, width:]
    grad_third = norm_back(grad_out, unit, inverse, gain)
    sums_ref[...] = jnp.zeros_like(sums_ref)
    sums_ref[2:3] = jnp.sum(grad_out[:local] * unit[:local], axis=0, keepdims=True)
    sums_ref[5:6] = jnp.sum(grad_out[:local], axis=0, keepdims=True)
    gradz = grad_third.astype(BF16)
    gradm_ref[...] = dot_nt(gradz, square(wc_ref[3])).astype(BF16)
    for pair, cols in enumerate(places):
        grads = pair_backward(
            proj_ref[:, cols[0]], proj_ref[:, cols[1]], proj_ref[:, cols[2]], probs_ref[pair], gradm_ref[:, cols[0]], first_half
        )
        for place, grad in zip(cols, grads):
            gradp_ref[:, place] = grad.astype(BF16)
    grad_edge = grad_third[:local]
    for part in range(3):
        grad_edge = grad_edge + dot_nt(gradp_ref[:local, part * width : (part + 1) * width], square(wc_ref[part]))
    rows = grad_c_ref.shape[1]
    own = pl.ds(pl.multiple_of(ids_ref[0] * rows, 8), rows)
    lying_ref[...] = low.astype(F32).T
    own_low = lying_ref[own, :].astype(BF16)
    for part in range(3):
        grad_c_ref[part] = dot_nn(own_low, gradp_ref[:, part * width : (part + 1) * width]).astype(BF16)
    lying_ref[...] = mixed_ref[...].astype(F32).T
    grad_c_ref[3] = dot_nn(lying_ref[own, :].astype(BF16), gradz).astype(BF16)
    unit, inverse = norm_parts(cls(CLS_TOTAL))
    sums_ref[1:2] = jnp.sum(grad_edge * unit, axis=0, keepdims=True)
    sums_ref[4:5] = jnp.sum(grad_edge, axis=0, keepdims=True)
    total = norm_back(grad_edge, unit, inverse, gains_ref[1:2].astype(F32))
    branch = total.astype(BF16)
    branch_ref[...] = branch
    for part in range(4):
        blocks = width // turned_ref.shape[1]
        turned = cls(CLS_ACT + part).T.reshape(blocks, turned_ref.shape[1], local)
        turned_ref[part * blocks : (part + 1) * blocks] = turned.astype(BF16)
    for copy in ffn_copies:
        copy.wait()
    for part in range(4):
        grad_act = dot_nt(branch, down_block(wdown_ref, part))
        grad_hidden = (grad_act * cls(CLS_SLOPE + part)).astype(BF16)
        hidden_ref[:, part * width : (part + 1) * width] = grad_hidden
        total = total + dot_nt(grad_hidden, square(wup_ref[part]))
    unit, inverse = norm_parts(cls(CLS_PRE))
    grad1 = norm_back(total, unit, inverse, gains_ref[0:1].astype(F32))
    grad1_ref[...] = grad1
    low1_ref[...] = grad1.astype(BF16)
    sums_ref[0:1] = jnp.sum(total * unit, axis=0, keepdims=True)
    sums_ref[3:4] = jnp.sum(total, axis=0, keepdims=True)
    table_grad_ref[...] = lax.dot_general(
        picks[:local].astype(F32), grad_edge, (((0,), (0,)), ((), ())),
        precision=lax.Precision.HIGHEST, preferred_element_type=F32,
    )


def cross_block(ids, edges, cls, key_col, key_row, place, table, gains, shifts, w_up, w_down, parts, shape):
    local, count, width = cls.shape[0], edges.shape[0], table.shape[1]
    read = [edges, cls, key_col, key_row, place, table, gains, shifts]
    part_specs, fetched = [whole(part.shape) for part in parts], []
    if shape is not None:
        part_specs = [ANYWHERE] * len(parts)
        fetched = [pltpu.VMEM(shape.shape, BF16), pltpu.SemaphoreType.DMA((4,))]
    shapes = (
        jax.ShapeDtypeStruct((local, width), BF16),
        jax.ShapeDtypeStruct((local, width), BF16),
        jax.ShapeDtypeStruct((4, width // lax.axis_size("seg"), width), BF16),
        jax.ShapeDtypeStruct((8, width), F32),
        jax.ShapeDtypeStruct(table.shape, F32),
        jax.ShapeDtypeStruct((local, 4 * width), BF16),
        jax.ShapeDtypeStruct((local, width), F32),
        jax.ShapeDtypeStruct((local, width), BF16),
        jax.ShapeDtypeStruct((4 * lax.axis_size("seg"), width // lax.axis_size("seg"), local), BF16),
    )
    return pl.pallas_call(
        partial(cross_kernel, local, shape is not None),
        out_shape=shapes,
        grid_spec=pltpu.PrefetchScalarGridSpec(
            num_scalar_prefetch=1,
            grid=(1,),
            in_specs=[whole(value.shape) for value in read] + [ANYWHERE] * 2 + part_specs,
            out_specs=[whole(value.shape) for value in shapes],
            scratch_shapes=[
                pltpu.VMEM((count, 3 * width), BF16),
                pltpu.VMEM((width // PAIR, count, 2 * count), BF16),
                pltpu.VMEM((count, width), BF16),
                pltpu.VMEM((count, width), BF16),
                pltpu.VMEM((count, 3 * width), BF16),
                pltpu.VMEM((width, count), F32),
                pltpu.VMEM(w_up.shape, BF16),
                pltpu.VMEM(w_down.shape, BF16),
                pltpu.SemaphoreType.DMA((2,)),
            ] + fetched,
        ),
        compiler_params=pltpu.CompilerParams(vmem_limit_bytes=56 * MIB),
        cost_estimate=cost(10_000_000_000, width * width * 8),
        name="cross_block",
    )(ids, *read, w_up, w_down, *parts)


def with_cls(left_ref, right_ref, cls_left_ref, cls_right_ref):
    cls_product = dot_tn(cls_left_ref[...].astype(BF16), cls_right_ref[...])
    return (dot_tn(left_ref[...], right_ref[...]) + cls_product).astype(BF16)


def cols_grad_kernel(side, ids_ref, left_ref, right_ref, cls_left_ref, cls_right_ref, rider_ref, *refs):
    out_ref = refs[-1]
    owners, rows = rider_ref.shape[0], left_ref.shape[1] // rider_ref.shape[0]
    block = half_block(side, pl.program_id(0), ids_ref)
    product = with_cls(left_ref, right_ref, cls_left_ref, cls_right_ref)
    out_ref[0, :, :rows] = product.reshape(owners, rows, product.shape[1])
    rider = rider_ref[...]
    out_ref[0, :, rows:] = jnp.where(block == 0, rider, jnp.zeros_like(rider))


def joint_grad_kernel(side, ids_ref, left_ref, last_left_ref, right_ref, last_right_ref, *refs):
    block = half_block(side, pl.program_id(0), ids_ref)

    @pl.when(block < 3)
    def main():
        refs[-1][0] = dot_tn(left_ref[...], right_ref[...]).astype(BF16)

    @pl.when(block == 3)
    def last():
        refs[-1][0] = dot_tn(last_left_ref[...], last_right_ref[...]).astype(BF16)


def half_block(side, step, ids):
    return 2 * ((ids[1] & 1) ^ side) + step


def half_grads(kernel, name, ids, operands, specs, shape, after, weight):
    rows, width = operands[0].shape
    return pl.pallas_call(
        kernel,
        out_shape=jax.ShapeDtypeStruct((2,) + shape, BF16),
        grid_spec=pltpu.PrefetchScalarGridSpec(
            num_scalar_prefetch=1,
            grid=(2,),
            in_specs=specs + [ANYWHERE] * len(after),
            out_specs=pl.BlockSpec((1,) + shape, lambda j, ids: (j,) + (0,) * len(shape)),
        ),
        compiler_params=pltpu.CompilerParams(vmem_limit_bytes=56 * MIB),
        cost_estimate=cost(4 * rows * width * width, 10 * rows * width, weight),
        name=name,
    )(ids, *operands, *after)


def plain_cols_kernel(ids_ref, left_ref, right_ref, cls_left_ref, cls_right_ref, *refs):
    refs[-1][0] = with_cls(left_ref, right_ref, cls_left_ref, cls_right_ref)


def cols_grads(side, ids, left, right, cls_left, cls_right, rider, after, weight):
    rows, width = left.shape
    owners, extra, unused = rider.shape
    specs = [
        whole(left.shape),
        pl.BlockSpec((rows, width), lambda j, ids: (0, half_block(side, j, ids))),
        pl.BlockSpec((cls_left.shape[0], width), lambda j, ids: (0, CLS_LOW), pipeline_mode=pl.Buffered(1)),
        pl.BlockSpec((cls_left.shape[0], width), lambda j, ids: (0, half_block(side, j, ids))),
    ]
    operands = [left, right, cls_left, cls_right]
    if width // owners % 16 == 0:
        return half_grads(
            partial(cols_grad_kernel, side), "cols_grads", ids, operands + [rider], specs + [whole(rider.shape)],
            (owners, width // owners + extra, width), after, weight,
        )
    product = half_grads(plain_cols_kernel, "cols_grads", ids, operands, specs, (width, width), after, weight)
    first = half_block(side, 0, ids) == 0
    rider = jnp.where(first, rider, jnp.zeros_like(rider))
    rider = jnp.stack([rider, jnp.zeros_like(rider)], axis=0)
    return jnp.concatenate([product.reshape(2, owners, width // owners, width), rider], axis=2)


def joint_grads(side, ids, left, last_left, right, last_right, after, weight):
    rows, width = left.shape
    specs = [
        whole(left.shape),
        whole(left.shape),
        pl.BlockSpec((rows, width), lambda j, ids: (0, jnp.minimum(half_block(side, j, ids), 2))),
        whole(left.shape),
    ]
    operands = [left, last_left, right, last_right]
    return half_grads(partial(joint_grad_kernel, side), "joint_grads", ids, operands, specs, (width, width), after, weight)


def rows_grad_kernel(ids_ref, left_ref, right_ref, *refs):
    send_ref, keep_ref, held_ref = refs[-3:]
    core = ids_ref[1] & 1
    held_ref[...] = dot_tn(left_ref[...], right_ref[...]).reshape(held_ref.shape)
    for share in range(2):
        send_ref[share] = held_ref[:, 2 * (1 - core) + share].astype(BF16)
        keep_ref[share] = held_ref[:, 2 * core + share].astype(BF16)


def rows_grads(ids, left, right, count, after):
    rows, width = right.shape
    hidden = left.shape[1]
    shard_rows = hidden // count // 4
    owners = count // 4
    half = jax.ShapeDtypeStruct((2, count, shard_rows, width), BF16)
    out_spec = pl.BlockSpec((2, owners, shard_rows, width), lambda j, ids: (0, j, 0, 0))
    return pl.pallas_call(
        rows_grad_kernel,
        out_shape=(half, half),
        grid_spec=pltpu.PrefetchScalarGridSpec(
            num_scalar_prefetch=1,
            grid=(4,),
            in_specs=[
                pl.BlockSpec((rows, hidden // 4), lambda j, ids: (0, j)),
                pl.BlockSpec((rows, width), lambda j, ids: (0, 0), pipeline_mode=pl.Buffered(1)),
            ] + [ANYWHERE] * len(after),
            out_specs=[out_spec, out_spec],
            scratch_shapes=[pltpu.VMEM((owners, 4, shard_rows, width), F32)],
        ),
        compiler_params=pltpu.CompilerParams(vmem_limit_bytes=56 * MIB),
        cost_estimate=cost(2 * rows * width * hidden, 10 * rows * width),
        name="rows_grads",
    )(ids, left, right, *after)


def later(value, *first):
    return lax.optimization_barrier((value,) + first)[0]


def seg_swap(value, mask):
    count = lax.axis_size("seg")
    return lax.ppermute(value, "seg", [(i, i ^ mask) for i in range(count)])


def rep_swap(value, mask):
    count = lax.axis_size("rep")
    return lax.ppermute(value, "rep", [(i, i ^ mask) for i in range(count)])


def both_swap(value, seg_mask, rep_mask):
    reps = lax.axis_size("rep")
    total = lax.axis_size("seg") * reps
    pairs = [(i, ((i // reps) ^ seg_mask) * reps + ((i % reps) ^ rep_mask)) for i in range(total)]
    return lax.ppermute(value, ("seg", "rep"), pairs)


def place_kernel(count, ids_ref, *refs):
    for copy in fetch_pieces(ids_ref, refs[:count], refs[count], refs[count + 1]):
        copy.wait()


def put_in_place(ids, pieces):
    parts, shape = pieces
    return pl.pallas_call(
        partial(place_kernel, len(parts)),
        out_shape=shape,
        in_specs=[pl.BlockSpec(memory_space=pltpu.SMEM)] + [ANYWHERE] * len(parts),
        out_specs=pl.BlockSpec(memory_space=pltpu.VMEM),
        scratch_shapes=[pltpu.SemaphoreType.DMA((len(parts) * parts[0].shape[0],))],
        compiler_params=pltpu.CompilerParams(vmem_limit_bytes=32 * MIB),
        cost_estimate=cost(0, 4 * shape.size),
        name="put_in_place",
    )(ids, *parts)


def far_pieces(piece):
    return [piece] + [seg_swap(piece, mask) for mask in range(2, lax.axis_size("seg"), 2)]


def after_all(value, first):
    return later(value, *first) if first else value


def gather_shares(piece):
    evens = jnp.stack(far_pieces(piece), axis=0)
    own = [evens, seg_swap(evens, 1)]
    across = [rep_swap(part, 2) for part in own]
    near, far = ([rep_swap(part, 1) for part in parts] for parts in (own, across))
    return own + near + across + far


class Gather:
    def __init__(self, piece):
        self.piece, self.came = piece, far_pieces(piece)

    def across(self, *first):
        self.evens = jnp.stack(self.came[:1] + [later(value, *first) for value in self.came[1:]], axis=0)
        self.came = seg_swap(self.evens, 1)

    def finish(self, *first):
        return jnp.stack([self.evens, later(self.came, *first)], axis=1).reshape((-1,) + self.piece.shape)


def spread_kernel(ids_ref, keep_ref, came_ref, *refs):
    stay_ref, x_ref, y_ref, xy_ref = refs[-4:]
    near, across, core = ids_ref[0] & 1, ids_ref[1] >> 1, ids_ref[1] & 1

    def total(share, side):
        value = keep_ref[share, 0, side].astype(F32) + came_ref[share, 0, side].astype(F32)
        if len(refs) > 4:
            for left_ref, right_ref in (refs[:2], refs[2:4]):
                value = value + dot_nn(left_ref[0, side, 2 * core + share], right_ref[...])
        return value.astype(BF16)

    stay_ref[0] = total(across, near)
    x_ref[0] = total(across, 1 - near)
    y_ref[0] = total(1 - across, near)
    xy_ref[0] = total(1 - across, 1 - near)


def spread(ids, keep, came, product=()):
    unused, count, rows, width = keep.shape
    far = count // 2
    shape = (2, far, 2, rows, width)
    in_spec = pl.BlockSpec((2, 1, 2, rows, width), lambda j: (0, j, 0, 0, 0))
    out_spec = pl.BlockSpec((1, rows, width), lambda j: (j, 0, 0))
    out = jax.ShapeDtypeStruct((far, rows, width), BF16)
    specs = [pl.BlockSpec(memory_space=pltpu.SMEM), in_spec, in_spec]
    if product:
        depth = product[1].shape[0]
        product = [value.reshape(far, 2, 4, rows, depth) if i % 2 == 0 else value for i, value in enumerate(product)]
        specs += [pl.BlockSpec((1, 2, 4, rows, depth), lambda j: (j, 0, 0, 0, 0)), whole(product[1].shape)] * 2
    return pl.pallas_call(
        spread_kernel,
        out_shape=(out,) * 4,
        grid=(far,),
        in_specs=specs,
        out_specs=[out_spec] * 4,
        compiler_params=pltpu.CompilerParams(vmem_limit_bytes=58 * MIB),
        cost_estimate=cost(0, 12 * count * rows * width),
        name="spread",
    )(ids, keep.reshape(shape), came.reshape(shape), *product)


def settle_kernel(ids_ref, *refs):
    far = refs[0].shape[0]
    parts, outs = refs[:-far], refs[-far:]
    start = 0
    for first in range(0, len(parts), 4):
        rows = parts[first].shape[1]
        for mask, out in enumerate(outs):
            a, b, c, d = (part[(ids_ref[0] >> 1) ^ mask].astype(F32) for part in parts[first : first + 4])
            out[start : start + rows] = ((a + b) + (c + d)).astype(BF16)
        start += rows


def settle(ids, *groups):
    far, unused, width = groups[0][0].shape
    heights = [group[0].shape[1] for group in groups]
    if len(groups) > 1 and any(rows % 16 for rows in heights):
        return [jnp.concatenate(parts, axis=0) for parts in zip(*[settle(ids, group) for group in groups])]
    whole_spec = pl.BlockSpec(memory_space=pltpu.VMEM)
    return pl.pallas_call(
        settle_kernel,
        out_shape=(jax.ShapeDtypeStruct((sum(heights), width), BF16),) * far,
        in_specs=[pl.BlockSpec(memory_space=pltpu.SMEM)] + [whole_spec] * (4 * len(groups)),
        out_specs=[whole_spec] * far,
        compiler_params=pltpu.CompilerParams(vmem_limit_bytes=58 * MIB),
        cost_estimate=cost(0, 10 * far * sum(heights) * width),
        name="settle",
    )(ids, *[part for group in groups for part in group])


def halve(value, axis, bit):
    own = lax.dynamic_index_in_dim(value, bit, axis, keepdims=False)
    other = lax.dynamic_index_in_dim(value, 1 - bit, axis, keepdims=False)
    return own, other


class Reduction:
    def __init__(self, ids, send, keep):
        count = lax.axis_size("seg")
        self.ids = ids
        self.shape = (2, count, send.size // (2 * count * send.shape[-1]), send.shape[-1])
        self.keep = keep
        self.came = rep_swap(send, 1)

    def spread(self, *first, product=()):
        came = after_all(self.came, first)
        self.stay, *sends = spread(self.ids, self.keep.reshape(self.shape), came.reshape(self.shape), product)
        self.came = [seg_swap(sends[0], 1), rep_swap(sends[1], 2), both_swap(sends[2], 1, 2)]

    def parts(self, *first):
        return [self.stay] + [after_all(value, first) for value in self.came]


def swap_far(others):
    return [seg_swap(other, 2 * mask) for mask, other in enumerate(others, 1)]


def add_up(own, came, *first):
    total = own.astype(F32)
    for value in came:
        total = total + after_all(value, first).astype(F32)
    return total.astype(BF16)


class Sharing:
    def __init__(self, ids, value):
        self.ids, self.value = ids, value
        self.came = rep_swap(value, 2)

    def step(self, *first):
        self.value = jnp.stack([self.value, later(self.came, *first)], axis=0)
        self.came = rep_swap(self.value, 1)

    def finish(self, *first):
        held = jnp.concatenate([self.value, later(self.came, *first)], axis=0)
        places = [self.ids[1] ^ owner for owner in (0, 2, 1, 3)]
        return [
            lax.dynamic_index_in_dim(held, 2 * (place & 1) + place // 2, 0, keepdims=False).astype(F32) for place in places
        ]


def body(tokens, cotangent, doc_counts, w_qkv, w_out, w_up, w_down, c_qkv, c_out, pos_table, norm_gains, norm_shifts):
    micro_count, unused, seg_local, seg_length, width = tokens.shape
    count = lax.axis_size("seg")
    me = lax.axis_index("seg").astype(jnp.int32)
    rep = lax.axis_index("rep").astype(jnp.int32)
    ids = jnp.stack([me, rep])
    shard_rows = w_qkv.shape[0]
    local = micro_count * seg_local
    rows = local * seg_length
    table_rows = pos_table.shape[0]
    norm_cols = norm_gains.shape[1]
    aligned = shard_rows % 16 == 0

    def half_columns(matrix):
        half = lax.dynamic_slice_in_dim(matrix, 2 * width * (rep & 1), 2 * width, 1)
        return jnp.stack([half[:, :width], half[:, width:]], axis=0)

    def half_of(wide, narrow):
        first = jnp.stack([wide[:, :width], wide[:, width : 2 * width]], axis=0)
        second = jnp.stack([wide[:, 2 * width :], narrow], axis=0)
        return jnp.where((rep & 1) == 0, first, second)

    norms = jnp.pad(jnp.concatenate([norm_gains, norm_shifts], axis=0), ((0, 2), (0, width - norm_cols)))
    small = jnp.stack([jnp.pad(pos_table, ((0, 8 - table_rows), (0, 0))), norms], axis=0)
    own_down = lax.dynamic_slice_in_dim(w_down, 2 * shard_rows * (rep & 1), 2 * shard_rows, 0)
    ffn_piece = jnp.concatenate([half_columns(w_up), own_down.reshape(2, shard_rows, width), small], axis=1)
    ffn_half = lax.all_gather(ffn_piece, "seg", axis=0)
    qo_piece = lax.dynamic_slice_in_dim(w_qkv, jnp.minimum(rep, 2) * width, width, 1)
    qo_piece = jnp.where(rep == 3, w_out, qo_piece)
    shapes = [shape_of((4, count, shard_rows, width), BF16), shape_of((count, 4, shard_rows, width), BF16)]
    qo_shares = gather_shares(qo_piece)
    qo_pieces = (qo_shares, shapes[0])
    cross_piece = half_of(c_qkv, c_out)
    cross_half = lax.all_gather(later(cross_piece, qo_shares[0]), "seg", axis=0)

    counts = doc_counts[:, 0]
    ends = jnp.cumsum(counts, axis=1)
    owners = me ^ jnp.arange(count, dtype=jnp.int32)
    seg_ids = owners[:, None, None] * seg_local + jnp.arange(seg_local, dtype=jnp.int32)[None, None, :]
    seg_ids = jnp.broadcast_to(seg_ids, (count, micro_count, seg_local))
    past = seg_ids[..., None] >= ends[None, :, None, :]
    doc_ids = jnp.sum(past.astype(jnp.int32), axis=-1)
    starts = jnp.sum(jnp.where(past, counts[None, :, None, :], 0), axis=-1)
    places = (seg_ids - starts).reshape(-1, 1)
    keys = (doc_ids + (counts.shape[1] + 1) * jnp.arange(micro_count, dtype=jnp.int32)[None, :, None]).reshape(-1)

    flat = tokens.reshape(rows, width)
    cot = cotangent.reshape(rows, width)
    block = 4 * seg_length
    steps = rows // block
    halves_of = ((0, steps // 2), (steps // 2, steps - steps // 2))

    everything = (0, steps)
    if aligned:
        proj, probs, mixed, pre_first, full_qo = attention_forward(
            flat, None, seg_length, block, everything, after=[keys, places], pieces=qo_pieces, ids=ids
        )
    else:
        full_qo = put_in_place(ids, qo_pieces).reshape(4, 1, width, width)
        proj, probs, mixed, pre_first = attention_forward(flat, full_qo, seg_length, block, everything)
    ffn_half = later(ffn_half, proj)
    small = ffn_half[:, :, 2 * shard_rows :]
    table = small[:, 0, :table_rows].reshape(count * table_rows, width)
    norms = small[:, 1, :6, :norm_cols].transpose(1, 0, 2).reshape(6, width)
    gains, shifts = norms[:3], norms[3:]
    ffn_other = rep_swap(ffn_half, 1)

    def joined(parts, start, owner_first):
        own, other = [part[:, :, start : start + shard_rows] for part in parts]
        both = jnp.where((rep & 1) == 0, jnp.concatenate([own, other], axis=1), jnp.concatenate([other, own], axis=1))
        return (both if owner_first else both.transpose(1, 0, 2, 3)).reshape(4, 1, width, width)

    small_block = 2 * seg_length
    if aligned:
        low, act, slope, out, branch, grad2, sums2, cls, full_up, full_down = ffn_forward(
            pre_first, cot, None, gains, shifts, seg_length, small_block, ([ffn_half, ffn_other], shapes), ids
        )
    else:
        full_up = joined([ffn_half, ffn_other], 0, False)
        full_down = joined([ffn_half, ffn_other], shard_rows, True)
        low, act, slope, out, branch, grad2, sums2, cls = ffn_forward(
            pre_first, cot, [full_up, full_down], gains, shifts, seg_length, small_block
        )

    def with_edge(values, edge):
        whole_rows = values.reshape(local, seg_length, values.shape[1])
        return lax.dynamic_update_slice(whole_rows, edge[:, None], (0, 0, 0)).reshape(values.shape)

    edges = Gather(cls[:, CLS_OUT * width : (CLS_COT + 1) * width])
    send_down, keep_down = rows_grads(ids, act, branch, count, [edges.piece])
    down = Reduction(ids, send_down, keep_down)
    edges.across(send_down)
    cross_half = later(cross_half, send_down)
    cross_other = rep_swap(cross_half, 1)
    *kept, sums1a = ffn_backward(
        branch, grad2, pre_first, slope, full_up, full_down, gains, small_block, (0, steps), LONG, after=[edges.evens, cross_half]
    )
    edges = edges.finish(kept[0]).reshape(-1, 2 * width)
    cross_parts, cross_shape = [cross_half, later(cross_other, kept[0])], shapes[0]
    if not aligned:
        cross_parts, cross_shape = [joined(cross_parts, 0, False)], None
    cls_new, cls_branch, grad_c, c_sums, table_grad, *cls_back = cross_block(
        ids, edges, cls, keys[:, None], jnp.concatenate([keys, keys])[None, :], places, table, gains, shifts, full_up,
        full_down, cross_parts, cross_shape,
    )
    cls_hidden, cls_grad1, cls_low1, cls_turned = cls_back
    operands = [cls_turned, cls_branch]
    c_own, c_other = halve(grad_c.reshape(2, 2, shard_rows, width), 0, rep & 1)
    c_came = rep_swap(c_other, 1)
    down.spread(kept[0], product=operands + [rep_swap(value, 1) for value in operands])
    grad_hidden, grad1, low1, sums1b = ffn_backward(
        branch, grad2, pre_first, slope, full_up, full_down, gains, small_block, (steps, steps), SHORT, prior=kept, after=[down.stay]
    )
    low1 = with_edge(low1, cls_low1)
    norm_sums = (sums2 + sums1a + sums1b + c_sums).reshape(8, count, norm_cols).transpose(1, 0, 2)
    norm_sums = jnp.pad(norm_sums, ((0, 0), (0, 0), (0, width - norm_cols)))
    rider = jnp.concatenate([norm_sums, table_grad.reshape(count, table_rows, width)], axis=1).astype(BF16)
    send_up = cols_grads(1, ids, low, grad_hidden, cls, cls_hidden, rider, [], SHORT)
    own_down, *others = settle(ids, down.parts(send_up))
    came_down = swap_far(others)
    keep_up = cols_grads(0, ids, low, grad_hidden, cls, cls_hidden, rider, [send_up, own_down], LONG)
    up = Reduction(ids, send_up, keep_up)
    up.spread(keep_up, *came_down[:1])
    grad_proj = attention_backward(low1, proj, probs, full_qo, seg_length, block, after=[up.stay])
    down_share = add_up(own_down, came_down, grad_proj)
    c_own, c_other = halve(c_own.astype(F32) + later(c_came, grad_proj).astype(F32), 0, rep >> 1)
    c_came = rep_swap(c_other.astype(BF16), 2)
    send_qo = joint_grads(1, ids, flat, mixed, grad_proj, low1, [], SHORT)
    own_up, *others = settle(ids, up.parts(send_qo))
    came_up = swap_far(others)
    keep_qo = joint_grads(0, ids, flat, mixed, grad_proj, low1, [send_qo, own_up], LONG)
    qo = Reduction(ids, send_qo, keep_qo)
    qo.spread(keep_qo, *came_up[:2])
    input_grad = input_gradient(with_edge(later(grad1, qo.stay), cls_grad1), grad_proj, full_qo, block, [qo.stay])
    own, *others = settle(ids, qo.parts(input_grad))
    came = swap_far(others)
    c_share = (c_own + later(c_came, own).astype(F32)).astype(BF16)
    early = Sharing(ids, jnp.concatenate([down_share, add_up(own_up, came_up, own), c_share], axis=0))
    late = Sharing(ids, add_up(own, came))
    early.step(late.value)
    layer_out = with_edge(later(out, late.value), cls_new)
    early_shares = early.finish(layer_out)
    starts = (0, shard_rows, 2 * shard_rows, 2 * shard_rows + 16, 3 * shard_rows + 16)
    down_parts, up_parts, riders, c_parts = [
        [part[first:last] for part in early_shares] for first, last in zip(starts, starts[1:])
    ]
    done = [
        jnp.concatenate(up_parts, axis=1),
        jnp.concatenate(down_parts, axis=0),
        jnp.concatenate(c_parts[:3], axis=1),
        c_parts[3],
    ]
    summed = riders[0]
    late.step(layer_out, *done)
    qo_parts = late.finish()

    return (
        layer_out.reshape(tokens.shape),
        input_grad.reshape(tokens.shape),
        jnp.concatenate(qo_parts[:3], axis=1),
        qo_parts[3],
        *done,
        summed[8 : 8 + table_rows],
        summed[:3, :norm_cols],
        summed[3:6, :norm_cols],
    )


def solution(mesh):
    rows = P(None, "rep", "seg", None, None)
    split = P("seg", None)
    last = P(None, "seg")
    return jax.shard_map(
        body,
        mesh=mesh,
        in_specs=(rows, rows, P(None, "rep", None)) + (split,) * 7 + (last, last),
        out_specs=(rows, rows) + (split,) * 7 + (last, last),
        check_vma=False,
    )
```

```python
from functools import partial
import jax
import jax.numpy as jnp
from jax import lax
from jax.experimental import pallas as pl
from jax.experimental.pallas import tpu as pltpu
from jax.sharding import PartitionSpec as P

HEAD_DIM = 64
PAIR = 2 * HEAD_DIM
EPSILON = 1e-05
NEGATIVE = -1e30
F32 = jnp.float32
BF16 = jnp.bfloat16
MIB = 1 << 20
LONG, SHORT = 6.0, 0.001
CLS_ACT, CLS_SLOPE, CLS_LOW, CLS_PRE, CLS_TOTAL, CLS_OUT, CLS_COT, CLS_BLOCKS = 0, 4, 8, 9, 10, 11, 12, 13


def dot_nn(left, right):
    return lax.dot_general(left, right, (((1,), (0,)), ((), ())), preferred_element_type=F32)


def dot_nt(left, right):
    return lax.dot_general(left, right, (((1,), (1,)), ((), ())), preferred_element_type=F32)


def dot_tn(left, right):
    return lax.dot_general(left, right, (((0,), (0,)), ((), ())), preferred_element_type=F32)


def norm_parts(values):
    center = values - jnp.mean(values, axis=-1, keepdims=True)
    spread = jnp.mean(center * center, axis=-1, keepdims=True)
    inverse = lax.rsqrt(spread + EPSILON)
    return center * inverse, inverse


def norm_back(grad, unit, inverse, gain):
    scaled = grad * gain
    first = jnp.mean(scaled, axis=-1, keepdims=True)
    second = jnp.mean(scaled * unit, axis=-1, keepdims=True)
    return inverse * (scaled - first - unit * second)


def gelu_parts(hidden):
    phi = 0.5 + 0.5 * lax.erf(hidden * 0.5 ** 0.5)
    bell = jnp.exp(hidden * hidden * -0.5) * 0.3989422804014327
    return hidden * phi, phi + hidden * bell


def halves(pair, first_half):
    zero = jnp.zeros_like(pair)
    return jnp.concatenate([jnp.where(first_half, pair, zero), jnp.where(first_half, zero, pair)], axis=0)


def pairs_forward(queries, keys, values, first_half, same=None):
    rows = queries[0].shape[0]
    scale = BF16(HEAD_DIM ** -0.5)
    scores = [dot_nt(key, halves(query * scale, first_half)) for query, key in zip(queries, keys)]
    if same is not None:
        scores = [jnp.where(same, score, NEGATIVE) for score in scores]
    raised = [jnp.exp(score - jnp.max(score, axis=0, keepdims=True)) for score in scores]
    probs = [(value * (1.0 / jnp.sum(value, axis=0, keepdims=True))).astype(BF16) for value in raised]
    both = [dot_tn(prob, value) for prob, value in zip(probs, values)]
    return probs, [jnp.where(first_half, value[:rows], value[rows:]) for value in both]


def pairs_backward(queries, keys, values, probs, grads_mixed, first_half):
    rows = queries[0].shape[0]
    scale = BF16(HEAD_DIM ** -0.5)
    grads_both = [halves(grad, first_half) for grad in grads_mixed]
    grads_probs = [dot_nt(value, grad) for value, grad in zip(values, grads_both)]
    grads_value = [dot_nn(prob, grad) for prob, grad in zip(probs, grads_both)]
    grads_scores = []
    for prob, grad in zip(probs, grads_probs):
        wide = prob.astype(F32)
        product = wide * grad
        grads_scores.append((product - wide * jnp.sum(product, axis=0, keepdims=True)).astype(BF16))
    grads_key = [dot_nn(grad, halves(query * scale, first_half)) for grad, query in zip(grads_scores, queries)]
    both = [dot_tn(grad, key) for grad, key in zip(grads_scores, keys)]
    grads_query = [jnp.where(first_half, value[:rows], value[rows:]) * (HEAD_DIM ** -0.5) for value in both]
    return grads_query, grads_key, grads_value


def pair_columns(width):
    starts = range(0, width, PAIR)
    return [[slice(part * width + start, part * width + start + PAIR) for start in starts] for part in range(3)]


def lane_half(shape):
    return lax.broadcasted_iota(jnp.int32, shape, 1) % PAIR < HEAD_DIM


def square(value):
    return value.reshape(-1, value.shape[-1])


def up_block(ref, part):
    return square(ref[:, part])


def down_block(ref, part):
    count = ref.shape[0] // 4
    return square(ref[part * count : (part + 1) * count])


def whole(shape):
    return pl.BlockSpec(shape, lambda *at: (0,) * len(shape), pipeline_mode=pl.Buffered(1))


ANYWHERE = pl.BlockSpec(memory_space=pl.ANY)


def cost(flops, moved, weight=1.0):
    return pl.CostEstimate(flops=int(flops * weight), bytes_accessed=int(moved * weight), transcendentals=0)


def rows_call(kernel, name, block, span, rowed, fixed, outs, flops, prior=(), after=(), extra=(), ids=None, scratch=(), weight=1.0):
    first, steps = span

    def cut(value):
        array, ratio = value if isinstance(value, tuple) else (value, 1)
        shape = (block // ratio,) + array.shape[1:]
        return array, pl.BlockSpec(shape, lambda i, *ids: (i + first,) + (0,) * (len(shape) - 1))

    ins = [cut(value) for value in rowed] + list(fixed)
    results = [cut(value) for value in outs] + [(shape, whole(shape.shape)) for shape in extra]
    unread = list(prior) + list(after)
    lead = 0 if ids is None else 1
    moved = sum(value.size * value.dtype.itemsize for value, unused in ins + results) // 2

    def run(*refs):
        start = lead + len(ins)
        kernel(*refs[:start], *refs[start + len(unread) :])

    return pl.pallas_call(
        run,
        out_shape=tuple(jax.ShapeDtypeStruct(shape.shape, shape.dtype) for shape, unused in results),
        grid_spec=pltpu.PrefetchScalarGridSpec(
            num_scalar_prefetch=lead,
            grid=(steps,),
            in_specs=[spec for unused, spec in ins] + [ANYWHERE] * len(unread),
            out_specs=[spec for unused, spec in results],
            scratch_shapes=list(scratch),
        ),
        input_output_aliases={lead + len(ins) + i: i for i in range(len(prior))},
        compiler_params=pltpu.CompilerParams(vmem_limit_bytes=58 * MIB),
        cost_estimate=cost(2 * flops * steps * block, moved, weight),
        name=name,
    )(*([] if ids is None else [ids]), *[array for array, unused in ins], *unread)


def shape_of(shape, dtype):
    return jax.ShapeDtypeStruct(shape, dtype)


def fetch_pieces(ids_ref, parts, out_ref, sems):
    me, rep = ids_ref[0], ids_ref[1]
    copies = []
    for number, part in enumerate(parts):
        for slot in range(part.shape[0]):
            target = out_ref.at[rep ^ (number // 2), me ^ (2 * slot + number % 2)]
            copies.append(pltpu.make_async_copy(part.at[slot], target, sems.at[number * part.shape[0] + slot]))
    for copy in copies:
        copy.start()
    return copies


def fetch_halves(ids_ref, parts, out_ref, sems, start=0, owner_first=False):
    core = ids_ref[1] & 1
    rows = out_ref.shape[2]
    base = 4 if owner_first else 0
    copies = []
    for side, part in enumerate(parts):
        owner_core = core if side == 0 else 1 - core
        for share in range(2):
            piece = part.at[:, share] if part.shape[-2] == rows else part.at[:, share, pl.ds(start, rows)]
            block = 2 * owner_core + share
            target = out_ref.at[:, block] if owner_first else out_ref.at[block]
            copies.append(pltpu.make_async_copy(piece, target, sems.at[base + 2 * side + share]))
    for copy in copies:
        copy.start()
    return copies


def attention_rows(seg_length, x_ref, wqo_ref, proj_ref, probs_ref, mixed_ref, pre_ref):
    rows, width = x_ref.shape
    pairs = width // PAIR
    for part in range(3):
        proj_ref[:, part * width : (part + 1) * width] = dot_nn(x_ref[...], square(wqo_ref[part])).astype(BF16)
    first_half = lane_half((seg_length, PAIR))
    columns = pair_columns(width)
    for seg in range(rows // seg_length):
        span = slice(seg * seg_length, (seg + 1) * seg_length)
        probs, mixed = pairs_forward(*[[proj_ref[span, cols] for cols in part] for part in columns], first_half)
        for pair in range(pairs):
            probs_ref[seg, pair] = probs[pair]
            mixed_ref[span, columns[0][pair]] = mixed[pair].astype(BF16)
    pre_ref[...] = x_ref[...].astype(F32) + dot_nn(mixed_ref[...], square(wqo_ref[3]))


def attention_first_kernel(seg_length, count, ids_ref, x_ref, *refs):
    parts, (proj_ref, probs_ref, mixed_ref, pre_ref, wqo_ref, sems) = refs[:count], refs[count:]

    @pl.when(pl.program_id(0) == 0)
    def fetch():
        for copy in fetch_pieces(ids_ref, parts, wqo_ref, sems):
            copy.wait()

    attention_rows(seg_length, x_ref, wqo_ref, proj_ref, probs_ref, mixed_ref, pre_ref)


def attention_shapes(rows, width, seg_length):
    probs = shape_of((rows // seg_length, width // PAIR, seg_length, 2 * seg_length), BF16)
    return [
        shape_of((rows, 3 * width), BF16), (probs, seg_length), shape_of((rows, width), BF16), shape_of((rows, width), F32),
    ]


def attention_forward(rows_in, weight, seg_length, block, span, prior=(), after=(), pieces=None, ids=None):
    rows, width = rows_in.shape
    outs = attention_shapes(rows, width, seg_length)
    flops = width * (4 * width + 8 * seg_length)
    if pieces is None:
        return rows_call(
            partial(attention_rows, seg_length), "attention_forward", block, span, [rows_in],
            [(weight, whole(weight.shape))], outs, flops, prior, after, weight=SHORT,
        )
    parts, shape = pieces
    return rows_call(
        partial(attention_first_kernel, seg_length, len(parts)), "attention_forward", block, span, [rows_in],
        [(part, ANYWHERE) for part in parts], outs, flops, prior, after, [shape], ids,
        [pltpu.SemaphoreType.DMA((len(parts) * parts[0].shape[0],))], SHORT,
    )


def ffn_rows(
    seg_length, pre_ref, cot_ref, wup_ref, wdown_ref, gains_ref, shifts_ref,
    low_ref, act_ref, slope_ref, out_ref, branch_ref, grad_ref, sums_ref, cls_ref,
):
    rows, width = pre_ref.shape
    segs = rows // seg_length

    def keep_cls(block, values):
        for seg in range(segs):
            row = values[seg * seg_length : seg * seg_length + 1].astype(F32)
            cls_ref[pl.ds(pl.program_id(0) * segs + seg, 1), block * width : (block + 1) * width] = row

    unit, unused = norm_parts(pre_ref[...])
    total = unit * gains_ref[0:1].astype(F32) + shifts_ref[0:1].astype(F32)
    low = total.astype(BF16)
    low_ref[...] = low
    held = dot_nn(low, square(wup_ref[0]))
    for part in range(4):
        cols = slice(part * width, (part + 1) * width)
        ahead = dot_nn(low, square(wup_ref[part + 1])) if part < 3 else None
        act, slope = gelu_parts(held)
        act, slope = act.astype(BF16), slope.astype(BF16)
        act_ref[:, cols] = act
        slope_ref[:, cols] = slope
        keep_cls(CLS_ACT + part, act)
        keep_cls(CLS_SLOPE + part, slope)
        total = total + dot_nn(act_ref[:, cols], down_block(wdown_ref, part))
        held = ahead
    gain = gains_ref[1:2].astype(F32)
    unit, inverse = norm_parts(total)
    out = unit * gain + shifts_ref[1:2].astype(F32)
    out_ref[...] = out.astype(BF16)
    keep_cls(CLS_LOW, low)
    keep_cls(CLS_PRE, pre_ref)
    keep_cls(CLS_TOTAL, total)
    keep_cls(CLS_OUT, out)
    keep_cls(CLS_COT, cot_ref)
    is_cls = lax.broadcasted_iota(jnp.int32, total.shape, 0) % seg_length == 0
    grad = jnp.where(is_cls, 0.0, cot_ref[...].astype(F32))
    pre_grad = norm_back(grad, unit, inverse, gain)
    grad_ref[...] = pre_grad
    branch_ref[...] = pre_grad.astype(BF16)

    @pl.when(pl.program_id(0) == 0)
    def start_sums():
        sums_ref[...] = jnp.zeros_like(sums_ref)

    sums_ref[1:2] += jnp.sum(grad * unit, axis=0, keepdims=True)
    sums_ref[4:5] += jnp.sum(grad, axis=0, keepdims=True)


def ffn_first_kernel(seg_length, ids_ref, pre_ref, cot_ref, gains_ref, shifts_ref, half_ref, other_ref, *refs):
    *outs, wup_ref, wdown_ref, sems = refs

    @pl.when(pl.program_id(0) == 0)
    def fetch():
        parts = (half_ref, other_ref)
        up = fetch_halves(ids_ref, parts, wup_ref, sems)
        down = fetch_halves(ids_ref, parts, wdown_ref, sems, wup_ref.shape[2], True)
        for copy in up + down:
            copy.wait()

    ffn_rows(seg_length, pre_ref, cot_ref, wup_ref, wdown_ref, gains_ref, shifts_ref, *outs)


def ffn_forward(pre_first, cot, weights, gains, shifts, seg_length, block, pieces=None, ids=None):
    rows, width = pre_first.shape
    span = (0, rows // block)
    wide, low = shape_of((rows, 4 * width), BF16), shape_of((rows, width), BF16)
    outs = [low, wide, wide, low, low, shape_of((rows, width), F32)]
    extra = [shape_of((8, width), F32), shape_of((rows // seg_length, CLS_BLOCKS * width), F32)]
    if pieces is None:
        return rows_call(
            partial(ffn_rows, seg_length), "ffn_forward", block, span, [pre_first, cot],
            [(value, whole(value.shape)) for value in (*weights, gains, shifts)], outs, 8 * width * width, extra=extra,
        )
    parts, shapes = pieces
    return rows_call(
        partial(ffn_first_kernel, seg_length), "ffn_forward", block, span, [pre_first, cot],
        [(gains, whole(gains.shape)), (shifts, whole(shifts.shape))] + [(part, ANYWHERE) for part in parts], outs,
        8 * width * width, extra=extra + shapes, ids=ids, scratch=[pltpu.SemaphoreType.DMA((8,))],
    )


def ffn_back_rows(branch_ref, grad2_ref, pre1_ref, slope_ref, wup_ref, wdown_ref, gains_ref, gradh_ref, grad1_ref, low1_ref, sums_ref):
    width = branch_ref.shape[1]
    total = grad2_ref[...]
    for part in range(4):
        cols = slice(part * width, (part + 1) * width)
        grad_act = dot_nt(branch_ref[...], down_block(wdown_ref, part))
        grad_hidden = (grad_act * slope_ref[:, cols].astype(F32)).astype(BF16)
        gradh_ref[:, cols] = grad_hidden
        total = total + dot_nt(grad_hidden, square(wup_ref[part]))
    unit, inverse = norm_parts(pre1_ref[...])
    grad1 = norm_back(total, unit, inverse, gains_ref[0:1].astype(F32))
    grad1_ref[...] = grad1
    low1_ref[...] = grad1.astype(BF16)

    @pl.when(pl.program_id(0) == 0)
    def start_sums():
        sums_ref[...] = jnp.zeros_like(sums_ref)

    sums_ref[0:1] += jnp.sum(total * unit, axis=0, keepdims=True)
    sums_ref[3:4] += jnp.sum(total, axis=0, keepdims=True)


def ffn_backward(branch, grad2, pre_first, slope, w_up, w_down, gains, block, span, weight, prior=(), after=()):
    rows, width = branch.shape
    return rows_call(
        ffn_back_rows, "ffn_backward", block, span, [branch, grad2, pre_first, slope],
        [(w_up, whole(w_up.shape)), (w_down, whole(w_down.shape)), (gains, whole(gains.shape))],
        [shape_of((rows, 4 * width), BF16), shape_of((rows, width), F32), shape_of((rows, width), BF16)],
        8 * width * width, prior, after, [shape_of((8, width), F32)], weight=weight,
    )


def attention_back_rows(seg_length, low1_ref, proj_ref, probs_ref, wqo_ref, gradp_ref, gradm_ref):
    rows, width = low1_ref.shape
    pairs = width // PAIR
    gradm_ref[...] = dot_nt(low1_ref[...], square(wqo_ref[3])).astype(BF16)
    first_half = lane_half((seg_length, PAIR))
    columns = pair_columns(width)
    for seg in range(rows // seg_length):
        span = slice(seg * seg_length, (seg + 1) * seg_length)
        grads = pairs_backward(
            *[[proj_ref[span, cols] for cols in part] for part in columns], [probs_ref[seg, pair] for pair in range(pairs)],
            [gradm_ref[span, cols] for cols in columns[0]], first_half,
        )
        for part, parts in zip(columns, grads):
            for cols, grad in zip(part, parts):
                gradp_ref[span, cols] = grad.astype(BF16)


def attention_backward(low1, proj, probs, w_qo, seg_length, block, after=()):
    rows, width = low1.shape
    return rows_call(
        partial(attention_back_rows, seg_length), "attention_backward", block, (0, rows // block),
        [low1, proj, (probs, seg_length)], [(w_qo, whole(w_qo.shape))],
        [shape_of((rows, 3 * width), BF16)],
        width * (width + 16 * seg_length), (), after, scratch=[pltpu.VMEM((block, width), BF16)], weight=SHORT,
    )[0]


def input_rows(grad1_ref, gradp_ref, wqo_ref, input_ref):
    width = grad1_ref.shape[1]
    total = grad1_ref[...]
    for part in range(3):
        total = total + dot_nt(gradp_ref[:, part * width : (part + 1) * width], square(wqo_ref[part]))
    input_ref[...] = total


def input_gradient(grad1, gradp, w_qo, block, after):
    rows, width = grad1.shape
    return rows_call(
        input_rows, "input_gradient", block, (0, rows // block), [grad1, gradp], [(w_qo, whole(w_qo.shape))],
        [shape_of((rows, width), F32)], 3 * width * width, (), after, weight=LONG,
    )[0]


def cross_kernel(
    local, fetch, ids_ref, rows_ref, cls_ref, keyc_ref, keyr_ref, place_ref, table_ref, gains_ref, shifts_ref,
    wup_hbm, wdown_hbm, *refs
):
    parts, refs = (refs[:2], refs[2:]) if fetch else (refs[:1], refs[1:])
    new_ref, branch_ref, grad_c_ref, sums_ref, table_grad_ref, hidden_ref, grad1_ref, low1_ref, turned_ref = refs[:9]
    proj_ref, probs_ref, gradm_ref, mixed_ref, gradp_ref, lying_ref, wup_ref, wdown_ref, ffn_sems = refs[9:18]
    ffn_copies = [
        pltpu.make_async_copy(wdown_hbm, wdown_ref, ffn_sems.at[0]), pltpu.make_async_copy(wup_hbm, wup_ref, ffn_sems.at[1]),
    ]
    wc_ref = parts[0]
    if fetch:
        wc_ref, sems = refs[18:]
        copies = fetch_halves(ids_ref, parts, wc_ref, sems)
    for copy in ffn_copies:
        copy.start()
    if fetch:
        for copy in copies:
            copy.wait()
    count, width = rows_ref.shape[0], rows_ref.shape[1] // 2

    def cls(block):
        return cls_ref[:, block * width : (block + 1) * width]

    pairs = width // PAIR
    entries = table_ref.shape[0]
    picks = place_ref[...] == lax.broadcasted_iota(jnp.int32, (count, entries), 1)
    embedded = rows_ref[:, :width] + dot_nn(picks.astype(BF16), table_ref[...])
    low = embedded.astype(BF16)
    for part in range(3):
        proj_ref[:, part * width : (part + 1) * width] = dot_nn(low, square(wc_ref[part])).astype(BF16)
    first_half = lane_half((count, PAIR))
    same = keyc_ref[...] == keyr_ref[...]
    columns = pair_columns(width)
    operands = [[proj_ref[:, cols] for cols in part] for part in columns]
    probs, mixed = pairs_forward(*operands, first_half, same)
    for pair, cols in enumerate(columns[0]):
        probs_ref[pair] = probs[pair]
        mixed_ref[:, cols] = mixed[pair].astype(BF16)
    pre_third = embedded + dot_nn(mixed_ref[...], square(wc_ref[3]))
    unit, inverse = norm_parts(pre_third)
    gain = gains_ref[2:3].astype(F32)
    new_ref[...] = (unit[:local] * gain + shifts_ref[2:3].astype(F32)).astype(BF16)
    grad_out = rows_ref[:, width:]
    grad_third = norm_back(grad_out, unit, inverse, gain)
    sums_ref[...] = jnp.zeros_like(sums_ref)
    sums_ref[2:3] = jnp.sum(grad_out[:local] * unit[:local], axis=0, keepdims=True)
    sums_ref[5:6] = jnp.sum(grad_out[:local], axis=0, keepdims=True)
    gradz = grad_third.astype(BF16)
    gradm_ref[...] = dot_nt(gradz, square(wc_ref[3])).astype(BF16)
    grads = pairs_backward(
        *operands, [probs_ref[pair] for pair in range(pairs)], [gradm_ref[:, cols] for cols in columns[0]], first_half
    )
    for part, parts in zip(columns, grads):
        for cols, grad in zip(part, parts):
            gradp_ref[:, cols] = grad.astype(BF16)
    grad_edge = grad_third[:local]
    for part in range(3):
        grad_edge = grad_edge + dot_nt(gradp_ref[:local, part * width : (part + 1) * width], square(wc_ref[part]))
    rows = grad_c_ref.shape[1]
    own = pl.ds(pl.multiple_of(ids_ref[0] * rows, 8), rows)
    lying_ref[...] = low.astype(F32).T
    own_low = lying_ref[own, :].astype(BF16)
    for part in range(3):
        grad_c_ref[part] = dot_nn(own_low, gradp_ref[:, part * width : (part + 1) * width]).astype(BF16)
    lying_ref[...] = mixed_ref[...].astype(F32).T
    grad_c_ref[3] = dot_nn(lying_ref[own, :].astype(BF16), gradz).astype(BF16)
    unit, inverse = norm_parts(cls(CLS_TOTAL))
    sums_ref[1:2] = jnp.sum(grad_edge * unit, axis=0, keepdims=True)
    sums_ref[4:5] = jnp.sum(grad_edge, axis=0, keepdims=True)
    total = norm_back(grad_edge, unit, inverse, gains_ref[1:2].astype(F32))
    branch = total.astype(BF16)
    branch_ref[...] = branch
    for part in range(4):
        blocks = width // turned_ref.shape[1]
        turned = cls(CLS_ACT + part).T.reshape(blocks, turned_ref.shape[1], local)
        turned_ref[part * blocks : (part + 1) * blocks] = turned.astype(BF16)
    for copy in ffn_copies:
        copy.wait()
    for part in range(4):
        grad_act = dot_nt(branch, down_block(wdown_ref, part))
        grad_hidden = (grad_act * cls(CLS_SLOPE + part)).astype(BF16)
        hidden_ref[:, part * width : (part + 1) * width] = grad_hidden
        total = total + dot_nt(grad_hidden, square(wup_ref[part]))
    unit, inverse = norm_parts(cls(CLS_PRE))
    grad1 = norm_back(total, unit, inverse, gains_ref[0:1].astype(F32))
    grad1_ref[...] = grad1
    low1_ref[...] = grad1.astype(BF16)
    sums_ref[0:1] = jnp.sum(total * unit, axis=0, keepdims=True)
    sums_ref[3:4] = jnp.sum(total, axis=0, keepdims=True)
    table_grad_ref[...] = lax.dot_general(
        picks[:local].astype(F32), grad_edge, (((0,), (0,)), ((), ())),
        precision=lax.Precision.HIGHEST, preferred_element_type=F32,
    )


def cross_block(ids, edges, cls, key_col, key_row, place, table, gains, shifts, w_up, w_down, parts, shape):
    local, count, width = cls.shape[0], edges.shape[0], table.shape[1]
    read = [edges, cls, key_col, key_row, place, table, gains, shifts]
    part_specs, fetched = [whole(part.shape) for part in parts], []
    if shape is not None:
        part_specs = [ANYWHERE] * len(parts)
        fetched = [pltpu.VMEM(shape.shape, BF16), pltpu.SemaphoreType.DMA((4,))]
    shapes = (
        jax.ShapeDtypeStruct((local, width), BF16),
        jax.ShapeDtypeStruct((local, width), BF16),
        jax.ShapeDtypeStruct((4, width // lax.axis_size("seg"), width), BF16),
        jax.ShapeDtypeStruct((8, width), F32),
        jax.ShapeDtypeStruct(table.shape, F32),
        jax.ShapeDtypeStruct((local, 4 * width), BF16),
        jax.ShapeDtypeStruct((local, width), F32),
        jax.ShapeDtypeStruct((local, width), BF16),
        jax.ShapeDtypeStruct((4 * lax.axis_size("seg"), width // lax.axis_size("seg"), local), BF16),
    )
    return pl.pallas_call(
        partial(cross_kernel, local, shape is not None),
        out_shape=shapes,
        grid_spec=pltpu.PrefetchScalarGridSpec(
            num_scalar_prefetch=1,
            grid=(1,),
            in_specs=[whole(value.shape) for value in read] + [ANYWHERE] * 2 + part_specs,
            out_specs=[whole(value.shape) for value in shapes],
            scratch_shapes=[
                pltpu.VMEM((count, 3 * width), BF16),
                pltpu.VMEM((width // PAIR, count, 2 * count), BF16),
                pltpu.VMEM((count, width), BF16),
                pltpu.VMEM((count, width), BF16),
                pltpu.VMEM((count, 3 * width), BF16),
                pltpu.VMEM((width, count), F32),
                pltpu.VMEM(w_up.shape, BF16),
                pltpu.VMEM(w_down.shape, BF16),
                pltpu.SemaphoreType.DMA((2,)),
            ] + fetched,
        ),
        compiler_params=pltpu.CompilerParams(vmem_limit_bytes=56 * MIB),
        cost_estimate=cost(10_000_000_000, width * width * 8),
        name="cross_block",
    )(ids, *read, w_up, w_down, *parts)


def with_cls(left_ref, right_ref, cls_left_ref, cls_right_ref):
    cls_product = dot_tn(cls_left_ref[...].astype(BF16), cls_right_ref[...])
    return (dot_tn(left_ref[...], right_ref[...]) + cls_product).astype(BF16)


def cols_grad_kernel(side, ids_ref, left_ref, right_ref, cls_left_ref, cls_right_ref, rider_ref, *refs):
    out_ref = refs[-1]
    owners, rows = rider_ref.shape[0], left_ref.shape[1] // rider_ref.shape[0]
    block = half_block(side, pl.program_id(0), ids_ref)
    product = with_cls(left_ref, right_ref, cls_left_ref, cls_right_ref)
    out_ref[0, :, :rows] = product.reshape(owners, rows, product.shape[1])
    rider = rider_ref[...]
    out_ref[0, :, rows:] = jnp.where(block == 0, rider, jnp.zeros_like(rider))


def joint_grad_kernel(side, ids_ref, left_ref, last_left_ref, right_ref, last_right_ref, *refs):
    block = half_block(side, pl.program_id(0), ids_ref)

    @pl.when(block < 3)
    def main():
        refs[-1][0] = dot_tn(left_ref[...], right_ref[...]).astype(BF16)

    @pl.when(block == 3)
    def last():
        refs[-1][0] = dot_tn(last_left_ref[...], last_right_ref[...]).astype(BF16)


def half_block(side, step, ids):
    return 2 * ((ids[1] & 1) ^ side) + step


def half_grads(kernel, name, ids, operands, specs, shape, after, weight):
    rows, width = operands[0].shape
    return pl.pallas_call(
        kernel,
        out_shape=jax.ShapeDtypeStruct((2,) + shape, BF16),
        grid_spec=pltpu.PrefetchScalarGridSpec(
            num_scalar_prefetch=1,
            grid=(2,),
            in_specs=specs + [ANYWHERE] * len(after),
            out_specs=pl.BlockSpec((1,) + shape, lambda j, ids: (j,) + (0,) * len(shape)),
        ),
        compiler_params=pltpu.CompilerParams(vmem_limit_bytes=56 * MIB),
        cost_estimate=cost(4 * rows * width * width, 10 * rows * width, weight),
        name=name,
    )(ids, *operands, *after)


def plain_cols_kernel(ids_ref, left_ref, right_ref, cls_left_ref, cls_right_ref, *refs):
    refs[-1][0] = with_cls(left_ref, right_ref, cls_left_ref, cls_right_ref)


def cols_grads(side, ids, left, right, cls_left, cls_right, rider, after, weight):
    rows, width = left.shape
    owners, extra, unused = rider.shape
    specs = [
        whole(left.shape),
        pl.BlockSpec((rows, width), lambda j, ids: (0, half_block(side, j, ids))),
        pl.BlockSpec((cls_left.shape[0], width), lambda j, ids: (0, CLS_LOW), pipeline_mode=pl.Buffered(1)),
        pl.BlockSpec((cls_left.shape[0], width), lambda j, ids: (0, half_block(side, j, ids))),
    ]
    operands = [left, right, cls_left, cls_right]
    if width // owners % 16 == 0:
        return half_grads(
            partial(cols_grad_kernel, side), "cols_grads", ids, operands + [rider], specs + [whole(rider.shape)],
            (owners, width // owners + extra, width), after, weight,
        )
    product = half_grads(plain_cols_kernel, "cols_grads", ids, operands, specs, (width, width), after, weight)
    first = half_block(side, 0, ids) == 0
    rider = jnp.where(first, rider, jnp.zeros_like(rider))
    rider = jnp.stack([rider, jnp.zeros_like(rider)], axis=0)
    return jnp.concatenate([product.reshape(2, owners, width // owners, width), rider], axis=2)


def joint_grads(side, ids, left, last_left, right, last_right, after, weight):
    rows, width = left.shape
    specs = [
        whole(left.shape),
        whole(left.shape),
        pl.BlockSpec((rows, width), lambda j, ids: (0, jnp.minimum(half_block(side, j, ids), 2))),
        whole(left.shape),
    ]
    operands = [left, last_left, right, last_right]
    return half_grads(partial(joint_grad_kernel, side), "joint_grads", ids, operands, specs, (width, width), after, weight)


def rows_grad_kernel(ids_ref, left_ref, right_ref, *refs):
    send_ref, keep_ref, held_ref = refs[-3:]
    core = ids_ref[1] & 1
    held_ref[...] = dot_tn(left_ref[...], right_ref[...]).reshape(held_ref.shape)
    for share in range(2):
        send_ref[share] = held_ref[:, 2 * (1 - core) + share].astype(BF16)
        keep_ref[share] = held_ref[:, 2 * core + share].astype(BF16)


def rows_grads(ids, left, right, count, after):
    rows, width = right.shape
    hidden = left.shape[1]
    shard_rows = hidden // count // 4
    owners = count // 4
    half = jax.ShapeDtypeStruct((2, count, shard_rows, width), BF16)
    out_spec = pl.BlockSpec((2, owners, shard_rows, width), lambda j, ids: (0, j, 0, 0))
    return pl.pallas_call(
        rows_grad_kernel,
        out_shape=(half, half),
        grid_spec=pltpu.PrefetchScalarGridSpec(
            num_scalar_prefetch=1,
            grid=(4,),
            in_specs=[
                pl.BlockSpec((rows, hidden // 4), lambda j, ids: (0, j)),
                pl.BlockSpec((rows, width), lambda j, ids: (0, 0), pipeline_mode=pl.Buffered(1)),
            ] + [ANYWHERE] * len(after),
            out_specs=[out_spec, out_spec],
            scratch_shapes=[pltpu.VMEM((owners, 4, shard_rows, width), F32)],
        ),
        compiler_params=pltpu.CompilerParams(vmem_limit_bytes=56 * MIB),
        cost_estimate=cost(2 * rows * width * hidden, 10 * rows * width),
        name="rows_grads",
    )(ids, left, right, *after)


def later(value, *first):
    return lax.optimization_barrier((value,) + first)[0]


def seg_swap(value, mask):
    count = lax.axis_size("seg")
    return lax.ppermute(value, "seg", [(i, i ^ mask) for i in range(count)])


def rep_swap(value, mask):
    count = lax.axis_size("rep")
    return lax.ppermute(value, "rep", [(i, i ^ mask) for i in range(count)])


def both_swap(value, seg_mask, rep_mask):
    reps = lax.axis_size("rep")
    total = lax.axis_size("seg") * reps
    pairs = [(i, ((i // reps) ^ seg_mask) * reps + ((i % reps) ^ rep_mask)) for i in range(total)]
    return lax.ppermute(value, ("seg", "rep"), pairs)


def place_kernel(count, ids_ref, *refs):
    for copy in fetch_pieces(ids_ref, refs[:count], refs[count], refs[count + 1]):
        copy.wait()


def put_in_place(ids, pieces):
    parts, shape = pieces
    return pl.pallas_call(
        partial(place_kernel, len(parts)),
        out_shape=shape,
        in_specs=[pl.BlockSpec(memory_space=pltpu.SMEM)] + [ANYWHERE] * len(parts),
        out_specs=pl.BlockSpec(memory_space=pltpu.VMEM),
        scratch_shapes=[pltpu.SemaphoreType.DMA((len(parts) * parts[0].shape[0],))],
        compiler_params=pltpu.CompilerParams(vmem_limit_bytes=32 * MIB),
        cost_estimate=cost(0, 4 * shape.size),
        name="put_in_place",
    )(ids, *parts)


def far_pieces(piece):
    return [piece] + [seg_swap(piece, mask) for mask in range(2, lax.axis_size("seg"), 2)]


def after_all(value, first):
    return later(value, *first) if first else value


def gather_shares(piece):
    evens = jnp.stack(far_pieces(piece), axis=0)
    own = [evens, seg_swap(evens, 1)]
    across = [rep_swap(part, 2) for part in own]
    near, far = ([rep_swap(part, 1) for part in parts] for parts in (own, across))
    return own + near + across + far


class Gather:
    def __init__(self, piece):
        self.piece, self.came = piece, far_pieces(piece)

    def across(self, *first):
        self.evens = jnp.stack(self.came[:1] + [later(value, *first) for value in self.came[1:]], axis=0)
        self.came = seg_swap(self.evens, 1)

    def finish(self, *first):
        return jnp.stack([self.evens, later(self.came, *first)], axis=1).reshape((-1,) + self.piece.shape)


def spread_kernel(ids_ref, keep_ref, came_ref, *refs):
    stay_ref, x_ref, y_ref, xy_ref = refs[-4:]
    near, across, core = ids_ref[0] & 1, ids_ref[1] >> 1, ids_ref[1] & 1

    def total(share, side):
        value = keep_ref[share, 0, side].astype(F32) + came_ref[share, 0, side].astype(F32)
        if len(refs) > 4:
            for left_ref, right_ref in (refs[:2], refs[2:4]):
                value = value + dot_nn(left_ref[0, side, 2 * core + share], right_ref[...])
        return value.astype(BF16)

    stay_ref[0] = total(across, near)
    x_ref[0] = total(across, 1 - near)
    y_ref[0] = total(1 - across, near)
    xy_ref[0] = total(1 - across, 1 - near)


def spread(ids, keep, came, product=()):
    unused, count, rows, width = keep.shape
    far = count // 2
    shape = (2, far, 2, rows, width)
    in_spec = pl.BlockSpec((2, 1, 2, rows, width), lambda j: (0, j, 0, 0, 0))
    out_spec = pl.BlockSpec((1, rows, width), lambda j: (j, 0, 0))
    out = jax.ShapeDtypeStruct((far, rows, width), BF16)
    specs = [pl.BlockSpec(memory_space=pltpu.SMEM), in_spec, in_spec]
    if product:
        depth = product[1].shape[0]
        product = [value.reshape(far, 2, 4, rows, depth) if i % 2 == 0 else value for i, value in enumerate(product)]
        specs += [pl.BlockSpec((1, 2, 4, rows, depth), lambda j: (j, 0, 0, 0, 0)), whole(product[1].shape)] * 2
    return pl.pallas_call(
        spread_kernel,
        out_shape=(out,) * 4,
        grid=(far,),
        in_specs=specs,
        out_specs=[out_spec] * 4,
        compiler_params=pltpu.CompilerParams(vmem_limit_bytes=58 * MIB),
        cost_estimate=cost(0, 12 * count * rows * width),
        name="spread",
    )(ids, keep.reshape(shape), came.reshape(shape), *product)


def settle_kernel(ids_ref, *refs):
    far = refs[0].shape[0]
    parts, outs = refs[:-far], refs[-far:]
    start = 0
    for first in range(0, len(parts), 4):
        rows = parts[first].shape[1]
        for mask, out in enumerate(outs):
            a, b, c, d = (part[(ids_ref[0] >> 1) ^ mask].astype(F32) for part in parts[first : first + 4])
            out[start : start + rows] = ((a + b) + (c + d)).astype(BF16)
        start += rows


def settle(ids, *groups):
    far, unused, width = groups[0][0].shape
    heights = [group[0].shape[1] for group in groups]
    if len(groups) > 1 and any(rows % 16 for rows in heights):
        return [jnp.concatenate(parts, axis=0) for parts in zip(*[settle(ids, group) for group in groups])]
    whole_spec = pl.BlockSpec(memory_space=pltpu.VMEM)
    return pl.pallas_call(
        settle_kernel,
        out_shape=(jax.ShapeDtypeStruct((sum(heights), width), BF16),) * far,
        in_specs=[pl.BlockSpec(memory_space=pltpu.SMEM)] + [whole_spec] * (4 * len(groups)),
        out_specs=[whole_spec] * far,
        compiler_params=pltpu.CompilerParams(vmem_limit_bytes=32 * MIB),
        cost_estimate=cost(0, 10 * far * sum(heights) * width),
        name="settle",
    )(ids, *[part for group in groups for part in group])


def halve(value, axis, bit):
    own = lax.dynamic_index_in_dim(value, bit, axis, keepdims=False)
    other = lax.dynamic_index_in_dim(value, 1 - bit, axis, keepdims=False)
    return own, other


class Reduction:
    def __init__(self, ids, send, keep):
        count = lax.axis_size("seg")
        self.ids = ids
        self.shape = (2, count, send.size // (2 * count * send.shape[-1]), send.shape[-1])
        self.keep = keep
        self.came = rep_swap(send, 1)

    def spread(self, *first, product=()):
        came = after_all(self.came, first)
        self.stay, *sends = spread(self.ids, self.keep.reshape(self.shape), came.reshape(self.shape), product)
        self.came = [seg_swap(sends[0], 1), rep_swap(sends[1], 2), both_swap(sends[2], 1, 2)]

    def parts(self, *first):
        return [self.stay] + [after_all(value, first) for value in self.came]


def swap_far(others):
    return [seg_swap(other, 2 * mask) for mask, other in enumerate(others, 1)]


def add_up(own, came, *first):
    total = own.astype(F32)
    for value in came:
        total = total + after_all(value, first).astype(F32)
    return total.astype(BF16)


class Sharing:
    def __init__(self, ids, value):
        self.ids, self.value = ids, value
        self.came = rep_swap(value, 2)

    def step(self, *first):
        self.value = jnp.stack([self.value, later(self.came, *first)], axis=0)
        self.came = rep_swap(self.value, 1)

    def finish(self, *first):
        held = jnp.concatenate([self.value, later(self.came, *first)], axis=0)
        places = [self.ids[1] ^ owner for owner in (0, 2, 1, 3)]
        return [
            lax.dynamic_index_in_dim(held, 2 * (place & 1) + place // 2, 0, keepdims=False).astype(F32) for place in places
        ]


def body(tokens, cotangent, doc_counts, w_qkv, w_out, w_up, w_down, c_qkv, c_out, pos_table, norm_gains, norm_shifts):
    micro_count, unused, seg_local, seg_length, width = tokens.shape
    count = lax.axis_size("seg")
    me = lax.axis_index("seg").astype(jnp.int32)
    rep = lax.axis_index("rep").astype(jnp.int32)
    ids = jnp.stack([me, rep])
    shard_rows = w_qkv.shape[0]
    local = micro_count * seg_local
    rows = local * seg_length
    table_rows = pos_table.shape[0]
    norm_cols = norm_gains.shape[1]
    aligned = shard_rows % 16 == 0

    def half_columns(matrix):
        half = lax.dynamic_slice_in_dim(matrix, 2 * width * (rep & 1), 2 * width, 1)
        return jnp.stack([half[:, :width], half[:, width:]], axis=0)

    def half_of(wide, narrow):
        first = jnp.stack([wide[:, :width], wide[:, width : 2 * width]], axis=0)
        second = jnp.stack([wide[:, 2 * width :], narrow], axis=0)
        return jnp.where((rep & 1) == 0, first, second)

    norms = jnp.pad(jnp.concatenate([norm_gains, norm_shifts], axis=0), ((0, 2), (0, width - norm_cols)))
    small = jnp.stack([jnp.pad(pos_table, ((0, 8 - table_rows), (0, 0))), norms], axis=0)
    own_down = lax.dynamic_slice_in_dim(w_down, 2 * shard_rows * (rep & 1), 2 * shard_rows, 0)
    ffn_piece = jnp.concatenate([half_columns(w_up), own_down.reshape(2, shard_rows, width), small], axis=1)
    ffn_half = lax.all_gather(ffn_piece, "seg", axis=0)
    qo_piece = lax.dynamic_slice_in_dim(w_qkv, jnp.minimum(rep, 2) * width, width, 1)
    qo_piece = jnp.where(rep == 3, w_out, qo_piece)
    shapes = [shape_of((4, count, shard_rows, width), BF16), shape_of((count, 4, shard_rows, width), BF16)]
    qo_shares = gather_shares(qo_piece)
    qo_pieces = (qo_shares, shapes[0])
    cross_piece = half_of(c_qkv, c_out)
    cross_half = lax.all_gather(later(cross_piece, qo_shares[0]), "seg", axis=0)

    counts = doc_counts[:, 0]
    ends = jnp.cumsum(counts, axis=1)
    owners = me ^ jnp.arange(count, dtype=jnp.int32)
    seg_ids = owners[:, None, None] * seg_local + jnp.arange(seg_local, dtype=jnp.int32)[None, None, :]
    seg_ids = jnp.broadcast_to(seg_ids, (count, micro_count, seg_local))
    past = seg_ids[..., None] >= ends[None, :, None, :]
    doc_ids = jnp.sum(past.astype(jnp.int32), axis=-1)
    starts = jnp.sum(jnp.where(past, counts[None, :, None, :], 0), axis=-1)
    places = (seg_ids - starts).reshape(-1, 1)
    keys = (doc_ids + (counts.shape[1] + 1) * jnp.arange(micro_count, dtype=jnp.int32)[None, :, None]).reshape(-1)

    flat = tokens.reshape(rows, width)
    cot = cotangent.reshape(rows, width)
    block = 4 * seg_length
    steps = rows // block
    halves_of = ((0, steps // 2), (steps // 2, steps - steps // 2))

    everything = (0, steps)
    if aligned:
        proj, probs, mixed, pre_first, full_qo = attention_forward(
            flat, None, seg_length, block, everything, after=[keys, places], pieces=qo_pieces, ids=ids
        )
    else:
        full_qo = put_in_place(ids, qo_pieces).reshape(4, 1, width, width)
        proj, probs, mixed, pre_first = attention_forward(flat, full_qo, seg_length, block, everything)
    ffn_half = later(ffn_half, proj)
    small = ffn_half[:, :, 2 * shard_rows :]
    table = small[:, 0, :table_rows].reshape(count * table_rows, width)
    norms = small[:, 1, :6, :norm_cols].transpose(1, 0, 2).reshape(6, width)
    gains, shifts = norms[:3], norms[3:]
    ffn_other = rep_swap(ffn_half, 1)

    def joined(parts, start, owner_first):
        own, other = [part[:, :, start : start + shard_rows] for part in parts]
        both = jnp.where((rep & 1) == 0, jnp.concatenate([own, other], axis=1), jnp.concatenate([other, own], axis=1))
        return (both if owner_first else both.transpose(1, 0, 2, 3)).reshape(4, 1, width, width)

    small_block = 2 * seg_length
    if aligned:
        low, act, slope, out, branch, grad2, sums2, cls, full_up, full_down = ffn_forward(
            pre_first, cot, None, gains, shifts, seg_length, small_block, ([ffn_half, ffn_other], shapes), ids
        )
    else:
        full_up = joined([ffn_half, ffn_other], 0, False)
        full_down = joined([ffn_half, ffn_other], shard_rows, True)
        low, act, slope, out, branch, grad2, sums2, cls = ffn_forward(
            pre_first, cot, [full_up, full_down], gains, shifts, seg_length, small_block
        )

    def with_edge(values, edge):
        whole_rows = values.reshape(local, seg_length, values.shape[1])
        return lax.dynamic_update_slice(whole_rows, edge[:, None], (0, 0, 0)).reshape(values.shape)

    edges = Gather(cls[:, CLS_OUT * width : (CLS_COT + 1) * width])
    send_down, keep_down = rows_grads(ids, act, branch, count, [edges.piece])
    down = Reduction(ids, send_down, keep_down)
    edges.across(send_down)
    cross_half = later(cross_half, send_down)
    cross_other = rep_swap(cross_half, 1)
    *kept, sums1a = ffn_backward(
        branch, grad2, pre_first, slope, full_up, full_down, gains, small_block, (0, steps), LONG, after=[edges.evens, cross_half]
    )
    edges = edges.finish(kept[0]).reshape(-1, 2 * width)
    cross_parts, cross_shape = [cross_half, later(cross_other, kept[0])], shapes[0]
    if not aligned:
        cross_parts, cross_shape = [joined(cross_parts, 0, False)], None
    cls_new, cls_branch, grad_c, c_sums, table_grad, *cls_back = cross_block(
        ids, edges, cls, keys[:, None], jnp.concatenate([keys, keys])[None, :], places, table, gains, shifts, full_up,
        full_down, cross_parts, cross_shape,
    )
    cls_hidden, cls_grad1, cls_low1, cls_turned = cls_back
    operands = [cls_turned, cls_branch]
    c_own, c_other = halve(grad_c.reshape(2, 2, shard_rows, width), 0, rep & 1)
    c_came = rep_swap(c_other, 1)
    down.spread(kept[0], product=operands + [rep_swap(value, 1) for value in operands])
    grad_hidden, grad1, low1, sums1b = ffn_backward(
        branch, grad2, pre_first, slope, full_up, full_down, gains, small_block, (steps, steps), SHORT, prior=kept, after=[down.stay]
    )
    low1 = with_edge(low1, cls_low1)
    norm_sums = (sums2 + sums1a + sums1b + c_sums).reshape(8, count, norm_cols).transpose(1, 0, 2)
    norm_sums = jnp.pad(norm_sums, ((0, 0), (0, 0), (0, width - norm_cols)))
    rider = jnp.concatenate([norm_sums, table_grad.reshape(count, table_rows, width)], axis=1).astype(BF16)
    send_up = cols_grads(1, ids, low, grad_hidden, cls, cls_hidden, rider, [], SHORT)
    own_down, *others = settle(ids, down.parts(send_up))
    came_down = swap_far(others)
    keep_up = cols_grads(0, ids, low, grad_hidden, cls, cls_hidden, rider, [send_up, own_down], LONG)
    up = Reduction(ids, send_up, keep_up)
    up.spread(keep_up, *came_down[:1])
    grad_proj = attention_backward(low1, proj, probs, full_qo, seg_length, block, after=[up.stay])
    down_share = add_up(own_down, came_down, grad_proj)
    send_qo = joint_grads(1, ids, flat, mixed, grad_proj, low1, [], SHORT)
    own_up, *others = settle(ids, up.parts(send_qo))
    came_up = swap_far(others)
    keep_qo = joint_grads(0, ids, flat, mixed, grad_proj, low1, [send_qo, own_up], LONG)
    qo = Reduction(ids, send_qo, keep_qo)
    qo.spread(keep_qo, *came_up[:2])
    c_own, c_other = halve(c_own.astype(F32) + later(c_came, qo.stay).astype(F32), 0, rep >> 1)
    c_came = rep_swap(c_other.astype(BF16), 2)
    input_grad = input_gradient(with_edge(later(grad1, qo.stay), cls_grad1), grad_proj, full_qo, block, [qo.stay])
    own, *others = settle(ids, qo.parts(input_grad))
    came = swap_far(others)
    c_share = (c_own + later(c_came, own).astype(F32)).astype(BF16)
    early = Sharing(ids, jnp.concatenate([down_share, add_up(own_up, came_up, own), c_share], axis=0))
    late = Sharing(ids, add_up(own, came))
    early.step(late.value)
    layer_out = with_edge(later(out, late.value), cls_new)
    early_shares = early.finish(layer_out)
    starts = (0, shard_rows, 2 * shard_rows, 2 * shard_rows + 16, 3 * shard_rows + 16)
    down_parts, up_parts, riders, c_parts = [
        [part[first:last] for part in early_shares] for first, last in zip(starts, starts[1:])
    ]
    done = [
        jnp.concatenate(up_parts, axis=1),
        jnp.concatenate(down_parts, axis=0),
        jnp.concatenate(c_parts[:3], axis=1),
        c_parts[3],
    ]
    summed = riders[0]
    late.step(layer_out, *done)
    qo_parts = late.finish()

    return (
        layer_out.reshape(tokens.shape),
        input_grad.reshape(tokens.shape),
        jnp.concatenate(qo_parts[:3], axis=1),
        qo_parts[3],
        *done,
        summed[8 : 8 + table_rows],
        summed[:3, :norm_cols],
        summed[3:6, :norm_cols],
    )


def solution(mesh):
    rows = P(None, "rep", "seg", None, None)
    split = P("seg", None)
    last = P(None, "seg")
    return jax.shard_map(
        body,
        mesh=mesh,
        in_specs=(rows, rows, P(None, "rep", None)) + (split,) * 7 + (last, last),
        out_specs=(rows, rows) + (split,) * 7 + (last, last),
        check_vma=False,
    )
```

```python
from functools import partial
import jax
import jax.numpy as jnp
from jax import lax
from jax.experimental import pallas as pl
from jax.experimental.pallas import tpu as pltpu
from jax.sharding import PartitionSpec as P

HEAD_DIM = 64
PAIR = 2 * HEAD_DIM
EPSILON = 1e-05
NEGATIVE = -1e30
F32 = jnp.float32
BF16 = jnp.bfloat16
MIB = 1 << 20
LONG, SHORT = 6.0, 0.001
CLS_ACT, CLS_SLOPE, CLS_LOW, CLS_PRE, CLS_TOTAL, CLS_OUT, CLS_COT, CLS_BLOCKS = 0, 4, 8, 9, 10, 11, 12, 13


def dot_nn(left, right):
    return lax.dot_general(left, right, (((1,), (0,)), ((), ())), preferred_element_type=F32)


def dot_nt(left, right):
    return lax.dot_general(left, right, (((1,), (1,)), ((), ())), preferred_element_type=F32)


def dot_tn(left, right):
    return lax.dot_general(left, right, (((0,), (0,)), ((), ())), preferred_element_type=F32)


def norm_parts(values):
    center = values - jnp.mean(values, axis=-1, keepdims=True)
    spread = jnp.mean(center * center, axis=-1, keepdims=True)
    inverse = lax.rsqrt(spread + EPSILON)
    return center * inverse, inverse


def norm_back(grad, unit, inverse, gain):
    scaled = grad * gain
    first = jnp.mean(scaled, axis=-1, keepdims=True)
    second = jnp.mean(scaled * unit, axis=-1, keepdims=True)
    return inverse * (scaled - first - unit * second)


def gelu_parts(hidden):
    phi = 0.5 + 0.5 * lax.erf(hidden * 0.5 ** 0.5)
    bell = jnp.exp(hidden * hidden * -0.5) * 0.3989422804014327
    return hidden * phi, phi + hidden * bell


def halves(pair, first_half):
    zero = jnp.zeros_like(pair)
    return jnp.concatenate([jnp.where(first_half, pair, zero), jnp.where(first_half, zero, pair)], axis=0)


def pairs_forward(queries, keys, values, first_half, same=None):
    rows = queries[0].shape[0]
    scale = BF16(HEAD_DIM ** -0.5)
    scores = [dot_nt(key, halves(query * scale, first_half)) for query, key in zip(queries, keys)]
    if same is not None:
        scores = [jnp.where(same, score, NEGATIVE) for score in scores]
    raised = [jnp.exp(score - jnp.max(score, axis=0, keepdims=True)) for score in scores]
    probs = [(value * (1.0 / jnp.sum(value, axis=0, keepdims=True))).astype(BF16) for value in raised]
    both = [dot_tn(prob, value) for prob, value in zip(probs, values)]
    return probs, [jnp.where(first_half, value[:rows], value[rows:]) for value in both]


def pairs_backward(queries, keys, values, probs, grads_mixed, first_half):
    rows = queries[0].shape[0]
    scale = BF16(HEAD_DIM ** -0.5)
    grads_both = [halves(grad, first_half) for grad in grads_mixed]
    grads_probs = [dot_nt(value, grad) for value, grad in zip(values, grads_both)]
    grads_value = [dot_nn(prob, grad) for prob, grad in zip(probs, grads_both)]
    grads_scores = []
    for prob, grad in zip(probs, grads_probs):
        wide = prob.astype(F32)
        product = wide * grad
        grads_scores.append((product - wide * jnp.sum(product, axis=0, keepdims=True)).astype(BF16))
    grads_key = [dot_nn(grad, halves(query * scale, first_half)) for grad, query in zip(grads_scores, queries)]
    both = [dot_tn(grad, key) for grad, key in zip(grads_scores, keys)]
    grads_query = [jnp.where(first_half, value[:rows], value[rows:]) * (HEAD_DIM ** -0.5) for value in both]
    return grads_query, grads_key, grads_value


def pair_columns(width):
    starts = range(0, width, PAIR)
    return [[slice(part * width + start, part * width + start + PAIR) for start in starts] for part in range(3)]


def lane_half(shape):
    return lax.broadcasted_iota(jnp.int32, shape, 1) % PAIR < HEAD_DIM


def square(value):
    return value.reshape(-1, value.shape[-1])


def up_block(ref, part):
    return square(ref[:, part])


def down_block(ref, part):
    count = ref.shape[0] // 4
    return square(ref[part * count : (part + 1) * count])


def whole(shape):
    return pl.BlockSpec(shape, lambda *at: (0,) * len(shape), pipeline_mode=pl.Buffered(1))


ANYWHERE = pl.BlockSpec(memory_space=pl.ANY)


def cost(flops, moved, weight=1.0):
    return pl.CostEstimate(flops=int(flops * weight), bytes_accessed=int(moved * weight), transcendentals=0)


def rows_call(kernel, name, block, span, rowed, fixed, outs, flops, prior=(), after=(), extra=(), ids=None, scratch=(), weight=1.0):
    first, steps = span

    def cut(value):
        array, ratio = value if isinstance(value, tuple) else (value, 1)
        shape = (block // ratio,) + array.shape[1:]
        return array, pl.BlockSpec(shape, lambda i, *ids: (i + first,) + (0,) * (len(shape) - 1))

    ins = [cut(value) for value in rowed] + list(fixed)
    results = [cut(value) for value in outs] + [(shape, whole(shape.shape)) for shape in extra]
    unread = list(prior) + list(after)
    lead = 0 if ids is None else 1
    moved = sum(value.size * value.dtype.itemsize for value, unused in ins + results) // 2

    def run(*refs):
        start = lead + len(ins)
        kernel(*refs[:start], *refs[start + len(unread) :])

    return pl.pallas_call(
        run,
        out_shape=tuple(jax.ShapeDtypeStruct(shape.shape, shape.dtype) for shape, unused in results),
        grid_spec=pltpu.PrefetchScalarGridSpec(
            num_scalar_prefetch=lead,
            grid=(steps,),
            in_specs=[spec for unused, spec in ins] + [ANYWHERE] * len(unread),
            out_specs=[spec for unused, spec in results],
            scratch_shapes=list(scratch),
        ),
        input_output_aliases={lead + len(ins) + i: i for i in range(len(prior))},
        compiler_params=pltpu.CompilerParams(vmem_limit_bytes=58 * MIB),
        cost_estimate=cost(2 * flops * steps * block, moved, weight),
        name=name,
    )(*([] if ids is None else [ids]), *[array for array, unused in ins], *unread)


def shape_of(shape, dtype):
    return jax.ShapeDtypeStruct(shape, dtype)


def fetch_pieces(ids_ref, parts, out_ref, sems):
    me, rep = ids_ref[0], ids_ref[1]
    copies = []
    for number, part in enumerate(parts):
        for slot in range(part.shape[0]):
            target = out_ref.at[rep ^ (number // 2), me ^ (2 * slot + number % 2)]
            copies.append(pltpu.make_async_copy(part.at[slot], target, sems.at[number * part.shape[0] + slot]))
    for copy in copies:
        copy.start()
    return copies


def fetch_halves(ids_ref, parts, out_ref, sems, start=0, owner_first=False):
    core = ids_ref[1] & 1
    rows = out_ref.shape[2]
    base = 4 if owner_first else 0
    copies = []
    for side, part in enumerate(parts):
        owner_core = core if side == 0 else 1 - core
        for share in range(2):
            piece = part.at[:, share] if part.shape[-2] == rows else part.at[:, share, pl.ds(start, rows)]
            block = 2 * owner_core + share
            target = out_ref.at[:, block] if owner_first else out_ref.at[block]
            copies.append(pltpu.make_async_copy(piece, target, sems.at[base + 2 * side + share]))
    for copy in copies:
        copy.start()
    return copies


def attention_rows(seg_length, x_ref, wqo_ref, proj_ref, probs_ref, mixed_ref, pre_ref):
    rows, width = x_ref.shape
    pairs = width // PAIR
    for part in range(3):
        proj_ref[:, part * width : (part + 1) * width] = dot_nn(x_ref[...], square(wqo_ref[part])).astype(BF16)
    first_half = lane_half((seg_length, PAIR))
    columns = pair_columns(width)
    for seg in range(rows // seg_length):
        span = slice(seg * seg_length, (seg + 1) * seg_length)
        probs, mixed = pairs_forward(*[[proj_ref[span, cols] for cols in part] for part in columns], first_half)
        for pair in range(pairs):
            probs_ref[seg, pair] = probs[pair]
            mixed_ref[span, columns[0][pair]] = mixed[pair].astype(BF16)
    pre_ref[...] = x_ref[...].astype(F32) + dot_nn(mixed_ref[...], square(wqo_ref[3]))


def attention_first_kernel(seg_length, count, ids_ref, x_ref, *refs):
    parts, (proj_ref, probs_ref, mixed_ref, pre_ref, wqo_ref, sems) = refs[:count], refs[count:]

    @pl.when(pl.program_id(0) == 0)
    def fetch():
        for copy in fetch_pieces(ids_ref, parts, wqo_ref, sems):
            copy.wait()

    attention_rows(seg_length, x_ref, wqo_ref, proj_ref, probs_ref, mixed_ref, pre_ref)


def attention_shapes(rows, width, seg_length):
    probs = shape_of((rows // seg_length, width // PAIR, seg_length, 2 * seg_length), BF16)
    return [
        shape_of((rows, 3 * width), BF16), (probs, seg_length), shape_of((rows, width), BF16), shape_of((rows, width), F32),
    ]


def attention_forward(rows_in, weight, seg_length, block, span, prior=(), after=(), pieces=None, ids=None):
    rows, width = rows_in.shape
    outs = attention_shapes(rows, width, seg_length)
    flops = width * (4 * width + 8 * seg_length)
    if pieces is None:
        return rows_call(
            partial(attention_rows, seg_length), "attention_forward", block, span, [rows_in],
            [(weight, whole(weight.shape))], outs, flops, prior, after, weight=SHORT,
        )
    parts, shape = pieces
    return rows_call(
        partial(attention_first_kernel, seg_length, len(parts)), "attention_forward", block, span, [rows_in],
        [(part, ANYWHERE) for part in parts], outs, flops, prior, after, [shape], ids,
        [pltpu.SemaphoreType.DMA((len(parts) * parts[0].shape[0],))], SHORT,
    )


def skewed(*chains):
    waiting, running = list(chains), []
    while waiting or running:
        running += waiting[:1]
        waiting = waiting[1:]
        running = [chain for chain in running if next(chain, None)]


def row_parts(rows, height):
    return [slice(start, start + height) for start in range(0, rows, height)]


def ffn_rows(
    seg_length, pre_ref, cot_ref, wup_ref, wdown_ref, gains_ref, shifts_ref,
    low_ref, act_ref, slope_ref, out_ref, branch_ref, grad_ref, sums_ref, cls_ref,
):
    rows, width = pre_ref.shape
    segs = rows // seg_length

    @pl.when(pl.program_id(0) == 0)
    def start_sums():
        sums_ref[...] = jnp.zeros_like(sums_ref)

    def chain(span):
        def keep_cls(block, values):
            for seg in range((span.stop - span.start) // seg_length):
                place = pl.ds(pl.program_id(0) * segs + span.start // seg_length + seg, 1)
                row = values[seg * seg_length : seg * seg_length + 1].astype(F32)
                cls_ref[place, block * width : (block + 1) * width] = row

        pre = pre_ref[span, :]
        unit, unused = norm_parts(pre)
        total = unit * gains_ref[0:1].astype(F32) + shifts_ref[0:1].astype(F32)
        low = total.astype(BF16)
        low_ref[span, :] = low
        keep_cls(CLS_LOW, low)
        keep_cls(CLS_PRE, pre)
        held = dot_nn(low, square(wup_ref[0]))
        yield True
        for part in range(4):
            cols = slice(part * width, (part + 1) * width)
            ahead = dot_nn(low, square(wup_ref[part + 1])) if part < 3 else None
            act, slope = gelu_parts(held)
            act, slope = act.astype(BF16), slope.astype(BF16)
            act_ref[span, cols] = act
            slope_ref[span, cols] = slope
            keep_cls(CLS_ACT + part, act)
            keep_cls(CLS_SLOPE + part, slope)
            total = total + dot_nn(act, down_block(wdown_ref, part))
            held = ahead
            yield True
        gain = gains_ref[1:2].astype(F32)
        unit, inverse = norm_parts(total)
        out = unit * gain + shifts_ref[1:2].astype(F32)
        out_ref[span, :] = out.astype(BF16)
        cot = cot_ref[span, :]
        keep_cls(CLS_TOTAL, total)
        keep_cls(CLS_OUT, out)
        keep_cls(CLS_COT, cot)
        is_cls = lax.broadcasted_iota(jnp.int32, total.shape, 0) % seg_length == 0
        grad = jnp.where(is_cls, 0.0, cot.astype(F32))
        pre_grad = norm_back(grad, unit, inverse, gain)
        grad_ref[span, :] = pre_grad
        branch_ref[span, :] = pre_grad.astype(BF16)
        sums_ref[1:2] += jnp.sum(grad * unit, axis=0, keepdims=True)
        sums_ref[4:5] += jnp.sum(grad, axis=0, keepdims=True)

    skewed(*[chain(span) for span in row_parts(rows, 2 * seg_length)])


def ffn_first_kernel(seg_length, ids_ref, pre_ref, cot_ref, gains_ref, shifts_ref, half_ref, other_ref, *refs):
    *outs, wup_ref, wdown_ref, sems = refs

    @pl.when(pl.program_id(0) == 0)
    def fetch():
        parts = (half_ref, other_ref)
        up = fetch_halves(ids_ref, parts, wup_ref, sems)
        down = fetch_halves(ids_ref, parts, wdown_ref, sems, wup_ref.shape[2], True)
        for copy in up + down:
            copy.wait()

    ffn_rows(seg_length, pre_ref, cot_ref, wup_ref, wdown_ref, gains_ref, shifts_ref, *outs)


def ffn_forward(pre_first, cot, weights, gains, shifts, seg_length, block, pieces=None, ids=None):
    rows, width = pre_first.shape
    span = (0, rows // block)
    wide, low = shape_of((rows, 4 * width), BF16), shape_of((rows, width), BF16)
    outs = [low, wide, wide, low, low, shape_of((rows, width), F32)]
    extra = [shape_of((8, width), F32), shape_of((rows // seg_length, CLS_BLOCKS * width), F32)]
    if pieces is None:
        return rows_call(
            partial(ffn_rows, seg_length), "ffn_forward", block, span, [pre_first, cot],
            [(value, whole(value.shape)) for value in (*weights, gains, shifts)], outs, 8 * width * width, extra=extra,
        )
    parts, shapes = pieces
    return rows_call(
        partial(ffn_first_kernel, seg_length), "ffn_forward", block, span, [pre_first, cot],
        [(gains, whole(gains.shape)), (shifts, whole(shifts.shape))] + [(part, ANYWHERE) for part in parts], outs,
        8 * width * width, extra=extra + shapes, ids=ids, scratch=[pltpu.SemaphoreType.DMA((8,))],
    )


def ffn_back_rows(branch_ref, grad2_ref, pre1_ref, slope_ref, wup_ref, wdown_ref, gains_ref, gradh_ref, grad1_ref, low1_ref, sums_ref):
    width = branch_ref.shape[1]
    total = grad2_ref[...]
    for part in range(4):
        cols = slice(part * width, (part + 1) * width)
        grad_act = dot_nt(branch_ref[...], down_block(wdown_ref, part))
        grad_hidden = (grad_act * slope_ref[:, cols].astype(F32)).astype(BF16)
        gradh_ref[:, cols] = grad_hidden
        total = total + dot_nt(grad_hidden, square(wup_ref[part]))
    unit, inverse = norm_parts(pre1_ref[...])
    grad1 = norm_back(total, unit, inverse, gains_ref[0:1].astype(F32))
    grad1_ref[...] = grad1
    low1_ref[...] = grad1.astype(BF16)

    @pl.when(pl.program_id(0) == 0)
    def start_sums():
        sums_ref[...] = jnp.zeros_like(sums_ref)

    sums_ref[0:1] += jnp.sum(total * unit, axis=0, keepdims=True)
    sums_ref[3:4] += jnp.sum(total, axis=0, keepdims=True)


def ffn_backward(branch, grad2, pre_first, slope, w_up, w_down, gains, block, span, weight, prior=(), after=()):
    rows, width = branch.shape
    return rows_call(
        ffn_back_rows, "ffn_backward", block, span, [branch, grad2, pre_first, slope],
        [(w_up, whole(w_up.shape)), (w_down, whole(w_down.shape)), (gains, whole(gains.shape))],
        [shape_of((rows, 4 * width), BF16), shape_of((rows, width), F32), shape_of((rows, width), BF16)],
        8 * width * width, prior, after, [shape_of((8, width), F32)], weight=weight,
    )


def attention_back_rows(seg_length, low1_ref, proj_ref, probs_ref, wqo_ref, gradp_ref, gradm_ref):
    rows, width = low1_ref.shape
    pairs = width // PAIR
    gradm_ref[...] = dot_nt(low1_ref[...], square(wqo_ref[3])).astype(BF16)
    first_half = lane_half((seg_length, PAIR))
    columns = pair_columns(width)
    for seg in range(rows // seg_length):
        span = slice(seg * seg_length, (seg + 1) * seg_length)
        grads = pairs_backward(
            *[[proj_ref[span, cols] for cols in part] for part in columns], [probs_ref[seg, pair] for pair in range(pairs)],
            [gradm_ref[span, cols] for cols in columns[0]], first_half,
        )
        for part, parts in zip(columns, grads):
            for cols, grad in zip(part, parts):
                gradp_ref[span, cols] = grad.astype(BF16)


def attention_backward(low1, proj, probs, w_qo, seg_length, block, after=()):
    rows, width = low1.shape
    return rows_call(
        partial(attention_back_rows, seg_length), "attention_backward", block, (0, rows // block),
        [low1, proj, (probs, seg_length)], [(w_qo, whole(w_qo.shape))],
        [shape_of((rows, 3 * width), BF16)],
        width * (width + 16 * seg_length), (), after, scratch=[pltpu.VMEM((block, width), BF16)], weight=SHORT,
    )[0]


def input_rows(grad1_ref, gradp_ref, wqo_ref, input_ref):
    width = grad1_ref.shape[1]
    total = grad1_ref[...]
    for part in range(3):
        total = total + dot_nt(gradp_ref[:, part * width : (part + 1) * width], square(wqo_ref[part]))
    input_ref[...] = total


def input_gradient(grad1, gradp, w_qo, block, after):
    rows, width = grad1.shape
    return rows_call(
        input_rows, "input_gradient", block, (0, rows // block), [grad1, gradp], [(w_qo, whole(w_qo.shape))],
        [shape_of((rows, width), F32)], 3 * width * width, (), after, weight=LONG,
    )[0]


def cross_kernel(
    local, fetch, ids_ref, rows_ref, cls_ref, keyc_ref, keyr_ref, place_ref, table_ref, gains_ref, shifts_ref,
    wup_hbm, wdown_hbm, *refs
):
    parts, refs = (refs[:2], refs[2:]) if fetch else (refs[:1], refs[1:])
    new_ref, branch_ref, grad_c_ref, sums_ref, table_grad_ref, hidden_ref, grad1_ref, low1_ref, turned_ref = refs[:9]
    proj_ref, probs_ref, gradm_ref, mixed_ref, gradp_ref, lying_ref, wup_ref, wdown_ref, ffn_sems = refs[9:18]
    ffn_copies = [
        pltpu.make_async_copy(wdown_hbm, wdown_ref, ffn_sems.at[0]), pltpu.make_async_copy(wup_hbm, wup_ref, ffn_sems.at[1]),
    ]
    wc_ref = parts[0]
    if fetch:
        wc_ref, sems = refs[18:]
        copies = fetch_halves(ids_ref, parts, wc_ref, sems)
    for copy in ffn_copies:
        copy.start()
    if fetch:
        for copy in copies:
            copy.wait()
    count, width = rows_ref.shape[0], rows_ref.shape[1] // 2

    def cls(block):
        return cls_ref[:, block * width : (block + 1) * width]

    pairs = width // PAIR
    entries = table_ref.shape[0]
    picks = place_ref[...] == lax.broadcasted_iota(jnp.int32, (count, entries), 1)
    embedded = rows_ref[:, :width] + dot_nn(picks.astype(BF16), table_ref[...])
    low = embedded.astype(BF16)
    for part in range(3):
        proj_ref[:, part * width : (part + 1) * width] = dot_nn(low, square(wc_ref[part])).astype(BF16)
    first_half = lane_half((count, PAIR))
    same = keyc_ref[...] == keyr_ref[...]
    columns = pair_columns(width)
    operands = [[proj_ref[:, cols] for cols in part] for part in columns]
    probs, mixed = pairs_forward(*operands, first_half, same)
    for pair, cols in enumerate(columns[0]):
        probs_ref[pair] = probs[pair]
        mixed_ref[:, cols] = mixed[pair].astype(BF16)
    pre_third = embedded + dot_nn(mixed_ref[...], square(wc_ref[3]))
    unit, inverse = norm_parts(pre_third)
    gain = gains_ref[2:3].astype(F32)
    new_ref[...] = (unit[:local] * gain + shifts_ref[2:3].astype(F32)).astype(BF16)
    grad_out = rows_ref[:, width:]
    grad_third = norm_back(grad_out, unit, inverse, gain)
    sums_ref[...] = jnp.zeros_like(sums_ref)
    sums_ref[2:3] = jnp.sum(grad_out[:local] * unit[:local], axis=0, keepdims=True)
    sums_ref[5:6] = jnp.sum(grad_out[:local], axis=0, keepdims=True)
    gradz = grad_third.astype(BF16)
    gradm_ref[...] = dot_nt(gradz, square(wc_ref[3])).astype(BF16)
    grads = pairs_backward(
        *operands, [probs_ref[pair] for pair in range(pairs)], [gradm_ref[:, cols] for cols in columns[0]], first_half
    )
    for part, parts in zip(columns, grads):
        for cols, grad in zip(part, parts):
            gradp_ref[:, cols] = grad.astype(BF16)
    grad_edge = grad_third[:local]
    for part in range(3):
        grad_edge = grad_edge + dot_nt(gradp_ref[:local, part * width : (part + 1) * width], square(wc_ref[part]))
    rows = grad_c_ref.shape[1]
    own = pl.ds(pl.multiple_of(ids_ref[0] * rows, 8), rows)
    lying_ref[...] = low.astype(F32).T
    own_low = lying_ref[own, :].astype(BF16)
    for part in range(3):
        grad_c_ref[part] = dot_nn(own_low, gradp_ref[:, part * width : (part + 1) * width]).astype(BF16)
    lying_ref[...] = mixed_ref[...].astype(F32).T
    grad_c_ref[3] = dot_nn(lying_ref[own, :].astype(BF16), gradz).astype(BF16)
    unit, inverse = norm_parts(cls(CLS_TOTAL))
    sums_ref[1:2] = jnp.sum(grad_edge * unit, axis=0, keepdims=True)
    sums_ref[4:5] = jnp.sum(grad_edge, axis=0, keepdims=True)
    total = norm_back(grad_edge, unit, inverse, gains_ref[1:2].astype(F32))
    branch = total.astype(BF16)

    def deep(values):
        empty = jnp.zeros((branch_ref.shape[0] - local, width), F32)
        return jnp.concatenate([values, empty], axis=0)

    branch_ref[...] = deep(total).astype(BF16)
    for part in range(4):
        blocks = width // turned_ref.shape[1]
        turned = deep(cls(CLS_ACT + part)).T.reshape(blocks, turned_ref.shape[1], branch_ref.shape[0])
        turned_ref[part * blocks : (part + 1) * blocks] = turned.astype(BF16)
    for copy in ffn_copies:
        copy.wait()
    for part in range(4):
        grad_act = dot_nt(branch, down_block(wdown_ref, part))
        grad_hidden = (grad_act * cls(CLS_SLOPE + part)).astype(BF16)
        hidden_ref[:, part * width : (part + 1) * width] = grad_hidden
        total = total + dot_nt(grad_hidden, square(wup_ref[part]))
    unit, inverse = norm_parts(cls(CLS_PRE))
    grad1 = norm_back(total, unit, inverse, gains_ref[0:1].astype(F32))
    grad1_ref[...] = grad1
    low1_ref[...] = grad1.astype(BF16)
    sums_ref[0:1] = jnp.sum(total * unit, axis=0, keepdims=True)
    sums_ref[3:4] = jnp.sum(total, axis=0, keepdims=True)
    table_grad_ref[...] = lax.dot_general(
        picks[:local].astype(F32), grad_edge, (((0,), (0,)), ((), ())),
        precision=lax.Precision.HIGHEST, preferred_element_type=F32,
    )


def cross_block(ids, edges, cls, key_col, key_row, place, table, gains, shifts, w_up, w_down, parts, shape):
    local, count, width = cls.shape[0], edges.shape[0], table.shape[1]
    depth = -(-local // 128) * 128
    read = [edges, cls, key_col, key_row, place, table, gains, shifts]
    part_specs, fetched = [whole(part.shape) for part in parts], []
    if shape is not None:
        part_specs = [ANYWHERE] * len(parts)
        fetched = [pltpu.VMEM(shape.shape, BF16), pltpu.SemaphoreType.DMA((4,))]
    shapes = (
        jax.ShapeDtypeStruct((local, width), BF16),
        jax.ShapeDtypeStruct((depth, width), BF16),
        jax.ShapeDtypeStruct((4, width // lax.axis_size("seg"), width), BF16),
        jax.ShapeDtypeStruct((8, width), F32),
        jax.ShapeDtypeStruct(table.shape, F32),
        jax.ShapeDtypeStruct((local, 4 * width), BF16),
        jax.ShapeDtypeStruct((local, width), F32),
        jax.ShapeDtypeStruct((local, width), BF16),
        jax.ShapeDtypeStruct((4 * lax.axis_size("seg"), width // lax.axis_size("seg"), depth), BF16),
    )
    return pl.pallas_call(
        partial(cross_kernel, local, shape is not None),
        out_shape=shapes,
        grid_spec=pltpu.PrefetchScalarGridSpec(
            num_scalar_prefetch=1,
            grid=(1,),
            in_specs=[whole(value.shape) for value in read] + [ANYWHERE] * 2 + part_specs,
            out_specs=[whole(value.shape) for value in shapes],
            scratch_shapes=[
                pltpu.VMEM((count, 3 * width), BF16),
                pltpu.VMEM((width // PAIR, count, 2 * count), BF16),
                pltpu.VMEM((count, width), BF16),
                pltpu.VMEM((count, width), BF16),
                pltpu.VMEM((count, 3 * width), BF16),
                pltpu.VMEM((width, count), F32),
                pltpu.VMEM(w_up.shape, BF16),
                pltpu.VMEM(w_down.shape, BF16),
                pltpu.SemaphoreType.DMA((2,)),
            ] + fetched,
        ),
        compiler_params=pltpu.CompilerParams(vmem_limit_bytes=56 * MIB),
        cost_estimate=cost(10_000_000_000, width * width * 8),
        name="cross_block",
    )(ids, *read, w_up, w_down, *parts)


def with_cls(left_ref, right_ref, cls_left_ref, cls_right_ref):
    cls_product = dot_tn(cls_left_ref[...].astype(BF16), cls_right_ref[...])
    return (dot_tn(left_ref[...], right_ref[...]) + cls_product).astype(BF16)


def cols_grad_kernel(side, ids_ref, left_ref, right_ref, cls_left_ref, cls_right_ref, rider_ref, *refs):
    out_ref = refs[-1]
    owners, rows = rider_ref.shape[0], left_ref.shape[1] // rider_ref.shape[0]
    block = half_block(side, pl.program_id(0), ids_ref)
    product = with_cls(left_ref, right_ref, cls_left_ref, cls_right_ref)
    out_ref[0, :, :rows] = product.reshape(owners, rows, product.shape[1])
    rider = rider_ref[...]
    out_ref[0, :, rows:] = jnp.where(block == 0, rider, jnp.zeros_like(rider))


def joint_grad_kernel(side, ids_ref, left_ref, last_left_ref, right_ref, last_right_ref, *refs):
    block = half_block(side, pl.program_id(0), ids_ref)

    @pl.when(block < 3)
    def main():
        refs[-1][0] = dot_tn(left_ref[...], right_ref[...]).astype(BF16)

    @pl.when(block == 3)
    def last():
        refs[-1][0] = dot_tn(last_left_ref[...], last_right_ref[...]).astype(BF16)


def half_block(side, step, ids):
    return 2 * ((ids[1] & 1) ^ side) + step


def half_grads(kernel, name, ids, operands, specs, shape, after, weight):
    rows, width = operands[0].shape
    return pl.pallas_call(
        kernel,
        out_shape=jax.ShapeDtypeStruct((2,) + shape, BF16),
        grid_spec=pltpu.PrefetchScalarGridSpec(
            num_scalar_prefetch=1,
            grid=(2,),
            in_specs=specs + [ANYWHERE] * len(after),
            out_specs=pl.BlockSpec((1,) + shape, lambda j, ids: (j,) + (0,) * len(shape)),
        ),
        compiler_params=pltpu.CompilerParams(vmem_limit_bytes=56 * MIB),
        cost_estimate=cost(4 * rows * width * width, 10 * rows * width, weight),
        name=name,
    )(ids, *operands, *after)


def plain_cols_kernel(ids_ref, left_ref, right_ref, cls_left_ref, cls_right_ref, *refs):
    refs[-1][0] = with_cls(left_ref, right_ref, cls_left_ref, cls_right_ref)


def cols_grads(side, ids, left, right, cls_left, cls_right, rider, after, weight):
    rows, width = left.shape
    owners, extra, unused = rider.shape
    specs = [
        whole(left.shape),
        pl.BlockSpec((rows, width), lambda j, ids: (0, half_block(side, j, ids))),
        pl.BlockSpec((cls_left.shape[0], width), lambda j, ids: (0, CLS_LOW), pipeline_mode=pl.Buffered(1)),
        pl.BlockSpec((cls_left.shape[0], width), lambda j, ids: (0, half_block(side, j, ids))),
    ]
    operands = [left, right, cls_left, cls_right]
    if width // owners % 16 == 0:
        return half_grads(
            partial(cols_grad_kernel, side), "cols_grads", ids, operands + [rider], specs + [whole(rider.shape)],
            (owners, width // owners + extra, width), after, weight,
        )
    product = half_grads(plain_cols_kernel, "cols_grads", ids, operands, specs, (width, width), after, weight)
    first = half_block(side, 0, ids) == 0
    rider = jnp.where(first, rider, jnp.zeros_like(rider))
    rider = jnp.stack([rider, jnp.zeros_like(rider)], axis=0)
    return jnp.concatenate([product.reshape(2, owners, width // owners, width), rider], axis=2)


def joint_grads(side, ids, left, last_left, right, last_right, after, weight):
    rows, width = left.shape
    specs = [
        whole(left.shape),
        whole(left.shape),
        pl.BlockSpec((rows, width), lambda j, ids: (0, jnp.minimum(half_block(side, j, ids), 2))),
        whole(left.shape),
    ]
    operands = [left, last_left, right, last_right]
    return half_grads(partial(joint_grad_kernel, side), "joint_grads", ids, operands, specs, (width, width), after, weight)


def rows_grad_kernel(ids_ref, left_ref, right_ref, *refs):
    send_ref, keep_ref, held_ref = refs[-3:]
    core = ids_ref[1] & 1
    held_ref[...] = dot_tn(left_ref[...], right_ref[...]).reshape(held_ref.shape)
    for share in range(2):
        send_ref[share] = held_ref[:, 2 * (1 - core) + share].astype(BF16)
        keep_ref[share] = held_ref[:, 2 * core + share].astype(BF16)


def rows_grads(ids, left, right, count, after):
    rows, width = right.shape
    hidden = left.shape[1]
    shard_rows = hidden // count // 4
    owners = count // 4
    half = jax.ShapeDtypeStruct((2, count, shard_rows, width), BF16)
    out_spec = pl.BlockSpec((2, owners, shard_rows, width), lambda j, ids: (0, j, 0, 0))
    return pl.pallas_call(
        rows_grad_kernel,
        out_shape=(half, half),
        grid_spec=pltpu.PrefetchScalarGridSpec(
            num_scalar_prefetch=1,
            grid=(4,),
            in_specs=[
                pl.BlockSpec((rows, hidden // 4), lambda j, ids: (0, j)),
                pl.BlockSpec((rows, width), lambda j, ids: (0, 0), pipeline_mode=pl.Buffered(1)),
            ] + [ANYWHERE] * len(after),
            out_specs=[out_spec, out_spec],
            scratch_shapes=[pltpu.VMEM((owners, 4, shard_rows, width), F32)],
        ),
        compiler_params=pltpu.CompilerParams(vmem_limit_bytes=56 * MIB),
        cost_estimate=cost(2 * rows * width * hidden, 10 * rows * width),
        name="rows_grads",
    )(ids, left, right, *after)


def later(value, *first):
    return lax.optimization_barrier((value,) + first)[0]


def seg_swap(value, mask):
    count = lax.axis_size("seg")
    return lax.ppermute(value, "seg", [(i, i ^ mask) for i in range(count)])


def rep_swap(value, mask):
    count = lax.axis_size("rep")
    return lax.ppermute(value, "rep", [(i, i ^ mask) for i in range(count)])


def both_swap(value, seg_mask, rep_mask):
    reps = lax.axis_size("rep")
    total = lax.axis_size("seg") * reps
    pairs = [(i, ((i // reps) ^ seg_mask) * reps + ((i % reps) ^ rep_mask)) for i in range(total)]
    return lax.ppermute(value, ("seg", "rep"), pairs)


def place_kernel(count, ids_ref, *refs):
    for copy in fetch_pieces(ids_ref, refs[:count], refs[count], refs[count + 1]):
        copy.wait()


def put_in_place(ids, pieces):
    parts, shape = pieces
    return pl.pallas_call(
        partial(place_kernel, len(parts)),
        out_shape=shape,
        in_specs=[pl.BlockSpec(memory_space=pltpu.SMEM)] + [ANYWHERE] * len(parts),
        out_specs=pl.BlockSpec(memory_space=pltpu.VMEM),
        scratch_shapes=[pltpu.SemaphoreType.DMA((len(parts) * parts[0].shape[0],))],
        compiler_params=pltpu.CompilerParams(vmem_limit_bytes=32 * MIB),
        cost_estimate=cost(0, 4 * shape.size),
        name="put_in_place",
    )(ids, *parts)


def far_pieces(piece):
    return [piece] + [seg_swap(piece, mask) for mask in range(2, lax.axis_size("seg"), 2)]


def after_all(value, first):
    return later(value, *first) if first else value


def gather_shares(piece):
    evens = jnp.stack(far_pieces(piece), axis=0)
    own = [evens, seg_swap(evens, 1)]
    across = [rep_swap(part, 2) for part in own]
    near, far = ([rep_swap(part, 1) for part in parts] for parts in (own, across))
    return own + near + across + far


class Gather:
    def __init__(self, piece):
        self.piece, self.came = piece, far_pieces(piece)

    def across(self, *first):
        self.evens = jnp.stack(self.came[:1] + [later(value, *first) for value in self.came[1:]], axis=0)
        self.came = seg_swap(self.evens, 1)

    def finish(self, *first):
        return jnp.stack([self.evens, later(self.came, *first)], axis=1).reshape((-1,) + self.piece.shape)


def spread_kernel(ids_ref, keep_ref, came_ref, *refs):
    stay_ref, x_ref, y_ref, xy_ref = refs[-4:]
    near, across, core = ids_ref[0] & 1, ids_ref[1] >> 1, ids_ref[1] & 1

    def total(share, side):
        value = keep_ref[share, 0, side].astype(F32) + came_ref[share, 0, side].astype(F32)
        if len(refs) > 4:
            for left_ref, right_ref in (refs[:2], refs[2:4]):
                value = value + dot_nn(left_ref[0, side, 2 * core + share], right_ref[...])
        return value.astype(BF16)

    stay_ref[0] = total(across, near)
    x_ref[0] = total(across, 1 - near)
    y_ref[0] = total(1 - across, near)
    xy_ref[0] = total(1 - across, 1 - near)


def spread(ids, keep, came, product=()):
    unused, count, rows, width = keep.shape
    far = count // 2
    shape = (2, far, 2, rows, width)
    in_spec = pl.BlockSpec((2, 1, 2, rows, width), lambda j: (0, j, 0, 0, 0))
    out_spec = pl.BlockSpec((1, rows, width), lambda j: (j, 0, 0))
    out = jax.ShapeDtypeStruct((far, rows, width), BF16)
    specs = [pl.BlockSpec(memory_space=pltpu.SMEM), in_spec, in_spec]
    if product:
        depth = product[1].shape[0]
        product = [value.reshape(far, 2, 4, rows, depth) if i % 2 == 0 else value for i, value in enumerate(product)]
        specs += [pl.BlockSpec((1, 2, 4, rows, depth), lambda j: (j, 0, 0, 0, 0)), whole(product[1].shape)] * 2
    return pl.pallas_call(
        spread_kernel,
        out_shape=(out,) * 4,
        grid=(far,),
        in_specs=specs,
        out_specs=[out_spec] * 4,
        compiler_params=pltpu.CompilerParams(vmem_limit_bytes=58 * MIB),
        cost_estimate=cost(0, 12 * count * rows * width),
        name="spread",
    )(ids, keep.reshape(shape), came.reshape(shape), *product)


def settle_kernel(ids_ref, *refs):
    far = refs[0].shape[0]
    parts, outs = refs[:-far], refs[-far:]
    start = 0
    for first in range(0, len(parts), 4):
        rows = parts[first].shape[1]
        for mask, out in enumerate(outs):
            a, b, c, d = (part[(ids_ref[0] >> 1) ^ mask].astype(F32) for part in parts[first : first + 4])
            out[start : start + rows] = ((a + b) + (c + d)).astype(BF16)
        start += rows


def settle(ids, *groups):
    far, unused, width = groups[0][0].shape
    heights = [group[0].shape[1] for group in groups]
    if len(groups) > 1 and any(rows % 16 for rows in heights):
        return [jnp.concatenate(parts, axis=0) for parts in zip(*[settle(ids, group) for group in groups])]
    whole_spec = pl.BlockSpec(memory_space=pltpu.VMEM)
    return pl.pallas_call(
        settle_kernel,
        out_shape=(jax.ShapeDtypeStruct((sum(heights), width), BF16),) * far,
        in_specs=[pl.BlockSpec(memory_space=pltpu.SMEM)] + [whole_spec] * (4 * len(groups)),
        out_specs=[whole_spec] * far,
        compiler_params=pltpu.CompilerParams(vmem_limit_bytes=32 * MIB),
        cost_estimate=cost(0, 10 * far * sum(heights) * width),
        name="settle",
    )(ids, *[part for group in groups for part in group])


def halve(value, axis, bit):
    own = lax.dynamic_index_in_dim(value, bit, axis, keepdims=False)
    other = lax.dynamic_index_in_dim(value, 1 - bit, axis, keepdims=False)
    return own, other


class Reduction:
    def __init__(self, ids, send, keep):
        count = lax.axis_size("seg")
        self.ids = ids
        self.shape = (2, count, send.size // (2 * count * send.shape[-1]), send.shape[-1])
        self.keep = keep
        self.came = rep_swap(send, 1)

    def spread(self, *first, product=()):
        came = after_all(self.came, first)
        self.stay, *sends = spread(self.ids, self.keep.reshape(self.shape), came.reshape(self.shape), product)
        self.came = [seg_swap(sends[0], 1), rep_swap(sends[1], 2), both_swap(sends[2], 1, 2)]

    def parts(self, *first):
        return [self.stay] + [after_all(value, first) for value in self.came]


def swap_far(others):
    return [seg_swap(other, 2 * mask) for mask, other in enumerate(others, 1)]


def add_up(own, came, *first):
    total = own.astype(F32)
    for value in came:
        total = total + after_all(value, first).astype(F32)
    return total.astype(BF16)


class Sharing:
    def __init__(self, ids, value):
        self.ids, self.value = ids, value
        self.came = rep_swap(value, 2)

    def step(self, *first):
        self.value = jnp.stack([self.value, later(self.came, *first)], axis=0)
        self.came = rep_swap(self.value, 1)

    def finish(self, *first):
        held = jnp.concatenate([self.value, later(self.came, *first)], axis=0)
        places = [self.ids[1] ^ owner for owner in (0, 2, 1, 3)]
        return [
            lax.dynamic_index_in_dim(held, 2 * (place & 1) + place // 2, 0, keepdims=False).astype(F32) for place in places
        ]


def body(tokens, cotangent, doc_counts, w_qkv, w_out, w_up, w_down, c_qkv, c_out, pos_table, norm_gains, norm_shifts):
    micro_count, unused, seg_local, seg_length, width = tokens.shape
    count = lax.axis_size("seg")
    me = lax.axis_index("seg").astype(jnp.int32)
    rep = lax.axis_index("rep").astype(jnp.int32)
    ids = jnp.stack([me, rep])
    shard_rows = w_qkv.shape[0]
    local = micro_count * seg_local
    rows = local * seg_length
    table_rows = pos_table.shape[0]
    norm_cols = norm_gains.shape[1]
    aligned = shard_rows % 16 == 0

    def half_columns(matrix):
        half = lax.dynamic_slice_in_dim(matrix, 2 * width * (rep & 1), 2 * width, 1)
        return jnp.stack([half[:, :width], half[:, width:]], axis=0)

    def half_of(wide, narrow):
        first = jnp.stack([wide[:, :width], wide[:, width : 2 * width]], axis=0)
        second = jnp.stack([wide[:, 2 * width :], narrow], axis=0)
        return jnp.where((rep & 1) == 0, first, second)

    norms = jnp.pad(jnp.concatenate([norm_gains, norm_shifts], axis=0), ((0, 2), (0, width - norm_cols)))
    small = jnp.stack([jnp.pad(pos_table, ((0, 8 - table_rows), (0, 0))), norms], axis=0)
    own_down = lax.dynamic_slice_in_dim(w_down, 2 * shard_rows * (rep & 1), 2 * shard_rows, 0)
    ffn_piece = jnp.concatenate([half_columns(w_up), own_down.reshape(2, shard_rows, width), small], axis=1)
    ffn_half = lax.all_gather(ffn_piece, "seg", axis=0)
    qo_piece = lax.dynamic_slice_in_dim(w_qkv, jnp.minimum(rep, 2) * width, width, 1)
    qo_piece = jnp.where(rep == 3, w_out, qo_piece)
    shapes = [shape_of((4, count, shard_rows, width), BF16), shape_of((count, 4, shard_rows, width), BF16)]
    qo_shares = gather_shares(qo_piece)
    qo_pieces = (qo_shares, shapes[0])
    cross_piece = half_of(c_qkv, c_out)
    cross_half = lax.all_gather(later(cross_piece, qo_shares[0]), "seg", axis=0)

    counts = doc_counts[:, 0]
    ends = jnp.cumsum(counts, axis=1)
    owners = me ^ jnp.arange(count, dtype=jnp.int32)
    seg_ids = owners[:, None, None] * seg_local + jnp.arange(seg_local, dtype=jnp.int32)[None, None, :]
    seg_ids = jnp.broadcast_to(seg_ids, (count, micro_count, seg_local))
    past = seg_ids[..., None] >= ends[None, :, None, :]
    doc_ids = jnp.sum(past.astype(jnp.int32), axis=-1)
    starts = jnp.sum(jnp.where(past, counts[None, :, None, :], 0), axis=-1)
    places = (seg_ids - starts).reshape(-1, 1)
    keys = (doc_ids + (counts.shape[1] + 1) * jnp.arange(micro_count, dtype=jnp.int32)[None, :, None]).reshape(-1)

    flat = tokens.reshape(rows, width)
    cot = cotangent.reshape(rows, width)
    block = 4 * seg_length
    steps = rows // block
    halves_of = ((0, steps // 2), (steps // 2, steps - steps // 2))

    everything = (0, steps)
    if aligned:
        proj, probs, mixed, pre_first, full_qo = attention_forward(
            flat, None, seg_length, block, everything, after=[keys, places], pieces=qo_pieces, ids=ids
        )
    else:
        full_qo = put_in_place(ids, qo_pieces).reshape(4, 1, width, width)
        proj, probs, mixed, pre_first = attention_forward(flat, full_qo, seg_length, block, everything)
    ffn_half = later(ffn_half, proj)
    small = ffn_half[:, :, 2 * shard_rows :]
    table = small[:, 0, :table_rows].reshape(count * table_rows, width)
    norms = small[:, 1, :6, :norm_cols].transpose(1, 0, 2).reshape(6, width)
    gains, shifts = norms[:3], norms[3:]
    ffn_other = rep_swap(ffn_half, 1)

    def joined(parts, start, owner_first):
        own, other = [part[:, :, start : start + shard_rows] for part in parts]
        both = jnp.where((rep & 1) == 0, jnp.concatenate([own, other], axis=1), jnp.concatenate([other, own], axis=1))
        return (both if owner_first else both.transpose(1, 0, 2, 3)).reshape(4, 1, width, width)

    small_block = 2 * seg_length
    if aligned:
        low, act, slope, out, branch, grad2, sums2, cls, full_up, full_down = ffn_forward(
            pre_first, cot, None, gains, shifts, seg_length, block, ([ffn_half, ffn_other], shapes), ids
        )
    else:
        full_up = joined([ffn_half, ffn_other], 0, False)
        full_down = joined([ffn_half, ffn_other], shard_rows, True)
        low, act, slope, out, branch, grad2, sums2, cls = ffn_forward(
            pre_first, cot, [full_up, full_down], gains, shifts, seg_length, block
        )

    def with_edge(values, edge):
        whole_rows = values.reshape(local, seg_length, values.shape[1])
        return lax.dynamic_update_slice(whole_rows, edge[:, None], (0, 0, 0)).reshape(values.shape)

    edges = Gather(cls[:, CLS_OUT * width : (CLS_COT + 1) * width])
    send_down, keep_down = rows_grads(ids, act, branch, count, [edges.piece])
    down = Reduction(ids, send_down, keep_down)
    edges.across(send_down)
    cross_half = later(cross_half, send_down)
    cross_other = rep_swap(cross_half, 1)
    *kept, sums1a = ffn_backward(
        branch, grad2, pre_first, slope, full_up, full_down, gains, small_block, (0, steps), LONG, after=[edges.evens, cross_half]
    )
    edges = edges.finish(kept[0]).reshape(-1, 2 * width)
    cross_parts, cross_shape = [cross_half, later(cross_other, kept[0])], shapes[0]
    if not aligned:
        cross_parts, cross_shape = [joined(cross_parts, 0, False)], None
    cls_new, cls_branch, grad_c, c_sums, table_grad, *cls_back = cross_block(
        ids, edges, cls, keys[:, None], jnp.concatenate([keys, keys])[None, :], places, table, gains, shifts, full_up,
        full_down, cross_parts, cross_shape,
    )
    cls_hidden, cls_grad1, cls_low1, cls_turned = cls_back
    operands = [cls_turned, cls_branch]
    c_own, c_other = halve(grad_c.reshape(2, 2, shard_rows, width), 0, rep & 1)
    c_came = rep_swap(c_other, 1)
    down.spread(kept[0], product=operands + [rep_swap(value, 1) for value in operands])
    grad_hidden, grad1, low1, sums1b = ffn_backward(
        branch, grad2, pre_first, slope, full_up, full_down, gains, small_block, (steps, steps), SHORT, prior=kept, after=[down.stay]
    )
    low1 = with_edge(low1, cls_low1)
    norm_sums = (sums2 + sums1a + sums1b + c_sums).reshape(8, count, norm_cols).transpose(1, 0, 2)
    norm_sums = jnp.pad(norm_sums, ((0, 0), (0, 0), (0, width - norm_cols)))
    rider = jnp.concatenate([norm_sums, table_grad.reshape(count, table_rows, width)], axis=1).astype(BF16)
    send_up = cols_grads(1, ids, low, grad_hidden, cls, cls_hidden, rider, [], SHORT)
    own_down, *others = settle(ids, down.parts(send_up))
    came_down = swap_far(others)
    keep_up = cols_grads(0, ids, low, grad_hidden, cls, cls_hidden, rider, [send_up, own_down], LONG)
    up = Reduction(ids, send_up, keep_up)
    up.spread(keep_up, *came_down[:1])
    grad_proj = attention_backward(low1, proj, probs, full_qo, seg_length, block, after=[up.stay])
    down_share = add_up(own_down, came_down, grad_proj)
    send_qo = joint_grads(1, ids, flat, mixed, grad_proj, low1, [], SHORT)
    own_up, *others = settle(ids, up.parts(send_qo))
    came_up = swap_far(others)
    keep_qo = joint_grads(0, ids, flat, mixed, grad_proj, low1, [send_qo, own_up], LONG)
    qo = Reduction(ids, send_qo, keep_qo)
    qo.spread(keep_qo, *came_up[:2])
    c_own, c_other = halve(c_own.astype(F32) + later(c_came, qo.stay).astype(F32), 0, rep >> 1)
    c_came = rep_swap(c_other.astype(BF16), 2)
    input_grad = input_gradient(with_edge(later(grad1, qo.stay), cls_grad1), grad_proj, full_qo, block, [qo.stay])
    own, *others = settle(ids, qo.parts(input_grad))
    came = swap_far(others)
    c_share = (c_own + later(c_came, own).astype(F32)).astype(BF16)
    early = Sharing(ids, jnp.concatenate([down_share, add_up(own_up, came_up, own), c_share], axis=0))
    late = Sharing(ids, add_up(own, came))
    early.step(late.value)
    layer_out = with_edge(later(out, late.value), cls_new)
    early_shares = early.finish(layer_out)
    starts = (0, shard_rows, 2 * shard_rows, 2 * shard_rows + 16, 3 * shard_rows + 16)
    down_parts, up_parts, riders, c_parts = [
        [part[first:last] for part in early_shares] for first, last in zip(starts, starts[1:])
    ]
    done = [
        jnp.concatenate(up_parts, axis=1),
        jnp.concatenate(down_parts, axis=0),
        jnp.concatenate(c_parts[:3], axis=1),
        c_parts[3],
    ]
    summed = riders[0]
    late.step(layer_out, *done)
    qo_parts = late.finish()

    return (
        layer_out.reshape(tokens.shape),
        input_grad.reshape(tokens.shape),
        jnp.concatenate(qo_parts[:3], axis=1),
        qo_parts[3],
        *done,
        summed[8 : 8 + table_rows],
        summed[:3, :norm_cols],
        summed[3:6, :norm_cols],
    )


def solution(mesh):
    rows = P(None, "rep", "seg", None, None)
    split = P("seg", None)
    last = P(None, "seg")
    return jax.shard_map(
        body,
        mesh=mesh,
        in_specs=(rows, rows, P(None, "rep", None)) + (split,) * 7 + (last, last),
        out_specs=(rows, rows) + (split,) * 7 + (last, last),
        check_vma=False,
    )
```
